128 devices in a mesh: lon: 16 (over x_lo, y, core), lat: 8 (over z, x_hi).
Axes of the slice: x: 4 (x_hi: 2, x_lo: 2; x = x_hi * 2 + x_lo), y: 4, z: 4, core: 2. Of those that a mesh axis runs over, the one named last changes fastest.
Arguments:
- tokens: bfloat16 [8, 192, 576, 192], P(None, 'lat', 'lon'), may hold values from -64 to 64
- cotangent: bfloat16 [8, 192, 576, 192], P(None, 'lat', 'lon'), may hold values from -6 to 6
- ln_gain: float32 [192], replicated, may hold values from 0.5 to 1.5
- qkv_weight: bfloat16 [192, 576], replicated, may hold values from -0.4375 to 0.4375
- out_weight: bfloat16 [192, 192], replicated, may hold values from -0.4375 to 0.4375
- pair_bias: float32 [6, 144, 144], replicated, may hold values from -4 to 250
Outputs:
- grad_x: bfloat16 [8, 192, 576, 192], P(None, 'lat', 'lon')
- grad_qkv: float32 [192, 576], replicated
- grad_out: float32 [192, 192], replicated
- grad_bias: float32 [6, 144, 144], replicated
- grad_gain: float32 [192], replicated
The draws below stay inside these ranges and needn't reach their ends.
All inputs are finite; a program needn't handle non-finite values.
Results may differ from the reference program's by a relative error of at most 0.0095.
Values may be sent and summed in bfloat16 or wider, within the bound.
No kernel may reach another device: no remote copies, remote signals or barrier semaphores. Data moves between devices by JAX's collectives and lax.ppermute only.
A program may use at most 128 MiB of HBM per device.

```python
import jax
import jax.numpy as jnp
from jax import lax

D = 192
HEADS = 6
WIN_LEV = 2
WIN_LAT = 6
WIN_LON = 12
W = 144
HALF_LAT = 3
HALF_LON = 6
LEV = 8
NLAT = 192
NLON = 576


def draw_tokens(key, part):
    key = jax.random.fold_in(key, 5)
    first = jax.random.fold_in(key, 0)
    base = jax.random.normal(first, (LEV, NLAT, NLON, D), jnp.float32)
    return jnp.clip(base, -64.0, 64.0).astype(jnp.bfloat16)


def draw_pair_bias(key, part):
    key = jax.random.fold_in(key, 11)
    first = jax.random.fold_in(key, 0)
    base = jnp.clip(jax.random.normal(first, (HEADS, W, W), jnp.float32), -4.0, 4.0)
    return base


def steps_of(key, shape, cuts, smallest, top_value):
    loudness = 1.0
    for dim, shards_of in cuts:
        draws = jax.random.uniform(jax.random.fold_in(jax.random.fold_in(key, 6), dim), (shards_of,), jnp.float32, smallest / len(cuts), top_value / len(cuts))
        loudness = loudness * jnp.repeat(jnp.exp(draws), shape[dim] // shards_of).reshape((-1,) + (1,) * (len(shape) - 1 - dim))
    return loudness


def normal_values(key, dims, scale, reach, cuts=(), kind=jnp.bfloat16):
    factor_of = steps_of(key, dims, cuts, -0.22, 0.18) if cuts else 1.0
    entries = jax.random.normal(key, dims, jnp.float32) * scale * factor_of
    return jnp.minimum(jnp.maximum(entries, -reach), reach).astype(kind)


def setup_inputs(seed: int = 0) -> dict:
    key_of = jax.random.split(jax.random.key(seed), 7)
    tokens = draw_tokens(jax.random.fold_in(key_of[6], 71), 0)
    cotangent = normal_values(key_of[1], (LEV, NLAT, NLON, D), 1.0, 6.0, ((1, 8), (2, 16)))
    ln_gain = jnp.clip(1.0 + 0.1 * jax.random.normal(key_of[2], (D,), jnp.float32), 0.5, 1.5)
    qkv_weight = normal_values(key_of[3], (D, 3 * D), D ** -0.5, 0.4375)
    out_weight = normal_values(key_of[4], (D, D), D ** -0.5, 0.4375)
    pair_bias = draw_pair_bias(jax.random.fold_in(key_of[6], 71), 0)
    return dict(tokens=tokens, cotangent=cotangent, ln_gain=ln_gain, qkv_weight=qkv_weight, out_weight=out_weight, pair_bias=pair_bias)


def window_grads(xwin, dywin, ln_gain, qkv_weight, out_weight, pair_bias, region):
    win_count, win_span, feature_width = xwin.shape
    head_count = pair_bias.shape[0]
    head_dim = feature_width // head_count
    score_scale = head_dim ** (-0.5)
    inputs = xwin.astype(jnp.float32)
    average = lax.optimization_barrier(jnp.mean(inputs, axis=-1, keepdims=True))
    centred = inputs - average
    inv_std = lax.rsqrt(lax.optimization_barrier(jnp.mean(centred * centred, axis=-1, keepdims=True)) + 1e-05)
    unit_rows = centred * inv_std
    normed = (unit_rows * ln_gain).astype(jnp.bfloat16)
    flat_normed = normed.reshape(win_count * win_span, feature_width)
    packed = jnp.dot(flat_normed, qkv_weight, preferred_element_type=jnp.float32).astype(jnp.bfloat16)
    packed = packed.reshape(win_count, win_span, 3, head_count, head_dim)
    queries = packed[:, :, 0].astype(jnp.float32)
    key_rows = packed[:, :, 1].astype(jnp.float32)
    values = packed[:, :, 2].astype(jnp.float32)
    scores = jnp.einsum('bihd,bjhd->bhij', queries, key_rows) * score_scale + pair_bias[None]
    same_region = region[:, None, :, None] == region[:, None, None, :]
    scores = jnp.where(same_region, scores, jnp.float32(-1e+30))
    row_peak = lax.optimization_barrier(jnp.max(scores, axis=-1, keepdims=True))
    exp_scores = jnp.exp(scores - row_peak)
    probs = exp_scores / lax.optimization_barrier(jnp.sum(exp_scores, axis=-1, keepdims=True))
    probs_low = probs.astype(jnp.bfloat16)
    attended = jnp.einsum('bhij,bjhd->bihd', probs_low.astype(jnp.float32), values).astype(jnp.bfloat16)
    flat_dy = dywin.reshape(win_count * win_span, feature_width)
    d_attended = jnp.dot(flat_dy, out_weight.T, preferred_element_type=jnp.float32).astype(jnp.bfloat16)
    d_attended = d_attended.reshape(win_count, win_span, head_count, head_dim).astype(jnp.float32)
    grad_out = jnp.dot(attended.reshape(win_count * win_span, feature_width).T, flat_dy, preferred_element_type=jnp.float32)
    d_probs = jnp.einsum('bihd,bjhd->bhij', d_attended, values)
    d_scores = probs * (d_probs - lax.optimization_barrier(jnp.sum(probs * d_probs, axis=-1, keepdims=True)))
    grad_bias = lax.optimization_barrier(jnp.sum(d_scores, axis=0))
    d_scores_low = d_scores.astype(jnp.bfloat16).astype(jnp.float32)
    d_queries = jnp.einsum('bhij,bjhd->bihd', d_scores_low, key_rows) * score_scale
    d_keys = jnp.einsum('bhij,bihd->bjhd', d_scores_low, queries) * score_scale
    d_values = jnp.einsum('bhij,bihd->bjhd', probs_low.astype(jnp.float32), d_attended)
    d_packed = jnp.stack([d_queries, d_keys, d_values], axis=2).astype(jnp.bfloat16)
    d_packed = d_packed.reshape(win_count * win_span, 3 * feature_width)
    grad_qkv = jnp.dot(flat_normed.T, d_packed, preferred_element_type=jnp.float32)
    d_normed = jnp.dot(d_packed, qkv_weight.T, preferred_element_type=jnp.float32)
    d_normed = d_normed.reshape(win_count, win_span, feature_width)
    grad_gain = lax.optimization_barrier(jnp.sum(d_normed * unit_rows, axis=(0, 1)))
    d_unit = d_normed * ln_gain
    d_inputs = inv_std * (d_unit - lax.optimization_barrier(jnp.mean(d_unit, axis=-1, keepdims=True)) - unit_rows * lax.optimization_barrier(jnp.mean(d_unit * unit_rows, axis=-1, keepdims=True)))
    d_tokens = (dywin.astype(jnp.float32) + d_inputs).astype(jnp.bfloat16)
    return (d_tokens, (grad_qkv, grad_out, grad_bias, grad_gain))

def to_windows(field):
    levels, lat_rows, lon_cols, channels = field.shape
    shaped = field.reshape(levels // WIN_LEV, WIN_LEV, lat_rows // WIN_LAT, WIN_LAT, lon_cols // WIN_LON, WIN_LON, channels)
    shaped = shaped.transpose(0, 2, 4, 1, 3, 5, 6)
    return shaped.reshape(levels // WIN_LEV * (lat_rows // WIN_LAT), lon_cols // WIN_LON, W, channels)

def from_windows(blocks, levels, lat_rows, lon_cols):
    channels = blocks.shape[-1]
    shaped = blocks.reshape(levels // WIN_LEV, lat_rows // WIN_LAT, lon_cols // WIN_LON, WIN_LEV, WIN_LAT, WIN_LON, channels)
    shaped = shaped.transpose(0, 3, 1, 4, 2, 5, 6)
    return shaped.reshape(levels, lat_rows, lon_cols, channels)

def reference(tokens, cotangent, ln_gain, qkv_weight, out_weight, pair_bias):
    levels, lat_rows, lon_cols, feature_width = tokens.shape
    rolled = jnp.roll(tokens, (-HALF_LAT, -HALF_LON), axis=(1, 2))
    rolled_cot = jnp.roll(cotangent, (-HALF_LAT, -HALF_LON), axis=(1, 2))
    row_index = jnp.arange(lat_rows, dtype=jnp.int32)
    region_rows = (row_index >= lat_rows - HALF_LAT).astype(jnp.int32)
    region = jnp.broadcast_to(region_rows[None, :, None, None], (levels, lat_rows, lon_cols, 1))
    x_blocks = to_windows(rolled)
    dy_blocks = to_windows(rolled_cot)
    region_blocks = to_windows(region)[..., 0]

    def window_step(carries, pieces):
        d_tokens, grads = window_grads(pieces[0], pieces[1], ln_gain, qkv_weight, out_weight, pair_bias, pieces[2])
        return (tuple((c + g for c, g in zip(carries, grads))), d_tokens)
    zeros_init = (jnp.zeros((feature_width, 3 * feature_width), jnp.float32), jnp.zeros((feature_width, feature_width), jnp.float32), jnp.zeros(pair_bias.shape, jnp.float32), jnp.zeros((feature_width,), jnp.float32))
    totals, d_blocks = lax.scan(window_step, zeros_init, (x_blocks, dy_blocks, region_blocks))
    d_rolled = from_windows(d_blocks, levels, lat_rows, lon_cols)
    grad_x = jnp.roll(d_rolled, (HALF_LAT, HALF_LON), axis=(1, 2))
    factor = float(levels * lat_rows * lon_cols) ** (-0.5)
    return (grad_x, totals[0] * factor, totals[1] * factor, totals[2], totals[3] * factor)
```

```python
import jax
import jax.numpy as jnp
from jax import lax
from jax.experimental import pallas as pl
from jax.experimental.pallas import tpu as pltpu
from jax.sharding import PartitionSpec as P

WIN_LEV = 2
WIN_LAT = 6
WIN_LON = 12
W = 144
HEADS = 6
HEAD = 32
D = 192
HALF_LAT = 3
HALF_LON = 6
LANES = 896
LOG2E = 1.4426950408889634
SCALE = HEAD**-0.5
F32 = jnp.float32
BF16 = jnp.bfloat16
WROWS = 6 * D
BROWS = 7 * W
ROWS = 2176

NN = (((1,), (0,)), ((), ()))
NT = (((1,), (1,)), ((), ()))
TN = (((0,), (0,)), ((), ()))


def mm(a, b, dims):
    return lax.dot_general(a, b, dims, preferred_element_type=F32)


def spread(rows16):
    head_of = lax.broadcasted_iota(jnp.int32, (1, D), 1) // HEAD
    main = rows16[:128]
    rest = rows16[128:]
    zero_main = jnp.zeros_like(main)
    zero_rest = jnp.zeros_like(rest)
    parts = []
    for pair in range(3):
        parts.append(
            jnp.concatenate(
                [jnp.where(head_of == 2 * pair + n, main, zero_main) for n in range(2)], axis=0
            )
        )
    parts.append(
        jnp.concatenate(
            [jnp.where(head_of == h, rest, zero_rest) for h in range(HEADS)]
            + [zero_rest, zero_rest],
            axis=0,
        )
    )
    return parts


def fold_rest(rest):
    head_of = lax.broadcasted_iota(jnp.int32, (1, D), 1) // HEAD
    total = rest[:16]
    for h in range(1, HEADS):
        total = jnp.where(head_of == h, rest[16 * h : 16 * h + 16], total)
    return total


def attention_window(q, k, v, da, bias_ref, gb_ref):
    qm = spread(q)
    dam = spread(da)
    kt = k.T
    vt = v.T
    dk = None
    dv = None
    a_rows = []
    dq_rows = []
    for c in range(4):
        lo = 256 * c
        width = 256 if c < 3 else 128
        s = mm(k, qm[c], NT) * (SCALE * LOG2E) + bias_ref[:, lo : lo + width]
        dp = mm(v, dam[c], NT)
        e = jnp.exp2(s - jnp.max(s, axis=0, keepdims=True))
        p = e * (1.0 / jnp.sum(e, axis=0, keepdims=True))
        ds = p * (dp - jnp.sum(p * dp, axis=0, keepdims=True))
        gb_ref[:, lo : lo + width] += ds
        pb = p.astype(BF16)
        dsb = ds.astype(BF16)
        dvc = mm(pb, dam[c], NN)
        dkc = mm(dsb, qm[c], NN)
        dv = dvc if dv is None else dv + dvc
        dk = dkc if dk is None else dk + dkc
        if c < 3:
            at = mm(vt[64 * c : 64 * c + 64], pb, NN)
            dqt = mm(kt[64 * c : 64 * c + 64], dsb, NN)
            a_rows += [at[:32, :128], at[32:, 128:]]
            dq_rows += [dqt[:32, :128], dqt[32:, 128:]]
        else:
            a_rest = fold_rest(mm(pb, v, TN))
            dq_rest = fold_rest(mm(dsb, k, TN))
    a = jnp.concatenate([jnp.concatenate(a_rows, axis=0).T, a_rest], axis=0).astype(BF16)
    dq = jnp.concatenate([jnp.concatenate(dq_rows, axis=0).T, dq_rest], axis=0)
    return a, (dq * SCALE).astype(BF16), (dk * SCALE).astype(BF16), dv.astype(BF16)


def windows_backward(x, dy, gain, wqkv_ref, wout_ref, bias_ref, gw_ref, gb_ref):
    count = x.shape[0] // W
    mean = jnp.mean(x, axis=-1, keepdims=True)
    centred = x - mean
    inv_std = lax.rsqrt(jnp.mean(centred * centred, axis=-1, keepdims=True) + 1e-05)
    unit = centred * inv_std
    normed = (unit * gain).astype(BF16)
    dyb = dy.astype(BF16)
    packed = mm(normed, wqkv_ref[...], NN).astype(BF16)
    datt = mm(dyb, wout_ref[...], NT).astype(BF16)
    grads = None
    parts = []
    for w in range(count):
        rows = slice(W * w, W * w + W)
        a, dq, dk, dv = attention_window(
            packed[rows, 0:192],
            packed[rows, 256:448],
            packed[rows, 512:704],
            datt[rows],
            bias_ref,
            gb_ref,
        )
        parts.append((a, dq, dk, dv))
    a, dq, dk, dv = (jnp.concatenate([p[n] for p in parts], axis=0) for n in range(4))
    gw_ref[0] += mm(normed, dq, TN)
    gw_ref[1] += mm(normed, dk, TN)
    gw_ref[2] += mm(normed, dv, TN)
    gw_ref[3] += mm(a, dyb, TN)
    dn = (
        mm(dq, wqkv_ref[:, 0:192], NT)
        + mm(dk, wqkv_ref[:, 256:448], NT)
        + mm(dv, wqkv_ref[:, 512:704], NT)
    )
    du = dn * gain
    dx = inv_std * (
        du
        - jnp.mean(du, axis=-1, keepdims=True)
        - unit * jnp.mean(du * unit, axis=-1, keepdims=True)
    )
    return dy + dx


def start_sums(first, gw_ref, gb_ref, gw_in, gb_in):
    @pl.when(first)
    def _():
        if gw_in is None:
            gw_ref[...] = jnp.zeros_like(gw_ref)
            gb_ref[...] = jnp.zeros_like(gb_ref)
        else:
            gw_ref[...] = gw_in[...]
            gb_ref[...] = gb_in[...]


def lat_rows(refs, levels):
    return [(refs[n // 3], lv, n % 3) for lv in levels for n in range(WIN_LAT)]


def inner_kernel(xt, xu, yt, yu, gain, wqkv, wout, bias, dx_ref, gw_ref, gb_ref):
    first = (pl.program_id(0) == 0) & (pl.program_id(1) == 0)
    start_sums(first, gw_ref, gb_ref, None, None)

    def load(refs):
        rows = [r[lv, la].astype(F32) for r, lv, la in lat_rows(refs, (0, 1))]
        return jnp.concatenate(
            [row[6 + 12 * n : 18 + 12 * n] for n in range(2) for row in rows], axis=0
        )

    out = windows_backward(
        load((xt, xu)), load((yt, yu)), gain[...], wqkv, wout, bias, gw_ref, gb_ref
    )
    for n in range(12):
        row = jnp.concatenate([out[12 * n : 12 * n + 12], out[W + 12 * n : W + 12 * n + 12]], axis=0)
        dx_ref[n // 6, n % 6] = row.astype(BF16)


def east_kernel(
    xt, xu, yt, yu, ext, exu, eyt, eyu, gain, wqkv, wout, bias, gw_in, gb_in, dx_ref, gw_ref, gb_ref
):
    first = (pl.program_id(0) == 0) & (pl.program_id(1) == 0)
    start_sums(first, gw_ref, gb_ref, gw_in, gb_in)

    def load(refs, east):
        pieces = []
        for (r, lv, la), (e, _, _) in zip(
            lat_rows(refs, range(4)), lat_rows(east, range(4))
        ):
            pieces += [r[lv, la].astype(F32)[30:36], e[lv, la].astype(F32)]
        return jnp.concatenate(pieces, axis=0)

    out = windows_backward(
        load((xt, xu), (ext, exu)),
        load((yt, yu), (eyt, eyu)),
        gain[...],
        wqkv,
        wout,
        bias,
        gw_ref,
        gb_ref,
    )
    for n in range(24):
        dx_ref[n // 6, n % 6] = out[12 * n : 12 * n + 12].astype(BF16)


def south_kernel(
    xt, xs, yt, ys, ext, exs, eyt, eys, gain, wqkv, wout, bias, gw_in, gb_in, dx_ref, sum_ref, gw_ref, gb_ref
):
    first = pl.program_id(0) == 0
    start_sums(first, gw_ref, gb_ref, gw_in, gb_in)

    def load(refs, east):
        rows = [r[lv, la].astype(F32) for r, lv, la in lat_rows(refs, (0, 1))]
        erows = [r[lv, la].astype(F32) for r, lv, la in lat_rows(east, (0, 1))]
        pieces = [row[6 + 12 * n : 18 + 12 * n] for n in range(2) for row in rows]
        for row, erow in zip(rows, erows):
            pieces += [row[30:36], erow]
        return jnp.concatenate(pieces, axis=0)

    out = windows_backward(
        load((xt, xs), (ext, exs)),
        load((yt, ys), (eyt, eys)),
        gain[...],
        wqkv,
        wout,
        bias,
        gw_ref,
        gb_ref,
    )
    for n in range(12):
        row = jnp.concatenate(
            [out[W * k + 12 * n : W * k + 12 * n + 12] for k in range(3)], axis=0
        )
        dx_ref[n // 6, n % 6] = row.astype(BF16)

    @pl.when(pl.program_id(0) == pl.num_programs(0) - 1)
    def _():
        whole = jnp.concatenate([gw_ref[n] for n in range(4)], axis=1)
        for t in range(6):
            sum_ref[D * t : D * t + D] = whole[:, 128 * t : 128 * t + 128]
        for t in range(7):
            sum_ref[WROWS + W * t : WROWS + W * t + W] = gb_ref[:, 128 * t : 128 * t + 128]
        sum_ref[WROWS + BROWS :] = jnp.zeros((ROWS - WROWS - BROWS, 128), F32)


def whole(shape):
    return pl.BlockSpec(shape, lambda *_: (0,) * len(shape))


PARAMS = pltpu.CompilerParams(vmem_limit_bytes=56 * 1024 * 1024)
GW = (4, D, D)
GB = (W, LANES)


def cost(count):
    return pl.CostEstimate(
        flops=count * 144 * 192 * 192 * 40, bytes_accessed=count * 144 * 192 * 6, transcendentals=0
    )


def const_specs():
    return [whole((1, D)), whole((D, 768)), whole((D, D)), whole((W, LANES))]


def inner_windows(x, y, consts):
    levels = x.shape[0]

    def rows(shift):
        return pl.BlockSpec((2, 3, 36, D), lambda i, b: (i, 2 * b + shift, 0, 0))

    return pl.pallas_call(
        inner_kernel,
        grid=(levels // 2, 3),
        in_specs=[rows(1), rows(2), rows(1), rows(2)] + const_specs(),
        out_specs=[pl.BlockSpec((2, 6, 24, D), lambda i, b: (i, b, 0, 0)), whole(GW), whole(GB)],
        out_shape=[
            jax.ShapeDtypeStruct((levels, 18, 24, D), BF16),
            jax.ShapeDtypeStruct(GW, F32),
            jax.ShapeDtypeStruct(GB, F32),
        ],
        compiler_params=PARAMS,
        cost_estimate=cost(24),
        name="inner_windows",
    )(x, x, y, y, *consts)


def east_windows(x, y, ex, ey, consts, sums):
    levels = x.shape[0]

    def rows(shift, lon):
        return pl.BlockSpec((4, 3, lon, D), lambda i, b: (i, 2 * b + shift, 0, 0))

    return pl.pallas_call(
        east_kernel,
        grid=(levels // 4, 3),
        in_specs=[rows(1, 36), rows(2, 36), rows(1, 36), rows(2, 36)]
        + [rows(1, 6), rows(2, 6), rows(1, 6), rows(2, 6)]
        + const_specs()
        + [whole(GW), whole(GB)],
        out_specs=[pl.BlockSpec((4, 6, 12, D), lambda i, b: (i, b, 0, 0)), whole(GW), whole(GB)],
        out_shape=[
            jax.ShapeDtypeStruct((levels, 18, 12, D), BF16),
            jax.ShapeDtypeStruct(GW, F32),
            jax.ShapeDtypeStruct(GB, F32),
        ],
        compiler_params=PARAMS,
        cost_estimate=cost(12),
        name="east_windows",
    )(x, x, y, y, ex, ex, ey, ey, *consts, *sums)


def south_windows(x, y, sx, sy, ex, ey, cx, cy, consts, sums):
    levels = x.shape[0]

    def rows(block, lon):
        return pl.BlockSpec((2, 3, lon, D), lambda i: (i, block, 0, 0))

    return pl.pallas_call(
        south_kernel,
        grid=(levels // 2,),
        in_specs=[rows(7, 36), rows(0, 36), rows(7, 36), rows(0, 36)]
        + [rows(7, 6), rows(0, 6), rows(7, 6), rows(0, 6)]
        + const_specs()
        + [whole(GW), whole(GB)],
        out_specs=[pl.BlockSpec((2, 6, 36, D), lambda i: (i, 0, 0, 0)), whole((ROWS, 128))],
        out_shape=[
            jax.ShapeDtypeStruct((levels, 6, 36, D), BF16),
            jax.ShapeDtypeStruct((ROWS, 128), F32),
        ],
        scratch_shapes=[pltpu.VMEM(GW, F32), pltpu.VMEM(GB, F32)],
        compiler_params=PARAMS,
        cost_estimate=cost(12),
        name="south_windows",
    )(x, sx, y, sy, ex, cx, ey, cy, *consts, *sums)


def finish_kernel(factor, sum_ref, gain_ref, w_ref, gq_ref, go_ref, gb_ref, gg_ref):
    both = jnp.concatenate(
        [sum_ref[D * t : D * t + D].astype(F32) for t in range(6)], axis=1
    )
    gq = both[:, : 3 * D] * factor
    gq_ref[...] = gq
    go_ref[...] = both[:, 3 * D :] * factor
    gg_ref[...] = jnp.sum(gq * w_ref[...].astype(F32), axis=1, keepdims=True) / gain_ref[...]
    base = WROWS + 6 * W
    rest = sum_ref[base : base + W].astype(F32).T
    for h in range(HEADS):
        main = sum_ref[WROWS + W * h : WROWS + W * h + W].astype(F32).T
        gb_ref[h, :128] = main
        gb_ref[h, 128:] = rest[16 * h : 16 * h + 16]


def finish(sums, gain_col, qkv_weight, factor):
    return pl.pallas_call(
        lambda *refs: finish_kernel(factor, *refs),
        out_shape=[
            jax.ShapeDtypeStruct((D, 3 * D), F32),
            jax.ShapeDtypeStruct((D, D), F32),
            jax.ShapeDtypeStruct((HEADS, W, W), F32),
            jax.ShapeDtypeStruct((D, 1), F32),
        ],
        compiler_params=PARAMS,
        name="finish_sums",
    )(sums, gain_col, qkv_weight)


def score_lanes(bias):
    turned = jnp.transpose(bias, (2, 0, 1))
    return jnp.concatenate(
        [
            turned[:, :, :128].reshape(W, HEADS * 128),
            turned[:, :, 128:].reshape(W, HEADS * 16),
            jnp.zeros((W, 32), F32),
        ],
        axis=1,
    )


def make_consts(ln_gain, qkv_weight, out_weight, pair_bias):
    wqkv = jnp.pad(qkv_weight.reshape(D, 3, D), ((0, 0), (0, 0), (0, 64))).reshape(D, 768)
    bias = score_lanes(pair_bias) * LOG2E
    return [ln_gain.reshape(1, D), wqkv, out_weight, bias]


def shift(value, axes, steps):
    sizes = [lax.axis_size(a) for a in axes]
    total = 1
    for s in sizes:
        total *= s
    pairs = []
    for source in range(total):
        rest, place = source, []
        for s in reversed(sizes):
            place.append(rest % s)
            rest //= s
        place.reverse()
        target = 0
        for p, s, d in zip(place, sizes, steps):
            target = target * s + (p + d) % s
        pairs.append((source, target))
    return lax.ppermute(value, axes if len(axes) > 1 else axes[0], pairs)


def moved(value, axis, to_of):
    count = lax.axis_size(axis)
    return lax.ppermute(value, axis, [(n, to_of(n)) for n in range(count)])


def flip(value, axis, bits):
    return moved(value, axis, lambda n: n ^ bits)


def lon_core(n):
    return n % 2


def sum_over_devices(sums):
    lon = lax.axis_index("lon")
    core = lon % 2
    y = (lon // 2) % 4
    halves = sums.reshape(2, ROWS // 2, 128)
    low = halves.astype(BF16)
    got = flip(lax.dynamic_index_in_dim(low, 1 - core, 0, keepdims=False), "lon", 1)
    mine = lax.dynamic_index_in_dim(halves, core, 0, keepdims=False) + got.astype(F32)
    quarters = mine.reshape(4, ROWS // 8, 128)
    qlow = quarters.astype(BF16)
    total = lax.dynamic_index_in_dim(quarters, y, 0, keepdims=False)
    for step in range(1, 4):
        piece = lax.dynamic_index_in_dim(qlow, y ^ step, 0, keepdims=False)
        total = total + flip(piece, "lon", 2 * step).astype(F32)
    low = total.astype(BF16)
    for step in range(1, 4):
        total = total + flip(low, "lat", 2 * step).astype(F32)
    low = total.astype(BF16)
    total = (
        total
        + flip(low, "lat", 1).astype(F32)
        + flip(low, "lon", 8).astype(F32)
        + shift_x(low).astype(F32)
    )
    low = total.astype(BF16)
    others = [low] + [flip(low, "lon", 2 * step) for step in range(1, 4)]
    stacked = jnp.stack(others)
    line = jnp.concatenate(
        [lax.dynamic_index_in_dim(stacked, y ^ n, 0, keepdims=True) for n in range(4)], axis=0
    )
    other = flip(line, "lon", 1)
    pair = jnp.stack([line, other])
    return jnp.concatenate(
        [
            lax.dynamic_index_in_dim(pair, core ^ n, 0, keepdims=False).reshape(ROWS // 2, 128)
            for n in range(2)
        ],
        axis=0,
    )


def shift_x(value):
    lat = lax.axis_size("lat")
    total = lax.axis_size("lon") * lat
    pairs = []
    for source in range(total):
        lon_at, lat_at = source // lat, source % lat
        pairs.append((source, (lon_at ^ 8) * lat + (lat_at ^ 1)))
    return lax.ppermute(value, ("lon", "lat"), pairs)


def local(tokens, cotangent, ln_gain, qkv_weight, out_weight, pair_bias):
    levels, lat_count, lon_count, _ = tokens.shape
    ex = shift(tokens[:, :, :HALF_LON], ("lon",), (-1,))
    ey = shift(cotangent[:, :, :HALF_LON], ("lon",), (-1,))
    sx = shift(tokens[:, :HALF_LAT], ("lat",), (-1,))
    sy = shift(cotangent[:, :HALF_LAT], ("lat",), (-1,))
    cx = shift(tokens[:, :HALF_LAT, :HALF_LON], ("lon", "lat"), (-1, -1))
    cy = shift(cotangent[:, :HALF_LAT, :HALF_LON], ("lon", "lat"), (-1, -1))
    consts = make_consts(ln_gain, qkv_weight, out_weight, pair_bias)
    last = lax.axis_index("lat") == lax.axis_size("lat") - 1
    region = (jnp.arange(W) // WIN_LON) % WIN_LAT >= HALF_LAT
    apart = jnp.broadcast_to(region[:, None] != region[None, :], (HEADS, W, W))
    masked = jnp.where(apart & last, F32(-1e30), pair_bias)
    edge_consts = consts[:3] + [score_lanes(masked) * LOG2E]
    inner, gw, gb = inner_windows(tokens, cotangent, consts)
    east, gw, gb = east_windows(tokens, cotangent, ex, ey, consts, (gw, gb))
    south, sums = south_windows(
        tokens, cotangent, sx, sy, ex, ey, cx, cy, edge_consts, (gw, gb)
    )
    back_lon = jnp.concatenate([east[:, :, HALF_LON:], south[:, :HALF_LAT, 30:]], axis=1)
    got_lon = shift(back_lon, ("lon",), (1,))
    got_lat = shift(south[:, HALF_LAT:, :30], ("lat",), (1,))
    got_both = shift(south[:, HALF_LAT:, 30:], ("lon", "lat"), (1, 1))
    grad_x = jnp.concatenate(
        [
            jnp.concatenate([got_both, got_lat], axis=2),
            jnp.concatenate([got_lon[:, :18], inner, east[:, :, :HALF_LON]], axis=2),
            jnp.concatenate([got_lon[:, 18:], south[:, :HALF_LAT, :30]], axis=2),
        ],
        axis=1,
    )
    sums = sum_over_devices(sums)
    factor = float(
        levels * lat_count * lax.axis_size("lat") * lon_count * lax.axis_size("lon")
    ) ** (-0.5)
    gq, go, gbias, gg = finish(sums, ln_gain.reshape(D, 1), qkv_weight, factor)
    return (grad_x, gq, go, gbias, gg.reshape(D))


def solution(mesh):
    placed = (P(None, "lat", "lon", None), P(None, "lat", "lon", None), P(), P(), P(), P())
    return jax.shard_map(
        local,
        mesh=mesh,
        in_specs=placed,
        out_specs=(P(None, "lat", "lon", None), P(), P(), P(), P()),
        check_vma=False,
    )
```

```python
import jax
import jax.numpy as jnp
from jax import lax
from jax.experimental import pallas as pl
from jax.experimental.pallas import tpu as pltpu
from jax.sharding import PartitionSpec as P

WIN_LEV = 2
WIN_LAT = 6
WIN_LON = 12
W = 144
HEADS = 6
HEAD = 32
D = 192
HALF_LAT = 3
HALF_LON = 6
LANES = 896
LOG2E = 1.4426950408889634
SCALE = HEAD**-0.5
F32 = jnp.float32
BF16 = jnp.bfloat16
WROWS = 6 * D
BROWS = 7 * W
ROWS = 2176

NN = (((1,), (0,)), ((), ()))
NT = (((1,), (1,)), ((), ()))
TN = (((0,), (0,)), ((), ()))


def mm(a, b, dims):
    return lax.dot_general(a, b, dims, preferred_element_type=F32)


def pair_rows(rows, c):
    part = rows[:128, 64 * c : 64 * c + 64]
    first = lax.broadcasted_iota(jnp.int32, (1, 64), 1) < HEAD
    zero = jnp.zeros_like(part)
    return jnp.concatenate([jnp.where(first, part, zero), jnp.where(first, zero, part)], axis=0)


def rest_rows(rows):
    head_of = lax.broadcasted_iota(jnp.int32, (1, D), 1) // HEAD
    rest = rows[128:]
    zero = jnp.zeros_like(rest)
    return jnp.concatenate(
        [jnp.where(head_of == h, rest, zero) for h in range(HEADS)] + [zero, zero], axis=0
    )


def fold_rest(rest):
    head_of = lax.broadcasted_iota(jnp.int32, (1, D), 1) // HEAD
    total = rest[:16]
    for h in range(1, HEADS):
        total = jnp.where(head_of == h, rest[16 * h : 16 * h + 16], total)
    return total


class Window:
    def __init__(self, fetch, put, bias_at, refs):
        self.fetch, self.put, self.bias_at, self.refs = fetch, put, bias_at, refs

    def front(self):
        r = self.refs
        x, dy = self.fetch()
        mean = jnp.mean(x, axis=-1, keepdims=True)
        centred = x - mean
        self.inv_std = lax.rsqrt(jnp.mean(centred * centred, axis=-1, keepdims=True) + 1e-05)
        self.unit = centred * self.inv_std
        self.normed = (self.unit * r["gain"][...]).astype(BF16)
        self.dy = dy
        self.dyb = dy.astype(BF16)
        packed = mm(self.normed, r["wqkv"][...], NN).astype(BF16)
        self.q = packed[:, 0:192]
        self.k = packed[:, 256:448]
        self.v = packed[:, 512:704]
        self.da = mm(self.dyb, r["wout_t"][...], NN).astype(BF16)
        self.kt = self.k.T
        self.vt = self.v.T
        self.raw, self.low, self.dv, self.dk, self.at, self.dqt = {}, {}, {}, {}, {}, {}
        self.qm, self.dam = {}, {}

    def scores(self, c):
        if c < 3:
            cols = slice(64 * c, 64 * c + 64)
            self.qm[c] = pair_rows(self.q, c)
            self.dam[c] = pair_rows(self.da, c)
            k, v = self.k[:, cols], self.v[:, cols]
        else:
            self.qm[c] = rest_rows(self.q)
            self.dam[c] = rest_rows(self.da)
            k, v = self.k, self.v
        self.raw[c] = (mm(k, self.qm[c], NT), mm(v, self.dam[c], NT))

    def softmax(self, c):
        lanes = slice(256 * c, 256 * c + 256) if c < 3 else slice(768, 896)
        raw, dp = self.raw.pop(c)
        s = raw * (SCALE * LOG2E) + self.refs["bias"][self.bias_at, :, lanes]
        e = jnp.exp2(s - jnp.max(s, axis=0, keepdims=True))
        p = e * (1.0 / jnp.sum(e, axis=0, keepdims=True))
        ds = p * (dp - jnp.sum(p * dp, axis=0, keepdims=True))
        self.refs["gb"][:, lanes] += ds
        self.low[c] = (p.astype(BF16), ds.astype(BF16))

    def products(self, c):
        pb, dsb = self.low.pop(c)
        self.dv[c] = mm(pb, self.dam.pop(c), NN)
        self.dk[c] = mm(dsb, self.qm.pop(c), NN)
        if c < 3:
            self.at[c] = mm(self.vt[64 * c : 64 * c + 64], pb, NN)
            self.dqt[c] = mm(self.kt[64 * c : 64 * c + 64], dsb, NN)
        else:
            self.at[c] = fold_rest(mm(pb, self.v, TN))
            self.dqt[c] = fold_rest(mm(dsb, self.k, TN))

    def back(self):
        r = self.refs

        def queries(parts):
            main = [p for c in range(3) for p in (parts[c][:32, :128], parts[c][32:, 128:])]
            return jnp.concatenate([jnp.concatenate(main, axis=0).T, parts[3]], axis=0)

        def keys(parts):
            return jnp.concatenate([parts[c] for c in range(3)], axis=1) + parts[3]

        self.a = queries(self.at).astype(BF16)
        self.dqb = (queries(self.dqt) * SCALE).astype(BF16)
        self.dkb = (keys(self.dk) * SCALE).astype(BF16)
        self.dvb = keys(self.dv).astype(BF16)
        w = r["wqkv_t"]
        dn = mm(self.dqb, w[0:192], NN) + mm(self.dkb, w[192:384], NN) + mm(self.dvb, w[384:576], NN)
        du = dn * r["gain"][...]
        dx = self.inv_std * (
            du
            - jnp.mean(du, axis=-1, keepdims=True)
            - self.unit * jnp.mean(du * self.unit, axis=-1, keepdims=True)
        )
        self.put(self.dy + dx)

    def steps(self):
        yield self.front
        yield lambda: self.scores(0)
        yield lambda: (self.scores(1), self.softmax(0))
        yield lambda: (self.scores(2), self.softmax(1), self.products(0))
        yield lambda: (self.scores(3), self.softmax(2), self.products(1))
        yield lambda: (self.softmax(3), self.products(2))
        yield lambda: self.products(3)
        yield self.back


STAGGER = 4


def run_windows(windows, gw_ref):
    plans = [list(w.steps()) for w in windows]
    for tick in range(STAGGER * (len(plans) - 1) + len(plans[0])):
        for n in reversed(range(len(plans))):
            at = tick - STAGGER * n
            if 0 <= at < len(plans[n]):
                plans[n][at]()
    normed = jnp.concatenate([w.normed for w in windows], axis=0)
    for n, name in enumerate(("dqb", "dkb", "dvb")):
        gw_ref[n] += mm(normed, jnp.concatenate([getattr(w, name) for w in windows], axis=0), TN)
    gw_ref[3] += mm(
        jnp.concatenate([w.a for w in windows], axis=0),
        jnp.concatenate([w.dyb for w in windows], axis=0),
        TN,
    )


def fetch_rows(low, high, start, stride):
    lats = [pl.ds(start + n, 24, stride=stride) for n in range(WIN_LAT)]
    return jnp.concatenate(
        [
            jnp.concatenate([low[at, :] for at in lats], axis=0),
            jnp.concatenate([high[at, :] for at in lats], axis=0)[:, :64],
        ],
        axis=1,
    )


def put_rows(low, high, start, stride, value):
    right = jnp.concatenate([value[:, 128:], jnp.zeros((W, 64), F32)], axis=1)
    for n in range(WIN_LAT):
        at = pl.ds(start + n, 24, stride=stride)
        low[at, :] = value[24 * n : 24 * n + 24, :128]
        high[at, :] = right[24 * n : 24 * n + 24]


def keep(low, high, at, rows):
    wide = rows.astype(F32)
    n = rows.shape[0]
    low[at : at + n, :] = wide[:, :128]
    high[at : at + n, :64] = wide[:, 128:]


def kept(low, high, at, n):
    return jnp.concatenate([low[at : at + n, :], high[at : at + n, :64]], axis=1).astype(BF16)


def window_of(scratch, start, stride, bias_at, refs):
    x0, x1, y0, y1, o0, o1 = scratch

    def fetch():
        return fetch_rows(x0, x1, start, stride), fetch_rows(y0, y1, start, stride)

    def put(value):
        put_rows(o0, o1, start, stride, value)

    return Window(fetch, put, bias_at, refs)


def regroup(rows, back=False):
    if back:
        order = [la * 2 + lv for lv in range(2) for la in range(6)]
    else:
        order = [lv * 6 + la for la in range(6) for lv in range(2)]
    return jnp.concatenate([rows[12 * n : 12 * n + 12] for n in order], axis=0)


def lay_bias(pair_ref, last_ref, bias_ref):
    turned = [regroup(regroup(pair_ref[h]).T) * LOG2E for h in range(HEADS)]
    flat = jnp.concatenate(
        [t[:, :128] for t in turned] + [t[:, 128:] for t in turned] + [jnp.zeros((W, 32), F32)],
        axis=1,
    )
    bias_ref[0] = flat
    key_south = lax.broadcasted_iota(jnp.int32, (W, LANES), 0) >= W // 2
    lane = lax.broadcasted_iota(jnp.int32, (W, LANES), 1)
    query_south = (lane >= 768) | (lane % 128 >= W // 2)
    apart = (key_south != query_south) & (last_ref[...] > 0)
    bias_ref[1] = jnp.where(apart, F32(-1e30), flat)


def inner_kernel(
    x0, x1, x2, x3, y0, y1, y2, y3, gain, wqkv, wqkv_t, wout_t, pair, last, dx_ref, gw_ref, gb_ref, bias_ref, *scratch
):
    @pl.when(pl.program_id(0) == 0)
    def _():
        gw_ref[...] = jnp.zeros_like(gw_ref)
        gb_ref[...] = jnp.zeros_like(gb_ref)
        lay_bias(pair, last, bias_ref)

    xs, ys = (x0, x1, x2, x3), (y0, y1, y2, y3)

    def place(lv, lon):
        return 24 * (24 * (lon // 12) + 12 * lv + lon % 12)

    for lv in range(2):
        for lon in range(24):
            keep(scratch[0], scratch[1], place(lv, lon), xs[lon // 6][lv, lon % 6])
            keep(scratch[2], scratch[3], place(lv, lon), ys[lon // 6][lv, lon % 6])
    refs = dict(
        gain=gain, wqkv=wqkv, wqkv_t=wqkv_t, wout_t=wout_t, bias=bias_ref, gb=gb_ref
    )
    run_windows(
        [
            window_of(scratch, 576 * k + 3 + 6 * a, 24, 0, refs)
            for k in range(2)
            for a in range(3)
        ],
        gw_ref,
    )
    for lv in range(2):
        for lon in range(24):
            dx_ref[lv, lon] = kept(scratch[4], scratch[5], place(lv, lon), 24)


def edge_kernel(
    x, y, e, s, c, gain, wqkv, wqkv_t, wout_t, bias, gw_in, gb_in, oe_ref, os_ref, sum_ref, gw_ref, gb_ref, *scratch
):
    @pl.when(pl.program_id(0) == 0)
    def _():
        gw_ref[...] = gw_in[...]
        gb_ref[...] = gb_in[...]

    def place(lv, lon):
        if lon < 12:
            return 32 * (12 * lv + lon)
        return 768 + 16 * (24 * ((lon - 12) // 12) + 12 * lv + lon % 12)

    for n, own in enumerate((x, y)):
        low, high = scratch[2 * n], scratch[2 * n + 1]
        for lv in range(2):
            for lon in range(6):
                at = place(lv, lon)
                keep(low, high, at, own[lv, 30 + lon])
                keep(low, high, at + 24, s[n, lv, 30 + lon])
                at = place(lv, 6 + lon)
                keep(low, high, at, e[n, lv, lon])
                keep(low, high, at + 24, c[n, lv, lon])
            for lon in range(24):
                at = place(lv, 12 + lon)
                keep(low, high, at, own[lv, 6 + lon].astype(F32)[16:])
                keep(low, high, at + 8, s[n, lv, 6 + lon])
    refs = dict(
        gain=gain, wqkv=wqkv, wqkv_t=wqkv_t, wout_t=wout_t, bias=bias, gb=gb_ref
    )
    run_windows(
        [window_of(scratch, 3 + 6 * a, 32, int(a == 3), refs) for a in range(4)]
        + [window_of(scratch, 768 + 384 * k + 5, 16, 1, refs) for k in range(2)],
        gw_ref,
    )
    for lv in range(2):
        for lon in range(12):
            oe_ref[lv, lon] = kept(scratch[4], scratch[5], place(lv, lon), 32)
        for lon in range(24):
            os_ref[lv, lon] = kept(scratch[4], scratch[5], place(lv, 12 + lon), 16)

    @pl.when(pl.program_id(0) == pl.num_programs(0) - 1)
    def _():
        whole = jnp.concatenate([gw_ref[n] for n in range(4)], axis=1)
        for t in range(6):
            sum_ref[D * t : D * t + D] = whole[:, 128 * t : 128 * t + 128]
        for t in range(7):
            sum_ref[WROWS + W * t : WROWS + W * t + W] = gb_ref[:, 128 * t : 128 * t + 128]
        sum_ref[WROWS + BROWS :] = jnp.zeros((ROWS - WROWS - BROWS, 128), F32)


def whole(shape):
    return pl.BlockSpec(shape, lambda *_: (0,) * len(shape))


PARAMS = pltpu.CompilerParams(vmem_limit_bytes=60 * 1024 * 1024)
GW = (4, D, D)
GB = (W, LANES)
BIAS = (2, W, LANES)


def cost(count):
    return pl.CostEstimate(
        flops=count * 144 * 192 * 192 * 40, bytes_accessed=count * 144 * 192 * 6, transcendentals=0
    )


def const_specs():
    return [whole((1, D)), whole((D, 768)), whole((3 * D, D)), whole((D, D))]


def halves(rows):
    return [pltpu.VMEM((rows, 128), F32) for _ in range(6)]


def inner_windows(x, y, consts, pair_bias, last):
    levels = x.shape[0]

    def cols(n):
        return pl.BlockSpec((2, 6, 24, D), lambda i: (i, n, 0, 0))

    four = [cols(n) for n in range(1, 5)]
    return pl.pallas_call(
        inner_kernel,
        grid=(levels // 2,),
        in_specs=four + four + const_specs() + [whole((HEADS, W, W)), whole((1, 1))],
        out_specs=[
            pl.BlockSpec((2, 24, 24, D), lambda i: (i, 0, 0, 0)),
            whole(GW),
            whole(GB),
            whole(BIAS),
        ],
        out_shape=[
            jax.ShapeDtypeStruct((levels, 24, 24, D), BF16),
            jax.ShapeDtypeStruct(GW, F32),
            jax.ShapeDtypeStruct(GB, F32),
            jax.ShapeDtypeStruct(BIAS, F32),
        ],
        scratch_shapes=halves(1152),
        compiler_params=PARAMS,
        cost_estimate=cost(24),
        name="inner_windows",
    )(x, x, x, x, y, y, y, y, *consts, pair_bias, last)


def edge_windows(x, y, e, s, c, consts, bias, sums):
    levels = x.shape[0]

    def both(lon, lat):
        return pl.BlockSpec((2, 2, lon, lat, D), lambda i: (0, i, 0, 0, 0))

    def one(lon, lat):
        return pl.BlockSpec((2, lon, lat, D), lambda i: (i, 0, 0, 0))

    return pl.pallas_call(
        edge_kernel,
        grid=(levels // 2,),
        in_specs=[one(36, 24), one(36, 24), both(6, 24), both(36, 3), both(6, 3)]
        + const_specs()
        + [whole(BIAS), whole(GW), whole(GB)],
        out_specs=[one(12, 32), one(24, 16), whole((ROWS, 128))],
        out_shape=[
            jax.ShapeDtypeStruct((levels, 12, 32, D), BF16),
            jax.ShapeDtypeStruct((levels, 24, 16, D), BF16),
            jax.ShapeDtypeStruct((ROWS, 128), F32),
        ],
        scratch_shapes=[pltpu.VMEM(GW, F32), pltpu.VMEM(GB, F32)] + halves(1536),
        compiler_params=PARAMS,
        cost_estimate=cost(24),
        name="edge_windows",
    )(x, y, e, s, c, *consts, bias, *sums)


def assemble_kernel(inner, oe, os_, gl, gs, gc, out_ref):
    row = lax.broadcasted_iota(jnp.int32, (8, D), 0)

    def head(got, tile):
        wide = jnp.concatenate([got.astype(F32), jnp.zeros((5, D), F32)], axis=0)
        return jnp.where(row < 3, wide, tile)

    for lon in range(36):
        if lon < 6:
            rows = gl[0, lon].astype(F32)
            got = gc[0, lon]
        elif lon < 30:
            rows = inner[0, lon - 6].astype(F32)
            tail = os_[0, lon - 6].astype(F32)[:8]
            rows = jnp.concatenate([rows[:16], jnp.where(row >= 5, tail, rows[16:])], axis=0)
            got = gs[0, lon - 6]
        else:
            rows = oe[0, lon - 30].astype(F32)[:24]
            got = gs[0, lon - 6]
        out_ref[0, lon] = jnp.concatenate([head(got, rows[:8]), rows[8:]], axis=0).astype(BF16)


def assemble(inner, oe, os_, got_lon, got_lat, got_both):
    levels = inner.shape[0]

    def one(lon, lat):
        return pl.BlockSpec((1, lon, lat, D), lambda i: (i, 0, 0, 0))

    return pl.pallas_call(
        assemble_kernel,
        grid=(levels,),
        in_specs=[one(24, 24), one(12, 32), one(24, 16), one(6, 24), one(30, 3), one(6, 3)],
        out_specs=one(36, 24),
        out_shape=jax.ShapeDtypeStruct((levels, 36, 24, D), BF16),
        compiler_params=PARAMS,
        cost_estimate=pl.CostEstimate(flops=0, bytes_accessed=6_000_000, transcendentals=0),
        name="assemble",
    )(inner, oe, os_, got_lon, got_lat, got_both)


def finish_kernel(factor, sum_ref, gain_ref, w_ref, gq_ref, go_ref, gb_ref, gg_ref):
    both = jnp.concatenate(
        [sum_ref[D * t : D * t + D].astype(F32) for t in range(6)], axis=1
    )
    gq = both[:, : 3 * D] * factor
    gq_ref[...] = gq
    go_ref[...] = both[:, 3 * D :] * factor
    products = (gq * w_ref[...].astype(F32)).T
    gg_ref[...] = jnp.sum(products, axis=0, keepdims=True) / gain_ref[...]
    base = WROWS + 6 * W
    rest = sum_ref[base : base + W].astype(F32)
    for h in range(HEADS):
        main = sum_ref[WROWS + W * h : WROWS + W * h + W].astype(F32)
        turned = jnp.concatenate([main, rest[:, 16 * h : 16 * h + 16]], axis=1)
        gb_ref[h] = regroup(regroup(turned, True).T, True)


def finish(sums, gain_row, qkv_weight, factor):
    return pl.pallas_call(
        lambda *refs: finish_kernel(factor, *refs),
        out_shape=[
            jax.ShapeDtypeStruct((D, 3 * D), F32),
            jax.ShapeDtypeStruct((D, D), F32),
            jax.ShapeDtypeStruct((HEADS, W, W), F32),
            jax.ShapeDtypeStruct((1, D), F32),
        ],
        compiler_params=PARAMS,
        name="finish_sums",
    )(sums, gain_row, qkv_weight)


def make_consts(ln_gain, qkv_weight, out_weight):
    wqkv = jnp.pad(qkv_weight.reshape(D, 3, D), ((0, 0), (0, 0), (0, 64))).reshape(D, 768)
    return [ln_gain.reshape(1, D), wqkv, qkv_weight.T, out_weight.T]


def shift(value, axes, steps):
    sizes = [lax.axis_size(a) for a in axes]
    total = 1
    for s in sizes:
        total *= s
    pairs = []
    for source in range(total):
        rest, place = source, []
        for s in reversed(sizes):
            place.append(rest % s)
            rest //= s
        place.reverse()
        target = 0
        for p, s, d in zip(place, sizes, steps):
            target = target * s + (p + d) % s
        pairs.append((source, target))
    return lax.ppermute(value, axes if len(axes) > 1 else axes[0], pairs)


def moved(value, axis, to_of):
    count = lax.axis_size(axis)
    return lax.ppermute(value, axis, [(n, to_of(n)) for n in range(count)])


def flip(value, axis, bits):
    return moved(value, axis, lambda n: n ^ bits)


def lon_core(n):
    return n % 2


def sum_over_devices(sums):
    lon = lax.axis_index("lon")
    core = lon % 2
    y = (lon // 2) % 4
    halves = sums.reshape(2, ROWS // 2, 128)
    low = halves.astype(BF16)
    got = flip(lax.dynamic_index_in_dim(low, 1 - core, 0, keepdims=False), "lon", 1)
    mine = lax.dynamic_index_in_dim(halves, core, 0, keepdims=False) + got.astype(F32)
    quarters = mine.reshape(4, ROWS // 8, 128)
    qlow = quarters.astype(BF16)
    total = lax.dynamic_index_in_dim(quarters, y, 0, keepdims=False)
    for step in range(1, 4):
        piece = lax.dynamic_index_in_dim(qlow, y ^ step, 0, keepdims=False)
        total = total + flip(piece, "lon", 2 * step).astype(F32)
    low = total.astype(BF16)
    for step in range(1, 4):
        total = total + flip(low, "lat", 2 * step).astype(F32)
    low = total.astype(BF16)
    total = (
        total
        + flip(low, "lat", 1).astype(F32)
        + flip(low, "lon", 8).astype(F32)
        + shift_x(low).astype(F32)
    )
    low = total.astype(BF16)
    others = [low] + [flip(low, "lon", 2 * step) for step in range(1, 4)]
    stacked = jnp.stack(others)
    line = jnp.concatenate(
        [lax.dynamic_index_in_dim(stacked, y ^ n, 0, keepdims=True) for n in range(4)], axis=0
    )
    other = flip(line, "lon", 1)
    pair = jnp.stack([line, other])
    return jnp.concatenate(
        [
            lax.dynamic_index_in_dim(pair, core ^ n, 0, keepdims=False).reshape(ROWS // 2, 128)
            for n in range(2)
        ],
        axis=0,
    )


def shift_x(value):
    lat = lax.axis_size("lat")
    total = lax.axis_size("lon") * lat
    pairs = []
    for source in range(total):
        lon_at, lat_at = source // lat, source % lat
        pairs.append((source, (lon_at ^ 8) * lat + (lat_at ^ 1)))
    return lax.ppermute(value, ("lon", "lat"), pairs)


def local(tokens, cotangent, ln_gain, qkv_weight, out_weight, pair_bias):
    levels, lat_count, lon_count, _ = tokens.shape
    x = jnp.transpose(tokens, (0, 2, 1, 3))
    y = jnp.transpose(cotangent, (0, 2, 1, 3))
    s = shift(jnp.stack([x[:, :, :HALF_LAT], y[:, :, :HALF_LAT]]), ("lat",), (-1,))
    e = shift(jnp.stack([x[:, :HALF_LON], y[:, :HALF_LON]]), ("lon",), (-1,))
    c = shift(
        jnp.stack([x[:, :HALF_LON, :HALF_LAT], y[:, :HALF_LON, :HALF_LAT]]), ("lon", "lat"), (-1, -1)
    )
    consts = make_consts(ln_gain, qkv_weight, out_weight)
    last = (lax.axis_index("lat") == lax.axis_size("lat") - 1).astype(jnp.int32).reshape(1, 1)
    inner, gw, gb, bias = inner_windows(x, y, consts, pair_bias, last)
    oe, os_, sums = edge_windows(x, y, e, s, c, consts, bias, (gw, gb))
    back_lat = jnp.concatenate([os_[:, :, 8:11], oe[:, :HALF_LON, 24:27]], axis=1)
    got_lat = shift(back_lat, ("lat",), (1,))
    got_lon = shift(oe[:, HALF_LON:, :24], ("lon",), (1,))
    got_both = shift(oe[:, HALF_LON:, 24:27], ("lon", "lat"), (1, 1))
    sums = sum_over_devices(sums)
    grad_x = assemble(inner, oe, os_, got_lon, got_lat, got_both)
    factor = float(
        levels * lat_count * lax.axis_size("lat") * lon_count * lax.axis_size("lon")
    ) ** (-0.5)
    gq, go, gbias, gg = finish(sums, ln_gain.reshape(1, D), qkv_weight, factor)
    return (jnp.transpose(grad_x, (0, 2, 1, 3)), gq, go, gbias, gg.reshape(D))


def solution(mesh):
    placed = (P(None, "lat", "lon", None), P(None, "lat", "lon", None), P(), P(), P(), P())
    return jax.shard_map(
        local,
        mesh=mesh,
        in_specs=placed,
        out_specs=(P(None, "lat", "lon", None), P(), P(), P(), P()),
        check_vma=False,
    )
```

```python
import jax
import jax.numpy as jnp
from jax import lax
from jax.experimental import pallas as pl
from jax.experimental.pallas import tpu as pltpu
from jax.sharding import PartitionSpec as P

WIN_LEV = 2
WIN_LAT = 6
WIN_LON = 12
W = 144
HEADS = 6
HEAD = 32
D = 192
HALF_LAT = 3
HALF_LON = 6
LANES = 896
LOG2E = 1.4426950408889634
SCALE = HEAD**-0.5
F32 = jnp.float32
BF16 = jnp.bfloat16
WROWS = 6 * D
BROWS = 7 * W
ROWS = 2176

NN = (((1,), (0,)), ((), ()))
NT = (((1,), (1,)), ((), ()))
TN = (((0,), (0,)), ((), ()))


def mm(a, b, dims):
    return lax.dot_general(a, b, dims, preferred_element_type=F32)


def pair_rows(rows, c):
    part = rows[:128, 64 * c : 64 * c + 64]
    first = lax.broadcasted_iota(jnp.int32, (1, 64), 1) < HEAD
    zero = jnp.zeros_like(part)
    return jnp.concatenate([jnp.where(first, part, zero), jnp.where(first, zero, part)], axis=0)


def rest_rows(rows):
    head_of = lax.broadcasted_iota(jnp.int32, (1, D), 1) // HEAD
    rest = rows[128:]
    zero = jnp.zeros_like(rest)
    return jnp.concatenate(
        [jnp.where(head_of == h, rest, zero) for h in range(HEADS)] + [zero, zero], axis=0
    )


def fold_rest(rest):
    head_of = lax.broadcasted_iota(jnp.int32, (1, D), 1) // HEAD
    total = rest[:16]
    for h in range(1, HEADS):
        total = jnp.where(head_of == h, rest[16 * h : 16 * h + 16], total)
    return total


class Window:
    def __init__(self, fetch, put, bias_at, refs):
        self.fetch, self.put, self.bias_at, self.refs = fetch, put, bias_at, refs

    def front(self):
        r = self.refs
        x, dy = self.fetch()
        mean = jnp.mean(x, axis=-1, keepdims=True)
        centred = x - mean
        self.inv_std = lax.rsqrt(jnp.mean(centred * centred, axis=-1, keepdims=True) + 1e-05)
        self.unit = centred * self.inv_std
        self.normed = (self.unit * r["gain"][...]).astype(BF16)
        self.dy = dy
        self.dyb = dy.astype(BF16)
        packed = mm(self.normed, r["wqkv"][...], NN).astype(BF16)
        self.q = packed[:, 0:192]
        self.k = packed[:, 256:448]
        self.v = packed[:, 512:704]
        self.da = mm(self.dyb, r["wout_t"][...], NN).astype(BF16)
        self.kt = self.k.T
        self.vt = self.v.T
        self.raw, self.low, self.dv, self.dk, self.at, self.dqt = {}, {}, {}, {}, {}, {}
        self.qm, self.dam = {}, {}

    def scores(self, c):
        if c < 3:
            cols = slice(64 * c, 64 * c + 64)
            self.qm[c] = pair_rows(self.q, c)
            self.dam[c] = pair_rows(self.da, c)
            k, v = self.k[:, cols], self.v[:, cols]
        else:
            self.qm[c] = rest_rows(self.q)
            self.dam[c] = rest_rows(self.da)
            k, v = self.k, self.v
        self.raw[c] = (mm(k, self.qm[c], NT), mm(v, self.dam[c], NT))

    def softmax(self, c):
        lanes = slice(256 * c, 256 * c + 256) if c < 3 else slice(768, 896)
        raw, dp = self.raw.pop(c)
        s = raw * (SCALE * LOG2E) + self.refs["bias"][self.bias_at, :, lanes]
        e = jnp.exp2(s - jnp.max(s, axis=0, keepdims=True))
        p = e * (1.0 / jnp.sum(e, axis=0, keepdims=True))
        ds = p * (dp - jnp.sum(p * dp, axis=0, keepdims=True))
        self.refs["gb"][:, lanes] += ds
        self.low[c] = (p.astype(BF16), ds.astype(BF16))

    def products(self, c):
        pb, dsb = self.low.pop(c)
        self.dv[c] = mm(pb, self.dam.pop(c), NN)
        self.dk[c] = mm(dsb, self.qm.pop(c), NN)
        if c < 3:
            self.at[c] = mm(self.vt[64 * c : 64 * c + 64], pb, NN)
            self.dqt[c] = mm(self.kt[64 * c : 64 * c + 64], dsb, NN)
        else:
            self.at[c] = fold_rest(mm(pb, self.v, TN))
            self.dqt[c] = fold_rest(mm(dsb, self.k, TN))

    def back(self):
        r = self.refs

        def queries(parts):
            main = [p for c in range(3) for p in (parts[c][:32, :128], parts[c][32:, 128:])]
            return jnp.concatenate([jnp.concatenate(main, axis=0).T, parts[3]], axis=0)

        def keys(parts):
            return jnp.concatenate([parts[c] for c in range(3)], axis=1) + parts[3]

        self.a = queries(self.at).astype(BF16)
        self.dqb = (queries(self.dqt) * SCALE).astype(BF16)
        self.dkb = (keys(self.dk) * SCALE).astype(BF16)
        self.dvb = keys(self.dv).astype(BF16)
        w = r["wqkv_t"]
        dn = mm(self.dqb, w[0:192], NN) + mm(self.dkb, w[192:384], NN) + mm(self.dvb, w[384:576], NN)
        du = dn * r["gain"][...]
        dx = self.inv_std * (
            du
            - jnp.mean(du, axis=-1, keepdims=True)
            - self.unit * jnp.mean(du * self.unit, axis=-1, keepdims=True)
        )
        self.put(self.dy + dx)

    def steps(self):
        yield self.front
        yield lambda: self.scores(0)
        yield lambda: (self.scores(1), self.softmax(0))
        yield lambda: (self.scores(2), self.softmax(1), self.products(0))
        yield lambda: (self.scores(3), self.softmax(2), self.products(1))
        yield lambda: (self.softmax(3), self.products(2))
        yield lambda: self.products(3)
        yield self.back


STAGGER = 4
EARLY = 3


def run_windows(windows, gw_ref):
    plans = [list(w.steps()) for w in windows]
    for tick in range(STAGGER * (len(plans) - 1) + len(plans[0])):
        for n in reversed(range(len(plans))):
            at = tick - STAGGER * n
            if 0 <= at < len(plans[n]):
                plans[n][at]()
    normed = jnp.concatenate([w.normed for w in windows], axis=0)
    for n, name in enumerate(("dqb", "dkb", "dvb")):
        gw_ref[n] += mm(normed, jnp.concatenate([getattr(w, name) for w in windows], axis=0), TN)
    gw_ref[3] += mm(
        jnp.concatenate([w.a for w in windows], axis=0),
        jnp.concatenate([w.dyb for w in windows], axis=0),
        TN,
    )


def fetch_rows(low, high, start, stride):
    lats = [pl.ds(start + n, 24, stride=stride) for n in range(WIN_LAT)]
    return jnp.concatenate(
        [
            jnp.concatenate([low[at, :] for at in lats], axis=0),
            jnp.concatenate([high[at, :] for at in lats], axis=0)[:, :64],
        ],
        axis=1,
    )


def put_rows(low, high, start, stride, value):
    right = jnp.concatenate([value[:, 128:], jnp.zeros((W, 64), F32)], axis=1)
    for n in range(WIN_LAT):
        at = pl.ds(start + n, 24, stride=stride)
        low[at, :] = value[24 * n : 24 * n + 24, :128]
        high[at, :] = right[24 * n : 24 * n + 24]


def keep(low, high, at, rows):
    wide = rows.astype(F32)
    n = rows.shape[0]
    low[at : at + n, :] = wide[:, :128]
    high[at : at + n, :64] = wide[:, 128:]


def kept(low, high, at, n):
    return jnp.concatenate([low[at : at + n, :], high[at : at + n, :64]], axis=1).astype(BF16)


def window_of(scratch, start, stride, bias_at, refs):
    x0, x1, y0, y1, o0, o1 = scratch

    def fetch():
        return fetch_rows(x0, x1, start, stride), fetch_rows(y0, y1, start, stride)

    def put(value):
        put_rows(o0, o1, start, stride, value)

    return Window(fetch, put, bias_at, refs)


def regroup(rows, back=False):
    if back:
        order = [la * 2 + lv for lv in range(2) for la in range(6)]
    else:
        order = [lv * 6 + la for la in range(6) for lv in range(2)]
    return jnp.concatenate([rows[12 * n : 12 * n + 12] for n in order], axis=0)


def lay_bias(pair_ref, last_ref, bias_ref):
    turned = [regroup(regroup(pair_ref[h]).T) * LOG2E for h in range(HEADS)]
    flat = jnp.concatenate(
        [t[:, :128] for t in turned] + [t[:, 128:] for t in turned] + [jnp.zeros((W, 32), F32)],
        axis=1,
    )
    bias_ref[0] = flat
    key_south = lax.broadcasted_iota(jnp.int32, (W, LANES), 0) >= W // 2
    lane = lax.broadcasted_iota(jnp.int32, (W, LANES), 1)
    query_south = (lane >= 768) | (lane % 128 >= W // 2)
    apart = (key_south != query_south) & (last_ref[...] > 0)
    bias_ref[1] = jnp.where(apart, F32(-1e30), flat)


def start_windows(scratch, xs, ys, place):
    for lv in range(2):
        for lon in range(24):
            keep(scratch[0], scratch[1], place(lv, lon), xs[lon // 6][lv, lon % 6])
            keep(scratch[2], scratch[3], place(lv, lon), ys[lon // 6][lv, lon % 6])


def inner_steps(xs, ys, consts, bias, dx_ref, gw_ref, gb_ref, scratch):
    def place(lv, lon):
        return 24 * (24 * (lon // 12) + 12 * lv + lon % 12)

    start_windows(scratch, xs, ys, place)
    refs = dict(zip(("gain", "wqkv", "wqkv_t", "wout_t"), consts), bias=bias, gb=gb_ref)
    run_windows(
        [
            window_of(scratch, 576 * k + 3 + 6 * a, 24, 0, refs)
            for k in range(2)
            for a in range(3)
        ],
        gw_ref,
    )
    for lv in range(2):
        for lon in range(24):
            dx_ref[lv, lon] = kept(scratch[4], scratch[5], place(lv, lon), 24)


def early_kernel(
    x0, x1, x2, x3, y0, y1, y2, y3, gain, wqkv, wqkv_t, wout_t, pair, last, dx_ref, gw_ref, gb_ref, bias_ref, *scratch
):
    @pl.when(pl.program_id(0) == 0)
    def _():
        gw_ref[...] = jnp.zeros_like(gw_ref)
        gb_ref[...] = jnp.zeros_like(gb_ref)
        lay_bias(pair, last, bias_ref)

    consts = (gain, wqkv, wqkv_t, wout_t)
    inner_steps((x0, x1, x2, x3), (y0, y1, y2, y3), consts, bias_ref, dx_ref, gw_ref, gb_ref, scratch)


def late_kernel(
    x0, x1, x2, x3, y0, y1, y2, y3, gain, wqkv, wqkv_t, wout_t, bias, gw_in, gb_in, _, dx_ref, sum_ref, gw_ref, gb_ref, *scratch
):
    @pl.when(pl.program_id(0) == 0)
    def _():
        gw_ref[...] = gw_in[...]
        gb_ref[...] = gb_in[...]

    consts = (gain, wqkv, wqkv_t, wout_t)
    inner_steps((x0, x1, x2, x3), (y0, y1, y2, y3), consts, bias, dx_ref, gw_ref, gb_ref, scratch)

    @pl.when(pl.program_id(0) == pl.num_programs(0) - 1)
    def _():
        whole = jnp.concatenate([gw_ref[n] for n in range(4)], axis=1)
        for t in range(6):
            sum_ref[D * t : D * t + D] = whole[:, 128 * t : 128 * t + 128]
        for t in range(7):
            sum_ref[WROWS + W * t : WROWS + W * t + W] = gb_ref[:, 128 * t : 128 * t + 128]
        sum_ref[WROWS + BROWS :] = jnp.zeros((ROWS - WROWS - BROWS, 128), F32)


def split(rows):
    return rows[:, :128], jnp.concatenate(
        [rows[:, 128:], jnp.zeros((rows.shape[0], 64), F32)], axis=1
    )


def joined(low, high, at):
    return jnp.concatenate([low[at, :], high[at, :][:, :64]], axis=1)


def dense(left, right):
    return jnp.concatenate(
        [left, jnp.concatenate([right[:48], right[48:]], axis=1)], axis=0
    ).astype(BF16)


def undense(packed):
    wide = packed.astype(F32)
    tail = wide[96:]
    high = jnp.concatenate([tail[:, :64], tail[:, 64:]], axis=0)
    return wide[:96], jnp.concatenate([high, jnp.zeros((96, 64), F32)], axis=1)


def pack_kernel(x, y, e_ref, s_ref, c_ref, low, high):
    for n, own in enumerate((x, y)):
        for lv in range(2):
            base = 128 * (2 * n + lv)
            for lon in range(36):
                if lon < 6:
                    e_ref[n, lv, lon] = own[lv, lon]
                    at = pl.ds(base + 96 + lon, 3, stride=8)
                else:
                    at = pl.ds(base + lon - 6, 3, stride=32)
                left, right = split(own[lv, lon].astype(F32)[:8])
                low[at, :] = left[:3]
                high[at, :] = right[:3]
            s_ref[n, lv] = dense(low[base : base + 96, :], high[base : base + 96, :][:, :64])
            c_ref[n, lv] = joined(low, high, pl.ds(base + 96, 24)).astype(BF16)


def edge_kernel(
    x, y, e, s, c, gain, wqkv, wqkv_t, wout_t, bias, gw_in, gb_in, oe_ref, os_ref, be_ref, bs_ref, bc_ref, gw_ref, gb_ref, *scratch
):
    @pl.when(pl.program_id(0) == 0)
    def _():
        gw_ref[...] = gw_in[...]
        gb_ref[...] = gb_in[...]

    def place(lv, lon):
        if lon < 12:
            return 32 * (12 * lv + lon)
        return 768 + 16 * (24 * ((lon - 12) // 12) + 12 * lv + lon % 12)

    def south(lv, t):
        return [
            pl.ds(place(lv, 12) + 8 + t, 12, stride=16),
            pl.ds(place(lv, 24) + 8 + t, 12, stride=16),
            pl.ds(place(lv, 0) + 24 + t, 6, stride=32),
        ]

    def corner(lv, t):
        return pl.ds(place(lv, 6) + 24 + t, 6, stride=32)

    for n, own in enumerate((x, y)):
        low, high = scratch[2 * n], scratch[2 * n + 1]
        for lv in range(2):
            for lon in range(6):
                keep(low, high, place(lv, lon), own[lv, 30 + lon])
                keep(low, high, place(lv, 6 + lon), e[n, lv, lon])
            for lon in range(24):
                keep(low, high, place(lv, 12 + lon), own[lv, 6 + lon].astype(F32)[16:])
            left, right = undense(s[n, lv])
            cleft, cright = split(c[n, lv].astype(F32))
            for t in range(3):
                for m, at in enumerate(south(lv, t)):
                    rows = slice(32 * t + 12 * m, 32 * t + min(12 * m + 12, 30))
                    low[at, :] = left[rows]
                    high[at, :] = right[rows]
                low[corner(lv, t), :] = cleft[8 * t : 8 * t + 6]
                high[corner(lv, t), :] = cright[8 * t : 8 * t + 6]
    refs = dict(
        gain=gain, wqkv=wqkv, wqkv_t=wqkv_t, wout_t=wout_t, bias=bias, gb=gb_ref
    )
    run_windows(
        [window_of(scratch, 3 + 6 * a, 32, int(a == 3), refs) for a in range(4)]
        + [window_of(scratch, 768 + 384 * k + 5, 16, 1, refs) for k in range(2)],
        gw_ref,
    )
    low, high = scratch[4], scratch[5]
    pad = jnp.zeros((2, D), F32)
    for lv in range(2):
        for lon in range(6):
            oe_ref[lv, lon] = kept(low, high, place(lv, lon), 24)
            be_ref[lv, lon] = kept(low, high, place(lv, 6 + lon), 24)
        for lon in range(24):
            os_ref[lv, lon] = kept(low, high, place(lv, 12 + lon), 8)
        parts = []
        corners = []
        for t in range(3):
            parts += [joined(low, high, at) for at in south(lv, t)] + [pad]
            corners += [joined(low, high, corner(lv, t)), pad]
        rows = jnp.concatenate(parts, axis=0)
        bs_ref[lv] = dense(rows[:, :128], rows[:, 128:])
        bc_ref[lv] = jnp.concatenate(corners, axis=0).astype(BF16)


def whole(shape):
    return pl.BlockSpec(shape, lambda *_: (0,) * len(shape))


PARAMS = pltpu.CompilerParams(vmem_limit_bytes=60 * 1024 * 1024)
GW = (4, D, D)
GB = (W, LANES)
BIAS = (2, W, LANES)


def cost(count):
    return pl.CostEstimate(
        flops=count * 144 * 192 * 192 * 40, bytes_accessed=count * 144 * 192 * 6, transcendentals=0
    )


def const_specs():
    return [whole((1, D)), whole((D, 768)), whole((3 * D, D)), whole((D, D))]


def halves(rows):
    return [pltpu.VMEM((rows, 128), F32) for _ in range(6)]


def inner_specs(first):
    def cols(n):
        return pl.BlockSpec((2, 6, 24, D), lambda i: (i + first, n, 0, 0))

    four = [cols(n) for n in range(1, 5)]
    return four + four, pl.BlockSpec((2, 24, 24, D), lambda i: (i + first, 0, 0, 0))


def early_windows(x, y, consts, pair_bias, last, steps):
    ins, out = inner_specs(0)
    return pl.pallas_call(
        early_kernel,
        grid=(steps,),
        in_specs=ins + const_specs() + [whole((HEADS, W, W)), whole((1, 1))],
        out_specs=[out, whole(GW), whole(GB), whole(BIAS)],
        out_shape=[
            jax.ShapeDtypeStruct((x.shape[0], 24, 24, D), BF16),
            jax.ShapeDtypeStruct(GW, F32),
            jax.ShapeDtypeStruct(GB, F32),
            jax.ShapeDtypeStruct(BIAS, F32),
        ],
        scratch_shapes=halves(1152),
        compiler_params=PARAMS,
        cost_estimate=cost(6 * steps),
        name="early_windows",
    )(x, x, x, x, y, y, y, y, *consts, pair_bias, last)


def late_windows(x, y, consts, bias, sums, inner, first):
    steps = x.shape[0] // 2 - first
    ins, out = inner_specs(first)
    return pl.pallas_call(
        late_kernel,
        grid=(steps,),
        in_specs=ins
        + const_specs()
        + [whole(BIAS), whole(GW), whole(GB), pl.BlockSpec(memory_space=pl.ANY)],
        out_specs=[out, whole((ROWS, 128))],
        out_shape=[
            jax.ShapeDtypeStruct(inner.shape, BF16),
            jax.ShapeDtypeStruct((ROWS, 128), F32),
        ],
        scratch_shapes=[pltpu.VMEM(GW, F32), pltpu.VMEM(GB, F32)] + halves(1152),
        input_output_aliases={15: 0},
        compiler_params=PARAMS,
        cost_estimate=cost(6 * steps),
        name="late_windows",
    )(x, x, x, x, y, y, y, y, *consts, bias, *sums, inner)


def both(*rest):
    zeros = (0,) * len(rest)
    return pl.BlockSpec((2, 2) + rest, lambda i: (0, i) + zeros)


def one(*rest):
    zeros = (0,) * len(rest)
    return pl.BlockSpec((2,) + rest, lambda i: (i,) + zeros)


def pack_halo(x, y):
    levels = x.shape[0]
    return pl.pallas_call(
        pack_kernel,
        grid=(levels // 2,),
        in_specs=[one(36, 24, D), one(36, 24, D)],
        out_specs=[both(6, 24, D), both(144, 128), both(24, D)],
        out_shape=[
            jax.ShapeDtypeStruct((2, levels, 6, 24, D), BF16),
            jax.ShapeDtypeStruct((2, levels, 144, 128), BF16),
            jax.ShapeDtypeStruct((2, levels, 24, D), BF16),
        ],
        scratch_shapes=[pltpu.VMEM((512, 128), F32), pltpu.VMEM((512, 128), F32)],
        compiler_params=PARAMS,
        name="pack_halo",
    )(x, y)


def edge_windows(x, y, e, s, c, consts, bias, sums):
    levels = x.shape[0]
    return pl.pallas_call(
        edge_kernel,
        grid=(levels // 2,),
        in_specs=[one(36, 24, D), one(36, 24, D), both(6, 24, D), both(144, 128), both(24, D)]
        + const_specs()
        + [whole(BIAS), whole(GW), whole(GB)],
        out_specs=[
            one(6, 24, D),
            one(24, 8, D),
            one(6, 24, D),
            one(144, 128),
            one(24, D),
            whole(GW),
            whole(GB),
        ],
        out_shape=[
            jax.ShapeDtypeStruct((levels, 6, 24, D), BF16),
            jax.ShapeDtypeStruct((levels, 24, 8, D), BF16),
            jax.ShapeDtypeStruct((levels, 6, 24, D), BF16),
            jax.ShapeDtypeStruct((levels, 144, 128), BF16),
            jax.ShapeDtypeStruct((levels, 24, D), BF16),
            jax.ShapeDtypeStruct(GW, F32),
            jax.ShapeDtypeStruct(GB, F32),
        ],
        scratch_shapes=halves(1536),
        compiler_params=PARAMS,
        cost_estimate=cost(24),
        name="edge_windows",
    )(x, y, e, s, c, *consts, bias, *sums)


def assemble_kernel(inner, oe, os_, gl, gs, gc, out_ref, low, high):
    row = lax.broadcasted_iota(jnp.int32, (8, D), 0)
    for lv in range(2):
        base = 288 * lv
        left, right = undense(gs[lv])
        cleft, cright = split(gc[lv].astype(F32))
        for t in range(3):
            at = pl.ds(base + 48 + t, 30, stride=8)
            low[at, :] = left[32 * t : 32 * t + 30]
            high[at, :] = right[32 * t : 32 * t + 30]
            at = pl.ds(base + t, 6, stride=8)
            low[at, :] = cleft[8 * t : 8 * t + 6]
            high[at, :] = cright[8 * t : 8 * t + 6]
        for lon in range(36):
            if lon < 6:
                rows = gl[lv, lon].astype(F32)
            elif lon < 30:
                rows = inner[lv, lon - 6].astype(F32)
                tail = os_[lv, lon - 6].astype(F32)
                rows = jnp.concatenate([rows[:16], jnp.where(row >= 5, tail, rows[16:])], axis=0)
            else:
                rows = oe[lv, lon - 30].astype(F32)
            head = jnp.where(row < 3, joined(low, high, pl.ds(base + 8 * lon, 8)), rows[:8])
            out_ref[lv, lon] = jnp.concatenate([head, rows[8:]], axis=0).astype(BF16)


def assemble(inner, oe, os_, got_lon, got_lat, got_both):
    levels = inner.shape[0]
    return pl.pallas_call(
        assemble_kernel,
        grid=(levels // 2,),
        in_specs=[
            one(24, 24, D),
            one(6, 24, D),
            one(24, 8, D),
            one(6, 24, D),
            one(144, 128),
            one(24, D),
        ],
        out_specs=one(36, 24, D),
        out_shape=jax.ShapeDtypeStruct((levels, 36, 24, D), BF16),
        scratch_shapes=[pltpu.VMEM((576, 128), F32), pltpu.VMEM((576, 128), F32)],
        compiler_params=PARAMS,
        cost_estimate=pl.CostEstimate(flops=0, bytes_accessed=6_000_000, transcendentals=0),
        name="assemble",
    )(inner, oe, os_, got_lon, got_lat, got_both)


def finish_kernel(factor, sum_ref, gain_ref, w_ref, gq_ref, go_ref, gb_ref, gg_ref):
    both = jnp.concatenate(
        [sum_ref[D * t : D * t + D].astype(F32) for t in range(6)], axis=1
    )
    gq = both[:, : 3 * D] * factor
    gq_ref[...] = gq
    go_ref[...] = both[:, 3 * D :] * factor
    products = (gq * w_ref[...].astype(F32)).T
    gg_ref[...] = jnp.sum(products, axis=0, keepdims=True) / gain_ref[...]
    base = WROWS + 6 * W
    rest = sum_ref[base : base + W].astype(F32)
    for h in range(HEADS):
        main = sum_ref[WROWS + W * h : WROWS + W * h + W].astype(F32)
        turned = jnp.concatenate([main, rest[:, 16 * h : 16 * h + 16]], axis=1)
        gb_ref[h] = regroup(regroup(turned, True).T, True)


def finish(sums, gain_row, qkv_weight, factor):
    return pl.pallas_call(
        lambda *refs: finish_kernel(factor, *refs),
        out_shape=[
            jax.ShapeDtypeStruct((D, 3 * D), F32),
            jax.ShapeDtypeStruct((D, D), F32),
            jax.ShapeDtypeStruct((HEADS, W, W), F32),
            jax.ShapeDtypeStruct((1, D), F32),
        ],
        compiler_params=PARAMS,
        name="finish_sums",
    )(sums, gain_row, qkv_weight)


def make_consts(ln_gain, qkv_weight, out_weight):
    wqkv = jnp.pad(qkv_weight.reshape(D, 3, D), ((0, 0), (0, 0), (0, 64))).reshape(D, 768)
    return [ln_gain.reshape(1, D), wqkv, qkv_weight.T, out_weight.T]


def shift(value, axes, steps):
    sizes = [lax.axis_size(a) for a in axes]
    total = 1
    for s in sizes:
        total *= s
    pairs = []
    for source in range(total):
        rest, place = source, []
        for s in reversed(sizes):
            place.append(rest % s)
            rest //= s
        place.reverse()
        target = 0
        for p, s, d in zip(place, sizes, steps):
            target = target * s + (p + d) % s
        pairs.append((source, target))
    return lax.ppermute(value, axes if len(axes) > 1 else axes[0], pairs)


def moved(value, axis, to_of):
    count = lax.axis_size(axis)
    return lax.ppermute(value, axis, [(n, to_of(n)) for n in range(count)])


def flip(value, axis, bits):
    return moved(value, axis, lambda n: n ^ bits)


def lon_core(n):
    return n % 2


def sum_over_devices(sums):
    lon = lax.axis_index("lon")
    core = lon % 2
    y = (lon // 2) % 4
    halves = sums.reshape(2, ROWS // 2, 128)
    low = halves.astype(BF16)
    got = flip(lax.dynamic_index_in_dim(low, 1 - core, 0, keepdims=False), "lon", 1)
    mine = lax.dynamic_index_in_dim(halves, core, 0, keepdims=False) + got.astype(F32)
    quarters = mine.reshape(4, ROWS // 8, 128)
    qlow = quarters.astype(BF16)
    total = lax.dynamic_index_in_dim(quarters, y, 0, keepdims=False)
    for step in range(1, 4):
        piece = lax.dynamic_index_in_dim(qlow, y ^ step, 0, keepdims=False)
        total = total + flip(piece, "lon", 2 * step).astype(F32)
    low = total.astype(BF16)
    for step in range(1, 4):
        total = total + flip(low, "lat", 2 * step).astype(F32)
    low = total.astype(BF16)
    total = (
        total
        + flip(low, "lat", 1).astype(F32)
        + flip(low, "lon", 8).astype(F32)
        + shift_x(low).astype(F32)
    )
    low = total.astype(BF16)
    others = [low] + [flip(low, "lon", 2 * step) for step in range(1, 4)]
    stacked = jnp.stack(others)
    line = jnp.concatenate(
        [lax.dynamic_index_in_dim(stacked, y ^ n, 0, keepdims=True) for n in range(4)], axis=0
    )
    other = flip(line, "lon", 1)
    pair = jnp.stack([line, other])
    return jnp.concatenate(
        [
            lax.dynamic_index_in_dim(pair, core ^ n, 0, keepdims=False).reshape(ROWS // 2, 128)
            for n in range(2)
        ],
        axis=0,
    )


def shift_x(value):
    lat = lax.axis_size("lat")
    total = lax.axis_size("lon") * lat
    pairs = []
    for source in range(total):
        lon_at, lat_at = source // lat, source % lat
        pairs.append((source, (lon_at ^ 8) * lat + (lat_at ^ 1)))
    return lax.ppermute(value, ("lon", "lat"), pairs)


def local(tokens, cotangent, ln_gain, qkv_weight, out_weight, pair_bias):
    levels, lat_count, lon_count, _ = tokens.shape
    x = jnp.transpose(tokens, (0, 2, 1, 3))
    y = jnp.transpose(cotangent, (0, 2, 1, 3))
    e, s, c = pack_halo(x, y)
    s = shift(s, ("lat",), (-1,))
    e = shift(e, ("lon",), (-1,))
    c = shift(c, ("lon", "lat"), (-1, -1))
    consts = make_consts(ln_gain, qkv_weight, out_weight)
    last = (lax.axis_index("lat") == lax.axis_size("lat") - 1).astype(jnp.int32).reshape(1, 1)
    inner, gw, gb, bias = early_windows(x, y, consts, pair_bias, last, EARLY)
    oe, os_, be, bs, bc, gw, gb = edge_windows(x, y, e, s, c, consts, bias, (gw, gb))
    got_lat = shift(bs, ("lat",), (1,))
    got_lon = shift(be, ("lon",), (1,))
    got_both = shift(bc, ("lon", "lat"), (1, 1))
    inner, sums = late_windows(x, y, consts, bias, (gw, gb), inner, EARLY)
    sums = sum_over_devices(sums)
    grad_x = assemble(inner, oe, os_, got_lon, got_lat, got_both)
    factor = float(
        levels * lat_count * lax.axis_size("lat") * lon_count * lax.axis_size("lon")
    ) ** (-0.5)
    gq, go, gbias, gg = finish(sums, ln_gain.reshape(1, D), qkv_weight, factor)
    return (jnp.transpose(grad_x, (0, 2, 1, 3)), gq, go, gbias, gg.reshape(D))


def solution(mesh):
    placed = (P(None, "lat", "lon", None), P(None, "lat", "lon", None), P(), P(), P(), P())
    return jax.shard_map(
        local,
        mesh=mesh,
        in_specs=placed,
        out_specs=(P(None, "lat", "lon", None), P(), P(), P(), P()),
        check_vma=False,
    )
```

```python
import jax
import jax.numpy as jnp
from jax import lax
from jax.experimental import pallas as pl
from jax.experimental.pallas import tpu as pltpu
from jax.sharding import PartitionSpec as P

WIN_LEV = 2
WIN_LAT = 6
WIN_LON = 12
W = 144
HEADS = 6
HEAD = 32
D = 192
HALF_LAT = 3
HALF_LON = 6
LANES = 896
LOG2E = 1.4426950408889634
SCALE = HEAD**-0.5
F32 = jnp.float32
BF16 = jnp.bfloat16
WROWS = 6 * D
BROWS = 7 * W
ROWS = 2176

NN = (((1,), (0,)), ((), ()))
NT = (((1,), (1,)), ((), ()))
TN = (((0,), (0,)), ((), ()))


def mm(a, b, dims):
    return lax.dot_general(a, b, dims, preferred_element_type=F32)


def pair_rows(rows, c):
    part = rows[:128, 64 * c : 64 * c + 64]
    first = lax.broadcasted_iota(jnp.int32, (1, 64), 1) < HEAD
    zero = jnp.zeros_like(part)
    return jnp.concatenate([jnp.where(first, part, zero), jnp.where(first, zero, part)], axis=0)


def rest_rows(rows):
    head_of = lax.broadcasted_iota(jnp.int32, (1, D), 1) // HEAD
    rest = rows[128:]
    zero = jnp.zeros_like(rest)
    return jnp.concatenate(
        [jnp.where(head_of == h, rest, zero) for h in range(HEADS)] + [zero, zero], axis=0
    )


def fold_rest(rest):
    head_of = lax.broadcasted_iota(jnp.int32, (1, D), 1) // HEAD
    total = rest[:16]
    for h in range(1, HEADS):
        total = jnp.where(head_of == h, rest[16 * h : 16 * h + 16], total)
    return total


class Window:
    def __init__(self, fetch, put, bias_at, refs):
        self.fetch, self.put, self.bias_at, self.refs = fetch, put, bias_at, refs

    def front(self):
        r = self.refs
        x, dy = self.fetch()
        mean = jnp.mean(x, axis=-1, keepdims=True)
        centred = x - mean
        self.inv_std = lax.rsqrt(jnp.mean(centred * centred, axis=-1, keepdims=True) + 1e-05)
        self.unit = centred * self.inv_std
        self.normed = (self.unit * r["gain"][...]).astype(BF16)
        self.dy = dy
        self.dyb = dy.astype(BF16)
        packed = mm(self.normed, r["wqkv"][...], NN).astype(BF16)
        self.q = packed[:, 0:192]
        self.k = packed[:, 256:448]
        self.v = packed[:, 512:704]
        self.da = mm(self.dyb, r["wout_t"][...], NN).astype(BF16)
        self.kt = self.k.T
        self.vt = self.v.T
        self.raw, self.low, self.dv, self.dk, self.at, self.dqt = {}, {}, {}, {}, {}, {}
        self.qm, self.dam = {}, {}

    def scores(self, c):
        if c < 3:
            cols = slice(64 * c, 64 * c + 64)
            self.qm[c] = pair_rows(self.q, c)
            self.dam[c] = pair_rows(self.da, c)
            k, v = self.k[:, cols], self.v[:, cols]
        else:
            self.qm[c] = rest_rows(self.q)
            self.dam[c] = rest_rows(self.da)
            k, v = self.k, self.v
        self.raw[c] = (mm(k, self.qm[c], NT), mm(v, self.dam[c], NT))

    def softmax(self, c):
        lanes = slice(256 * c, 256 * c + 256) if c < 3 else slice(768, 896)
        raw, dp = self.raw.pop(c)
        s = raw * (SCALE * LOG2E) + self.refs["bias"][self.bias_at, :, lanes]
        e = jnp.exp2(s - jnp.max(s, axis=0, keepdims=True))
        p = e * (1.0 / jnp.sum(e, axis=0, keepdims=True))
        ds = p * (dp - jnp.sum(p * dp, axis=0, keepdims=True))
        self.refs["gb"][:, lanes] += ds
        self.low[c] = (p.astype(BF16), ds.astype(BF16))

    def products(self, c):
        pb, dsb = self.low.pop(c)
        self.dv[c] = mm(pb, self.dam.pop(c), NN)
        self.dk[c] = mm(dsb, self.qm.pop(c), NN)
        if c < 3:
            self.at[c] = mm(self.vt[64 * c : 64 * c + 64], pb, NN)
            self.dqt[c] = mm(self.kt[64 * c : 64 * c + 64], dsb, NN)
        else:
            self.at[c] = fold_rest(mm(pb, self.v, TN))
            self.dqt[c] = fold_rest(mm(dsb, self.k, TN))

    def back(self):
        r = self.refs

        def queries(parts):
            main = [p for c in range(3) for p in (parts[c][:32, :128], parts[c][32:, 128:])]
            return jnp.concatenate([jnp.concatenate(main, axis=0).T, parts[3]], axis=0)

        def keys(parts):
            return jnp.concatenate([parts[c] for c in range(3)], axis=1) + parts[3]

        self.a = queries(self.at).astype(BF16)
        self.dqb = (queries(self.dqt) * SCALE).astype(BF16)
        self.dkb = (keys(self.dk) * SCALE).astype(BF16)
        self.dvb = keys(self.dv).astype(BF16)
        w = r["wqkv_t"]
        dn = mm(self.dqb, w[0:192], NN) + mm(self.dkb, w[192:384], NN) + mm(self.dvb, w[384:576], NN)
        du = dn * r["gain"][...]
        dx = self.inv_std * (
            du
            - jnp.mean(du, axis=-1, keepdims=True)
            - self.unit * jnp.mean(du * self.unit, axis=-1, keepdims=True)
        )
        self.put(self.dy + dx)

    def steps(self):
        yield self.front
        yield lambda: self.scores(0)
        yield lambda: (self.scores(1), self.softmax(0))
        yield lambda: (self.scores(2), self.softmax(1), self.products(0))
        yield lambda: (self.scores(3), self.softmax(2), self.products(1))
        yield lambda: (self.softmax(3), self.products(2))
        yield lambda: self.products(3)
        yield self.back


STAGGER = 2
EARLY = 3


def run_windows(windows, gw_ref):
    plans = [list(w.steps()) for w in windows]
    for tick in range(STAGGER * (len(plans) - 1) + len(plans[0])):
        for n in reversed(range(len(plans))):
            at = tick - STAGGER * n
            if 0 <= at < len(plans[n]):
                plans[n][at]()
    normed = jnp.concatenate([w.normed for w in windows], axis=0)
    for n, name in enumerate(("dqb", "dkb", "dvb")):
        gw_ref[n] += mm(normed, jnp.concatenate([getattr(w, name) for w in windows], axis=0), TN)
    gw_ref[3] += mm(
        jnp.concatenate([w.a for w in windows], axis=0),
        jnp.concatenate([w.dyb for w in windows], axis=0),
        TN,
    )


def fetch_rows(low, high, start, stride):
    lats = [pl.ds(start + n, 24, stride=stride) for n in range(WIN_LAT)]
    return jnp.concatenate(
        [
            jnp.concatenate([low[at, :] for at in lats], axis=0),
            jnp.concatenate([high[at, :] for at in lats], axis=0)[:, :64],
        ],
        axis=1,
    )


def put_rows(low, high, start, stride, value):
    right = jnp.concatenate([value[:, 128:], jnp.zeros((W, 64), F32)], axis=1)
    for n in range(WIN_LAT):
        at = pl.ds(start + n, 24, stride=stride)
        low[at, :] = value[24 * n : 24 * n + 24, :128]
        high[at, :] = right[24 * n : 24 * n + 24]


def keep(low, high, at, rows):
    wide = rows.astype(F32)
    n = rows.shape[0]
    low[at : at + n, :] = wide[:, :128]
    high[at : at + n, :64] = wide[:, 128:]


def kept(low, high, at, n):
    return jnp.concatenate([low[at : at + n, :], high[at : at + n, :64]], axis=1).astype(BF16)


def window_of(scratch, start, stride, bias_at, refs):
    x0, x1, y0, y1, o0, o1 = scratch

    def fetch():
        return fetch_rows(x0, x1, start, stride), fetch_rows(y0, y1, start, stride)

    def put(value):
        put_rows(o0, o1, start, stride, value)

    return Window(fetch, put, bias_at, refs)


def regroup(rows, back=False):
    if back:
        order = [la * 2 + lv for lv in range(2) for la in range(6)]
    else:
        order = [lv * 6 + la for la in range(6) for lv in range(2)]
    return jnp.concatenate([rows[12 * n : 12 * n + 12] for n in order], axis=0)


def lay_bias(pair_ref, last_ref, bias_ref):
    turned = [regroup(regroup(pair_ref[h]).T) * LOG2E for h in range(HEADS)]
    flat = jnp.concatenate(
        [t[:, :128] for t in turned] + [t[:, 128:] for t in turned] + [jnp.zeros((W, 32), F32)],
        axis=1,
    )
    bias_ref[0] = flat
    key_south = lax.broadcasted_iota(jnp.int32, (W, LANES), 0) >= W // 2
    lane = lax.broadcasted_iota(jnp.int32, (W, LANES), 1)
    query_south = (lane >= 768) | (lane % 128 >= W // 2)
    apart = (key_south != query_south) & (last_ref[...] > 0)
    bias_ref[1] = jnp.where(apart, F32(-1e30), flat)


def start_windows(scratch, xs, ys, place):
    for lv in range(2):
        for lon in range(24):
            keep(scratch[0], scratch[1], place(lv, lon), xs[lon // 6][lv, lon % 6])
            keep(scratch[2], scratch[3], place(lv, lon), ys[lon // 6][lv, lon % 6])


def inner_steps(xs, ys, consts, bias, dx_ref, gw_ref, gb_ref, scratch):
    def place(lv, lon):
        return 24 * (24 * (lon // 12) + 12 * lv + lon % 12)

    start_windows(scratch, xs, ys, place)
    refs = dict(zip(("gain", "wqkv", "wqkv_t", "wout_t"), consts), bias=bias, gb=gb_ref)
    run_windows(
        [
            window_of(scratch, 576 * k + 3 + 6 * a, 24, 0, refs)
            for k in range(2)
            for a in range(3)
        ],
        gw_ref,
    )
    for lv in range(2):
        for lon in range(24):
            dx_ref[lv, lon] = kept(scratch[4], scratch[5], place(lv, lon), 24)


def early_kernel(
    x0, x1, x2, x3, y0, y1, y2, y3, gain, weight, out_weight, pair, last, dx_ref, gw_ref, gb_ref, bias_ref, wqkv, wqkv_t, wout_t, *scratch
):
    @pl.when(pl.program_id(0) == 0)
    def _():
        gw_ref[...] = jnp.zeros_like(gw_ref)
        gb_ref[...] = jnp.zeros_like(gb_ref)
        lay_bias(pair, last, bias_ref)
        part = weight[...]
        gap = jnp.zeros((D, 64), BF16)
        wqkv[...] = jnp.concatenate(
            [p for n in range(3) for p in (part[:, D * n : D * n + D], gap)], axis=1
        )
        wqkv_t[...] = part.T
        wout_t[...] = out_weight[...].T

    consts = (gain, wqkv, wqkv_t, wout_t)
    inner_steps((x0, x1, x2, x3), (y0, y1, y2, y3), consts, bias_ref, dx_ref, gw_ref, gb_ref, scratch)


def late_kernel(
    x0, x1, x2, x3, y0, y1, y2, y3, gain, wqkv, wqkv_t, wout_t, bias, gw_in, gb_in, core, _, dx_ref, give_ref, mine_ref, gw_ref, gb_ref, sum_ref, *scratch
):
    @pl.when(pl.program_id(0) == 0)
    def _():
        gw_ref[...] = gw_in[...]
        gb_ref[...] = gb_in[...]

    consts = (gain, wqkv, wqkv_t, wout_t)
    inner_steps((x0, x1, x2, x3), (y0, y1, y2, y3), consts, bias, dx_ref, gw_ref, gb_ref, scratch)

    @pl.when(pl.program_id(0) == pl.num_programs(0) - 1)
    def _():
        whole = jnp.concatenate([gw_ref[n] for n in range(4)], axis=1)
        for t in range(6):
            sum_ref[D * t : D * t + D] = whole[:, 128 * t : 128 * t + 128]
        for t in range(7):
            sum_ref[WROWS + W * t : WROWS + W * t + W] = gb_ref[:, 128 * t : 128 * t + 128]
        sum_ref[WROWS + BROWS :] = jnp.zeros((ROWS - WROWS - BROWS, 128), F32)
        first = core[...] == 0
        upper, lower = sum_ref[: ROWS // 2], sum_ref[ROWS // 2 :]
        give_ref[...] = jnp.where(first, lower, upper).astype(BF16)
        mine_ref[...] = jnp.where(first, upper, lower)


def split(rows):
    return rows[:, :128], jnp.concatenate(
        [rows[:, 128:], jnp.zeros((rows.shape[0], 64), F32)], axis=1
    )


def joined(low, high, at):
    return jnp.concatenate([low[at, :], high[at, :][:, :64]], axis=1)


def dense(left, right):
    half = left.shape[0] // 2
    return jnp.concatenate(
        [left, jnp.concatenate([right[:half], right[half:]], axis=1)], axis=0
    ).astype(BF16)


def undense(packed):
    wide = packed.astype(F32)
    rows = 2 * packed.shape[0] // 3
    tail = wide[rows:]
    high = jnp.concatenate([tail[:, :64], tail[:, 64:]], axis=0)
    return wide[:rows], jnp.concatenate([high, jnp.zeros((rows, 64), F32)], axis=1)


def pack_kernel(x, y, e_ref, s_ref, c_ref, low, high):
    for n, own in enumerate((x, y)):
        for lv in range(2):
            base = 128 * (2 * n + lv)
            east = jnp.concatenate([own[lv, lon].astype(F32) for lon in range(6)], axis=0)
            e_ref[n, lv] = dense(east[:, :128], east[:, 128:])
            for lon in range(36):
                if lon < 6:
                    at = pl.ds(base + 96 + lon, 3, stride=8)
                else:
                    at = pl.ds(base + lon - 6, 3, stride=32)
                left, right = split(own[lv, lon].astype(F32)[:8])
                low[at, :] = left[:3]
                high[at, :] = right[:3]
            s_ref[n, lv] = dense(low[base : base + 96, :], high[base : base + 96, :][:, :64])
            c_ref[n, lv] = joined(low, high, pl.ds(base + 96, 24)).astype(BF16)


def edge_kernel(
    x, y, e, s, c, gain, wqkv, wqkv_t, wout_t, bias, gw_in, gb_in, oe_ref, os_ref, be_ref, bs_ref, bc_ref, gw_ref, gb_ref, *scratch
):
    @pl.when(pl.program_id(0) == 0)
    def _():
        gw_ref[...] = gw_in[...]
        gb_ref[...] = gb_in[...]

    def place(lv, lon):
        if lon < 12:
            return 32 * (12 * lv + lon)
        return 768 + 16 * (24 * ((lon - 12) // 12) + 12 * lv + lon % 12)

    def south(lv, t):
        return [
            pl.ds(place(lv, 12) + 8 + t, 12, stride=16),
            pl.ds(place(lv, 24) + 8 + t, 12, stride=16),
            pl.ds(place(lv, 0) + 24 + t, 6, stride=32),
        ]

    def corner(lv, t):
        return pl.ds(place(lv, 6) + 24 + t, 6, stride=32)

    for n, own in enumerate((x, y)):
        low, high = scratch[2 * n], scratch[2 * n + 1]
        for lv in range(2):
            for lon in range(6):
                keep(low, high, place(lv, lon), own[lv, 30 + lon])
            for lon in range(24):
                keep(low, high, place(lv, 12 + lon), own[lv, 6 + lon].astype(F32)[16:])
            left, right = undense(e[n, lv])
            for lon in range(6):
                at = place(lv, 6 + lon)
                low[at : at + 24, :] = left[24 * lon : 24 * lon + 24]
                high[at : at + 24, :] = right[24 * lon : 24 * lon + 24]
            left, right = undense(s[n, lv])
            cleft, cright = split(c[n, lv].astype(F32))
            for t in range(3):
                for m, at in enumerate(south(lv, t)):
                    rows = slice(32 * t + 12 * m, 32 * t + min(12 * m + 12, 30))
                    low[at, :] = left[rows]
                    high[at, :] = right[rows]
                low[corner(lv, t), :] = cleft[8 * t : 8 * t + 6]
                high[corner(lv, t), :] = cright[8 * t : 8 * t + 6]
    refs = dict(
        gain=gain, wqkv=wqkv, wqkv_t=wqkv_t, wout_t=wout_t, bias=bias, gb=gb_ref
    )
    run_windows(
        [window_of(scratch, 3 + 6 * a, 32, int(a == 3), refs) for a in range(4)]
        + [window_of(scratch, 768 + 384 * k + 5, 16, 1, refs) for k in range(2)],
        gw_ref,
    )
    low, high = scratch[4], scratch[5]
    pad = jnp.zeros((2, D), F32)
    for lv in range(2):
        for lon in range(6):
            oe_ref[lv, lon] = kept(low, high, place(lv, lon), 24)
        east = jnp.concatenate(
            [joined(low, high, pl.ds(place(lv, 6 + lon), 24)) for lon in range(6)], axis=0
        )
        be_ref[lv] = dense(east[:, :128], east[:, 128:])
        for lon in range(24):
            os_ref[lv, lon] = kept(low, high, place(lv, 12 + lon), 8)
        parts = []
        corners = []
        for t in range(3):
            parts += [joined(low, high, at) for at in south(lv, t)] + [pad]
            corners += [joined(low, high, corner(lv, t)), pad]
        rows = jnp.concatenate(parts, axis=0)
        bs_ref[lv] = dense(rows[:, :128], rows[:, 128:])
        bc_ref[lv] = jnp.concatenate(corners, axis=0).astype(BF16)


def whole(shape):
    return pl.BlockSpec(shape, lambda *_: (0,) * len(shape))


PARAMS = pltpu.CompilerParams(vmem_limit_bytes=60 * 1024 * 1024)
GW = (4, D, D)
GB = (W, LANES)
BIAS = (2, W, LANES)


def cost(count):
    return pl.CostEstimate(
        flops=count * 144 * 192 * 192 * 40, bytes_accessed=count * 144 * 192 * 6, transcendentals=0
    )


def const_specs():
    return [whole((1, D)), whole((D, 768)), whole((3 * D, D)), whole((D, D))]


def halves(rows):
    return [pltpu.VMEM((rows, 128), F32) for _ in range(6)]


def inner_specs(first):
    def cols(n):
        return pl.BlockSpec((2, 6, 24, D), lambda i: (i + first, n, 0, 0))

    four = [cols(n) for n in range(1, 5)]
    return four + four, pl.BlockSpec((2, 24, 24, D), lambda i: (i + first, 0, 0, 0))


def early_windows(x, y, weights, pair_bias, last, steps):
    ins, out = inner_specs(0)
    return pl.pallas_call(
        early_kernel,
        grid=(steps,),
        in_specs=ins
        + [whole((1, D)), whole((D, 3 * D)), whole((D, D)), whole((HEADS, W, W)), whole((1, 1))],
        out_specs=[out, whole(GW), whole(GB), whole(BIAS)] + const_specs()[1:],
        out_shape=[
            jax.ShapeDtypeStruct((x.shape[0], 24, 24, D), BF16),
            jax.ShapeDtypeStruct(GW, F32),
            jax.ShapeDtypeStruct(GB, F32),
            jax.ShapeDtypeStruct(BIAS, F32),
            jax.ShapeDtypeStruct((D, 768), BF16),
            jax.ShapeDtypeStruct((3 * D, D), BF16),
            jax.ShapeDtypeStruct((D, D), BF16),
        ],
        scratch_shapes=halves(1152),
        compiler_params=PARAMS,
        cost_estimate=cost(6 * steps),
        name="early_windows",
    )(x, x, x, x, y, y, y, y, *weights, pair_bias, last)


def late_windows(x, y, consts, bias, sums, core, inner, first):
    steps = x.shape[0] // 2 - first
    ins, out = inner_specs(first)
    return pl.pallas_call(
        late_kernel,
        grid=(steps,),
        in_specs=ins
        + const_specs()
        + [whole(BIAS), whole(GW), whole(GB), whole((1, 1)), pl.BlockSpec(memory_space=pl.ANY)],
        out_specs=[out, whole((ROWS // 2, 128)), whole((ROWS // 2, 128))],
        out_shape=[
            jax.ShapeDtypeStruct(inner.shape, BF16),
            jax.ShapeDtypeStruct((ROWS // 2, 128), BF16),
            jax.ShapeDtypeStruct((ROWS // 2, 128), F32),
        ],
        scratch_shapes=[pltpu.VMEM(GW, F32), pltpu.VMEM(GB, F32), pltpu.VMEM((ROWS, 128), F32)]
        + halves(1152),
        input_output_aliases={16: 0},
        compiler_params=PARAMS,
        cost_estimate=cost(6 * steps),
        name="late_windows",
    )(x, x, x, x, y, y, y, y, *consts, bias, *sums, core, inner)


def both(*rest):
    zeros = (0,) * len(rest)
    return pl.BlockSpec((2, 2) + rest, lambda i: (0, i) + zeros)


def one(*rest):
    zeros = (0,) * len(rest)
    return pl.BlockSpec((2,) + rest, lambda i: (i,) + zeros)


def pack_halo(x, y):
    levels = x.shape[0]
    return pl.pallas_call(
        pack_kernel,
        grid=(levels // 2,),
        in_specs=[one(36, 24, D), one(36, 24, D)],
        out_specs=[both(216, 128), both(144, 128), both(24, D)],
        out_shape=[
            jax.ShapeDtypeStruct((2, levels, 216, 128), BF16),
            jax.ShapeDtypeStruct((2, levels, 144, 128), BF16),
            jax.ShapeDtypeStruct((2, levels, 24, D), BF16),
        ],
        scratch_shapes=[pltpu.VMEM((512, 128), F32), pltpu.VMEM((512, 128), F32)],
        compiler_params=PARAMS,
        name="pack_halo",
    )(x, y)


def edge_windows(x, y, e, s, c, consts, bias, sums):
    levels = x.shape[0]
    return pl.pallas_call(
        edge_kernel,
        grid=(levels // 2,),
        in_specs=[one(36, 24, D), one(36, 24, D), both(216, 128), both(144, 128), both(24, D)]
        + const_specs()
        + [whole(BIAS), whole(GW), whole(GB)],
        out_specs=[
            one(6, 24, D),
            one(24, 8, D),
            one(216, 128),
            one(144, 128),
            one(24, D),
            whole(GW),
            whole(GB),
        ],
        out_shape=[
            jax.ShapeDtypeStruct((levels, 6, 24, D), BF16),
            jax.ShapeDtypeStruct((levels, 24, 8, D), BF16),
            jax.ShapeDtypeStruct((levels, 216, 128), BF16),
            jax.ShapeDtypeStruct((levels, 144, 128), BF16),
            jax.ShapeDtypeStruct((levels, 24, D), BF16),
            jax.ShapeDtypeStruct(GW, F32),
            jax.ShapeDtypeStruct(GB, F32),
        ],
        scratch_shapes=halves(1536),
        compiler_params=PARAMS,
        cost_estimate=cost(24),
        name="edge_windows",
    )(x, y, e, s, c, *consts, bias, *sums)


def assemble_kernel(inner, oe, os_, gl, gs, gc, out_ref, low, high):
    row = lax.broadcasted_iota(jnp.int32, (8, D), 0)
    for lv in range(2):
        base = 288 * lv
        left, right = undense(gs[lv])
        cleft, cright = split(gc[lv].astype(F32))
        for t in range(3):
            at = pl.ds(base + 48 + t, 30, stride=8)
            low[at, :] = left[32 * t : 32 * t + 30]
            high[at, :] = right[32 * t : 32 * t + 30]
            at = pl.ds(base + t, 6, stride=8)
            low[at, :] = cleft[8 * t : 8 * t + 6]
            high[at, :] = cright[8 * t : 8 * t + 6]
        left, right = undense(gl[lv])
        for lon in range(36):
            if lon < 6:
                at = slice(24 * lon, 24 * lon + 24)
                rows = jnp.concatenate([left[at], right[at, :64]], axis=1)
            elif lon < 30:
                rows = inner[lv, lon - 6].astype(F32)
                tail = os_[lv, lon - 6].astype(F32)
                rows = jnp.concatenate([rows[:16], jnp.where(row >= 5, tail, rows[16:])], axis=0)
            else:
                rows = oe[lv, lon - 30].astype(F32)
            head = jnp.where(row < 3, joined(low, high, pl.ds(base + 8 * lon, 8)), rows[:8])
            out_ref[lv, lon] = jnp.concatenate([head, rows[8:]], axis=0).astype(BF16)


def assemble(inner, oe, os_, got_lon, got_lat, got_both):
    levels = inner.shape[0]
    return pl.pallas_call(
        assemble_kernel,
        grid=(levels // 2,),
        in_specs=[
            one(24, 24, D),
            one(6, 24, D),
            one(24, 8, D),
            one(216, 128),
            one(144, 128),
            one(24, D),
        ],
        out_specs=one(36, 24, D),
        out_shape=jax.ShapeDtypeStruct((levels, 36, 24, D), BF16),
        scratch_shapes=[pltpu.VMEM((576, 128), F32), pltpu.VMEM((576, 128), F32)],
        compiler_params=PARAMS,
        cost_estimate=pl.CostEstimate(flops=0, bytes_accessed=6_000_000, transcendentals=0),
        name="assemble",
    )(inner, oe, os_, got_lon, got_lat, got_both)


def finish_kernel(
    factor, line_ref, other_ref, core, gain_ref, w_ref, gq_ref, go_ref, gb_ref, gg_ref, sum_ref
):
    line, other = line_ref[...].astype(F32), other_ref[...].astype(F32)
    first = core[...] == 0
    sum_ref[: ROWS // 2] = jnp.where(first, line, other)
    sum_ref[ROWS // 2 :] = jnp.where(first, other, line)
    both = jnp.concatenate(
        [sum_ref[D * t : D * t + D] for t in range(6)], axis=1
    )
    gq = both[:, : 3 * D] * factor
    gq_ref[...] = gq
    go_ref[...] = both[:, 3 * D :] * factor
    products = (gq * w_ref[...].astype(F32)).T
    gg_ref[...] = jnp.sum(products, axis=0, keepdims=True) / gain_ref[...]
    base = WROWS + 6 * W
    rest = sum_ref[base : base + W]
    for h in range(HEADS):
        main = sum_ref[WROWS + W * h : WROWS + W * h + W]
        turned = jnp.concatenate([main, rest[:, 16 * h : 16 * h + 16]], axis=1)
        gb_ref[h] = regroup(regroup(turned, True).T, True)


def finish(line, other, core, gain_row, qkv_weight, factor):
    return pl.pallas_call(
        lambda *refs: finish_kernel(factor, *refs),
        out_shape=[
            jax.ShapeDtypeStruct((D, 3 * D), F32),
            jax.ShapeDtypeStruct((D, D), F32),
            jax.ShapeDtypeStruct((HEADS, W, W), F32),
            jax.ShapeDtypeStruct((1, D), F32),
        ],
        scratch_shapes=[pltpu.VMEM((ROWS, 128), F32)],
        compiler_params=PARAMS,
        name="finish_sums",
    )(line, other, core, gain_row, qkv_weight)


def shift(value, axes, steps):
    sizes = [lax.axis_size(a) for a in axes]
    total = 1
    for s in sizes:
        total *= s
    pairs = []
    for source in range(total):
        rest, place = source, []
        for s in reversed(sizes):
            place.append(rest % s)
            rest //= s
        place.reverse()
        target = 0
        for p, s, d in zip(place, sizes, steps):
            target = target * s + (p + d) % s
        pairs.append((source, target))
    return lax.ppermute(value, axes if len(axes) > 1 else axes[0], pairs)


def moved(value, axis, to_of):
    count = lax.axis_size(axis)
    return lax.ppermute(value, axis, [(n, to_of(n)) for n in range(count)])


def flip(value, axis, bits):
    return moved(value, axis, lambda n: n ^ bits)


def lon_core(n):
    return n % 2


def sum_over_devices(give, mine):
    y = (lax.axis_index("lon") // 2) % 4
    mine = mine + flip(give, "lon", 1).astype(F32)
    quarters = mine.reshape(4, ROWS // 8, 128)
    qlow = quarters.astype(BF16)
    total = lax.dynamic_index_in_dim(quarters, y, 0, keepdims=False)
    for step in range(1, 4):
        piece = lax.dynamic_index_in_dim(qlow, y ^ step, 0, keepdims=False)
        total = total + flip(piece, "lon", 2 * step).astype(F32)
    low = total.astype(BF16)
    for step in range(1, 4):
        total = total + flip(low, "lat", 2 * step).astype(F32)
    low = total.astype(BF16)
    total = (
        total
        + flip(low, "lat", 1).astype(F32)
        + flip(low, "lon", 8).astype(F32)
        + shift_x(low).astype(F32)
    )
    low = total.astype(BF16)
    others = [low] + [flip(low, "lon", 2 * step) for step in range(1, 4)]
    stacked = jnp.stack(others)
    line = jnp.concatenate(
        [lax.dynamic_index_in_dim(stacked, y ^ n, 0, keepdims=True) for n in range(4)], axis=0
    )
    return line.reshape(ROWS // 2, 128), flip(line, "lon", 1).reshape(ROWS // 2, 128)


def shift_x(value):
    lat = lax.axis_size("lat")
    total = lax.axis_size("lon") * lat
    pairs = []
    for source in range(total):
        lon_at, lat_at = source // lat, source % lat
        pairs.append((source, (lon_at ^ 8) * lat + (lat_at ^ 1)))
    return lax.ppermute(value, ("lon", "lat"), pairs)


def local(tokens, cotangent, ln_gain, qkv_weight, out_weight, pair_bias):
    levels, lat_count, lon_count, _ = tokens.shape
    x = jnp.transpose(tokens, (0, 2, 1, 3))
    y = jnp.transpose(cotangent, (0, 2, 1, 3))
    e, s, c = pack_halo(x, y)
    s = shift(s, ("lat",), (-1,))
    e = shift(e, ("lon",), (-1,))
    c = shift(c, ("lon", "lat"), (-1, -1))
    gain = ln_gain.reshape(1, D)
    core = (lax.axis_index("lon") % 2).astype(jnp.int32).reshape(1, 1)
    last = (lax.axis_index("lat") == lax.axis_size("lat") - 1).astype(jnp.int32).reshape(1, 1)
    inner, gw, gb, bias, *laid = early_windows(
        x, y, (gain, qkv_weight, out_weight), pair_bias, last, EARLY
    )
    consts = [gain] + laid
    oe, os_, be, bs, bc, gw, gb = edge_windows(x, y, e, s, c, consts, bias, (gw, gb))
    got_lat = shift(bs, ("lat",), (1,))
    got_lon = shift(be, ("lon",), (1,))
    got_both = shift(bc, ("lon", "lat"), (1, 1))
    inner, give, mine = late_windows(x, y, consts, bias, (gw, gb), core, inner, EARLY)
    give, got_lat, got_lon, got_both = lax.optimization_barrier((give, got_lat, got_lon, got_both))
    sums = sum_over_devices(give, mine)
    grad_x = assemble(inner, oe, os_, got_lon, got_lat, got_both)
    factor = float(
        levels * lat_count * lax.axis_size("lat") * lon_count * lax.axis_size("lon")
    ) ** (-0.5)
    gq, go, gbias, gg = finish(*sums, core, gain, qkv_weight, factor)
    return (jnp.transpose(grad_x, (0, 2, 1, 3)), gq, go, gbias, gg.reshape(D))


def solution(mesh):
    placed = (P(None, "lat", "lon", None), P(None, "lat", "lon", None), P(), P(), P(), P())
    return jax.shard_map(
        local,
        mesh=mesh,
        in_specs=placed,
        out_specs=(P(None, "lat", "lon", None), P(), P(), P(), P()),
        check_vma=False,
    )
```

```python
import jax
import jax.numpy as jnp
from jax import lax
from jax.experimental import pallas as pl
from jax.experimental.pallas import tpu as pltpu
from jax.sharding import PartitionSpec as P

WIN_LEV = 2
WIN_LAT = 6
WIN_LON = 12
W = 144
HEADS = 6
HEAD = 32
D = 192
HALF_LAT = 3
HALF_LON = 6
LANES = 896
LOG2E = 1.4426950408889634
SCALE = HEAD**-0.5
F32 = jnp.float32
BF16 = jnp.bfloat16
WROWS = 6 * D
BROWS = 7 * W
ROWS = 2176

NN = (((1,), (0,)), ((), ()))
NT = (((1,), (1,)), ((), ()))
TN = (((0,), (0,)), ((), ()))


def mm(a, b, dims):
    return lax.dot_general(a, b, dims, preferred_element_type=F32)


def pair_rows(rows, c):
    part = rows[:128, 64 * c : 64 * c + 64]
    first = lax.broadcasted_iota(jnp.int32, (1, 64), 1) < HEAD
    zero = jnp.zeros_like(part)
    return jnp.concatenate([jnp.where(first, part, zero), jnp.where(first, zero, part)], axis=0)


def rest_rows(rows):
    head_of = lax.broadcasted_iota(jnp.int32, (1, D), 1) // HEAD
    rest = rows[128:]
    zero = jnp.zeros_like(rest)
    return jnp.concatenate(
        [jnp.where(head_of == h, rest, zero) for h in range(HEADS)] + [zero, zero], axis=0
    )


def fold_rest(rest):
    head_of = lax.broadcasted_iota(jnp.int32, (1, D), 1) // HEAD
    total = rest[:16]
    for h in range(1, HEADS):
        total = jnp.where(head_of == h, rest[16 * h : 16 * h + 16], total)
    return total


class Window:
    def __init__(self, fetch, put, bias_at, refs):
        self.fetch, self.put, self.bias_at, self.refs = fetch, put, bias_at, refs
        self.also_first = self.also_last = lambda: None

    def front(self):
        r = self.refs
        x, dy = self.fetch()
        mean = jnp.mean(x, axis=-1, keepdims=True)
        centred = x - mean
        self.inv_std = lax.rsqrt(jnp.mean(centred * centred, axis=-1, keepdims=True) + 1e-05)
        self.unit = centred * self.inv_std
        self.normed = (self.unit * r["gain"][...]).astype(BF16)
        self.dy = dy
        self.dyb = dy.astype(BF16)
        packed = mm(self.normed, r["wqkv"][...], NN).astype(BF16)
        self.q = packed[:, 0:192]
        self.k = packed[:, 256:448]
        self.v = packed[:, 512:704]
        self.da = mm(self.dyb, r["wout_t"][...], NN).astype(BF16)
        self.kt = self.k.T
        self.vt = self.v.T
        self.raw, self.low, self.dv, self.dk, self.at, self.dqt = {}, {}, {}, {}, {}, {}
        self.qm, self.dam = {}, {}

    def scores(self, c):
        if c < 3:
            cols = slice(64 * c, 64 * c + 64)
            self.qm[c] = pair_rows(self.q, c)
            self.dam[c] = pair_rows(self.da, c)
            k, v = self.k[:, cols], self.v[:, cols]
        else:
            self.qm[c] = rest_rows(self.q)
            self.dam[c] = rest_rows(self.da)
            k, v = self.k, self.v
        self.raw[c] = (mm(k, self.qm[c], NT), mm(v, self.dam[c], NT))

    def softmax(self, c):
        lanes = slice(256 * c, 256 * c + 256) if c < 3 else slice(768, 896)
        raw, dp = self.raw.pop(c)
        s = raw * (SCALE * LOG2E) + self.refs["bias"][self.bias_at, :, lanes]
        e = jnp.exp2(s - jnp.max(s, axis=0, keepdims=True))
        p = e * (1.0 / jnp.sum(e, axis=0, keepdims=True))
        ds = p * (dp - jnp.sum(p * dp, axis=0, keepdims=True))
        self.refs["gb"][:, lanes] += ds
        self.low[c] = (p.astype(BF16), ds.astype(BF16))

    def products(self, c):
        pb, dsb = self.low.pop(c)
        self.dv[c] = mm(pb, self.dam.pop(c), NN)
        self.dk[c] = mm(dsb, self.qm.pop(c), NN)
        if c < 3:
            self.at[c] = mm(self.vt[64 * c : 64 * c + 64], pb, NN)
            self.dqt[c] = mm(self.kt[64 * c : 64 * c + 64], dsb, NN)
        else:
            self.at[c] = fold_rest(mm(pb, self.v, TN))
            self.dqt[c] = fold_rest(mm(dsb, self.k, TN))

    def back(self):
        r = self.refs

        def queries(parts):
            main = [p for c in range(3) for p in (parts[c][:32, :128], parts[c][32:, 128:])]
            return jnp.concatenate([jnp.concatenate(main, axis=0).T, parts[3]], axis=0)

        def keys(parts):
            return jnp.concatenate([parts[c] for c in range(3)], axis=1) + parts[3]

        self.a = queries(self.at).astype(BF16)
        self.dqb = (queries(self.dqt) * SCALE).astype(BF16)
        self.dkb = (keys(self.dk) * SCALE).astype(BF16)
        self.dvb = keys(self.dv).astype(BF16)
        w = r["wqkv_t"]
        dn = mm(self.dqb, w[0:192], NN) + mm(self.dkb, w[192:384], NN) + mm(self.dvb, w[384:576], NN)
        du = dn * r["gain"][...]
        dx = self.inv_std * (
            du
            - jnp.mean(du, axis=-1, keepdims=True)
            - self.unit * jnp.mean(du * self.unit, axis=-1, keepdims=True)
        )
        self.put(self.dy + dx)

    def steps(self):
        yield lambda: (self.front(), self.also_first())
        yield lambda: self.scores(0)
        yield lambda: (self.scores(1), self.softmax(0))
        yield lambda: (self.scores(2), self.softmax(1), self.products(0))
        yield lambda: (self.scores(3), self.softmax(2), self.products(1))
        yield lambda: (self.softmax(3), self.products(2))
        yield lambda: self.products(3)
        yield lambda: (self.back(), self.also_last())


STAGGER = 2
EARLY = 3


def run_windows(windows, gw_ref):
    plans = [list(w.steps()) for w in windows]
    for tick in range(STAGGER * (len(plans) - 1) + len(plans[0])):
        for n in reversed(range(len(plans))):
            at = tick - STAGGER * n
            if 0 <= at < len(plans[n]):
                plans[n][at]()
    normed = jnp.concatenate([w.normed for w in windows], axis=0)
    for n, name in enumerate(("dqb", "dkb", "dvb")):
        gw_ref[n] += mm(normed, jnp.concatenate([getattr(w, name) for w in windows], axis=0), TN)
    gw_ref[3] += mm(
        jnp.concatenate([w.a for w in windows], axis=0),
        jnp.concatenate([w.dyb for w in windows], axis=0),
        TN,
    )


def fetch_rows(low, high, start, stride):
    lats = [pl.ds(start + n, 24, stride=stride) for n in range(WIN_LAT)]
    return jnp.concatenate(
        [
            jnp.concatenate([low[at, :] for at in lats], axis=0),
            jnp.concatenate([high[at, :] for at in lats], axis=0)[:, :64],
        ],
        axis=1,
    )


def put_rows(low, high, start, stride, value):
    right = jnp.concatenate([value[:, 128:], jnp.zeros((W, 64), F32)], axis=1)
    for n in range(WIN_LAT):
        at = pl.ds(start + n, 24, stride=stride)
        low[at, :] = value[24 * n : 24 * n + 24, :128]
        high[at, :] = right[24 * n : 24 * n + 24]


def keep(low, high, at, rows):
    wide = rows.astype(F32)
    n = rows.shape[0]
    low[at : at + n, :] = wide[:, :128]
    high[at : at + n, :64] = wide[:, 128:]


def kept(low, high, at, n):
    return jnp.concatenate([low[at : at + n, :], high[at : at + n, :64]], axis=1).astype(BF16)


def window_of(scratch, start, stride, bias_at, refs):
    x0, x1, y0, y1, o0, o1 = scratch

    def fetch():
        return fetch_rows(x0, x1, start, stride), fetch_rows(y0, y1, start, stride)

    def put(value):
        put_rows(o0, o1, start, stride, value)

    return Window(fetch, put, bias_at, refs)


def regroup(rows, back=False):
    if back:
        order = [la * 2 + lv for lv in range(2) for la in range(6)]
    else:
        order = [lv * 6 + la for la in range(6) for lv in range(2)]
    return jnp.concatenate([rows[12 * n : 12 * n + 12] for n in order], axis=0)


def lay_bias(pair_ref, last_ref, bias_ref):
    turned = [regroup(regroup(pair_ref[h]).T) * LOG2E for h in range(HEADS)]
    flat = jnp.concatenate(
        [t[:, :128] for t in turned] + [t[:, 128:] for t in turned] + [jnp.zeros((W, 32), F32)],
        axis=1,
    )
    bias_ref[0] = flat
    key_south = lax.broadcasted_iota(jnp.int32, (W, LANES), 0) >= W // 2
    lane = lax.broadcasted_iota(jnp.int32, (W, LANES), 1)
    query_south = (lane >= 768) | (lane % 128 >= W // 2)
    apart = (key_south != query_south) & (last_ref[...] > 0)
    bias_ref[1] = jnp.where(apart, F32(-1e30), flat)


def inner_steps(xs, ys, consts, bias, dx_ref, gw_ref, gb_ref, scratch):
    def place(lv, lon):
        return 24 * (24 * (lon // 12) + 12 * lv + lon % 12)

    def take(k):
        for lv in range(2):
            for lon in range(12 * k, 12 * k + 12):
                keep(scratch[0], scratch[1], place(lv, lon), xs[lon // 6][lv, lon % 6])
                keep(scratch[2], scratch[3], place(lv, lon), ys[lon // 6][lv, lon % 6])

    def give(k):
        for lv in range(2):
            for lon in range(12 * k, 12 * k + 12):
                dx_ref[lv, lon] = kept(scratch[4], scratch[5], place(lv, lon), 24)

    take(0)
    refs = dict(zip(("gain", "wqkv", "wqkv_t", "wout_t"), consts), bias=bias, gb=gb_ref)
    windows = [
        window_of(scratch, 576 * k + 3 + 6 * a, 24, 0, refs) for k in range(2) for a in range(3)
    ]
    windows[1].also_first = lambda: take(1)
    windows[2].also_last = lambda: give(0)
    run_windows(windows, gw_ref)
    give(1)


def early_kernel(
    x0, x1, x2, x3, y0, y1, y2, y3, gain, weight, out_weight, pair, last, dx_ref, gw_ref, gb_ref, bias_ref, wqkv, wqkv_t, wout_t, *scratch
):
    @pl.when(pl.program_id(0) == 0)
    def _():
        gw_ref[...] = jnp.zeros_like(gw_ref)
        gb_ref[...] = jnp.zeros_like(gb_ref)
        lay_bias(pair, last, bias_ref)
        part = weight[...]
        gap = jnp.zeros((D, 64), BF16)
        wqkv[...] = jnp.concatenate(
            [p for n in range(3) for p in (part[:, D * n : D * n + D], gap)], axis=1
        )
        wqkv_t[...] = part.T
        wout_t[...] = out_weight[...].T

    consts = (gain, wqkv, wqkv_t, wout_t)
    inner_steps((x0, x1, x2, x3), (y0, y1, y2, y3), consts, bias_ref, dx_ref, gw_ref, gb_ref, scratch)


def late_kernel(
    x0, x1, x2, x3, y0, y1, y2, y3, gain, wqkv, wqkv_t, wout_t, bias, gw_in, gb_in, core, _, dx_ref, give_ref, mine_ref, gw_ref, gb_ref, sum_ref, *scratch
):
    @pl.when(pl.program_id(0) == 0)
    def _():
        gw_ref[...] = gw_in[...]
        gb_ref[...] = gb_in[...]

    consts = (gain, wqkv, wqkv_t, wout_t)
    inner_steps((x0, x1, x2, x3), (y0, y1, y2, y3), consts, bias, dx_ref, gw_ref, gb_ref, scratch)

    @pl.when(pl.program_id(0) == pl.num_programs(0) - 1)
    def _():
        whole = jnp.concatenate([gw_ref[n] for n in range(4)], axis=1)
        for t in range(6):
            sum_ref[D * t : D * t + D] = whole[:, 128 * t : 128 * t + 128]
        for t in range(7):
            sum_ref[WROWS + W * t : WROWS + W * t + W] = gb_ref[:, 128 * t : 128 * t + 128]
        sum_ref[WROWS + BROWS :] = jnp.zeros((ROWS - WROWS - BROWS, 128), F32)
        first = core[...] == 0
        upper, lower = sum_ref[: ROWS // 2], sum_ref[ROWS // 2 :]
        give_ref[...] = jnp.where(first, lower, upper).astype(BF16)
        mine_ref[...] = jnp.where(first, upper, lower)


def split(rows):
    return rows[:, :128], jnp.concatenate(
        [rows[:, 128:], jnp.zeros((rows.shape[0], 64), F32)], axis=1
    )


def joined(low, high, at):
    return jnp.concatenate([low[at, :], high[at, :][:, :64]], axis=1)


def dense(left, right):
    half = left.shape[0] // 2
    return jnp.concatenate(
        [left, jnp.concatenate([right[:half], right[half:]], axis=1)], axis=0
    ).astype(BF16)


def undense(packed):
    wide = packed.astype(F32)
    rows = 2 * packed.shape[0] // 3
    tail = wide[rows:]
    high = jnp.concatenate([tail[:, :64], tail[:, 64:]], axis=0)
    return wide[:rows], jnp.concatenate([high, jnp.zeros((rows, 64), F32)], axis=1)


def dense_corner(rows):
    right = jnp.concatenate([rows[:18, 128:], rows[18:, 128:]], axis=1)
    return jnp.concatenate([rows[:, :128], right, jnp.zeros((2, 128), F32)], axis=0).astype(BF16)


def undense_corner(packed):
    wide = packed.astype(F32)
    high = jnp.concatenate([wide[36:54, :64], wide[36:54, 64:]], axis=0)
    return wide[:36], jnp.concatenate([high, jnp.zeros((36, 64), F32)], axis=1)


def pack_kernel(x, y, e_ref, s_ref, c_ref, low, high):
    for n, own in enumerate((x, y)):
        for lv in range(2):
            base = 128 * (2 * n + lv)
            east = jnp.concatenate([own[lv, lon].astype(F32) for lon in range(6)], axis=0)
            e_ref[n, lv] = dense(east[:, :128], east[:, 128:])
            for lon in range(36):
                if lon < 6:
                    at = pl.ds(base + 96 + lon, 3, stride=8)
                else:
                    at = pl.ds(base + lon - 6, 3, stride=32)
                left, right = split(own[lv, lon].astype(F32)[:8])
                low[at, :] = left[:3]
                high[at, :] = right[:3]
            s_ref[n, lv] = dense(low[base : base + 96, :], high[base : base + 96, :][:, :64])
        c_ref[n, 0] = dense_corner(
            jnp.concatenate(
                [
                    joined(low, high, pl.ds(128 * (2 * n + lv) + 96 + 8 * t, 8))[:6]
                    for lv in range(2)
                    for t in range(3)
                ],
                axis=0,
            )
        )


def edge_kernel(
    x, y, e, s, c, gain, wqkv, wqkv_t, wout_t, bias, gw_in, gb_in, oe_ref, os_ref, be_ref, bs_ref, bc_ref, gw_ref, gb_ref, *scratch
):
    @pl.when(pl.program_id(0) == 0)
    def _():
        gw_ref[...] = gw_in[...]
        gb_ref[...] = gb_in[...]

    def place(lv, lon):
        if lon < 12:
            return 32 * (12 * lv + lon)
        return 768 + 16 * (24 * ((lon - 12) // 12) + 12 * lv + lon % 12)

    def south(lv, t):
        return [
            pl.ds(place(lv, 12) + 8 + t, 12, stride=16),
            pl.ds(place(lv, 24) + 8 + t, 12, stride=16),
            pl.ds(place(lv, 0) + 24 + t, 6, stride=32),
        ]

    def corner(lv, t):
        return pl.ds(place(lv, 6) + 24 + t, 6, stride=32)

    for n, own in enumerate((x, y)):
        low, high = scratch[2 * n], scratch[2 * n + 1]
        cleft, cright = undense_corner(c[n, 0])
        for lv in range(2):
            for lon in range(6):
                keep(low, high, place(lv, lon), own[lv, 30 + lon])
            for lon in range(24):
                keep(low, high, place(lv, 12 + lon), own[lv, 6 + lon].astype(F32)[16:])
            left, right = undense(e[n, lv])
            for lon in range(6):
                at = place(lv, 6 + lon)
                low[at : at + 24, :] = left[24 * lon : 24 * lon + 24]
                high[at : at + 24, :] = right[24 * lon : 24 * lon + 24]
            left, right = undense(s[n, lv])
            for t in range(3):
                for m, at in enumerate(south(lv, t)):
                    rows = slice(32 * t + 12 * m, 32 * t + min(12 * m + 12, 30))
                    low[at, :] = left[rows]
                    high[at, :] = right[rows]
                rows = slice(18 * lv + 6 * t, 18 * lv + 6 * t + 6)
                low[corner(lv, t), :] = cleft[rows]
                high[corner(lv, t), :] = cright[rows]
    refs = dict(
        gain=gain, wqkv=wqkv, wqkv_t=wqkv_t, wout_t=wout_t, bias=bias, gb=gb_ref
    )
    run_windows(
        [window_of(scratch, 3 + 6 * a, 32, int(a == 3), refs) for a in range(4)]
        + [window_of(scratch, 768 + 384 * k + 5, 16, 1, refs) for k in range(2)],
        gw_ref,
    )
    low, high = scratch[4], scratch[5]
    pad = jnp.zeros((2, D), F32)
    corners = []
    for lv in range(2):
        for lon in range(6):
            oe_ref[lv, lon] = kept(low, high, place(lv, lon), 24)
        east = jnp.concatenate(
            [joined(low, high, pl.ds(place(lv, 6 + lon), 24)) for lon in range(6)], axis=0
        )
        be_ref[lv] = dense(east[:, :128], east[:, 128:])
        for lon in range(24):
            os_ref[lv, lon] = kept(low, high, place(lv, 12 + lon), 8)
        parts = []
        for t in range(3):
            parts += [joined(low, high, at) for at in south(lv, t)] + [pad]
            corners.append(joined(low, high, corner(lv, t)))
        rows = jnp.concatenate(parts, axis=0)
        bs_ref[lv] = dense(rows[:, :128], rows[:, 128:])
    bc_ref[0] = dense_corner(jnp.concatenate(corners, axis=0))


def whole(shape):
    return pl.BlockSpec(shape, lambda *_: (0,) * len(shape))


PARAMS = pltpu.CompilerParams(vmem_limit_bytes=60 * 1024 * 1024)
GW = (4, D, D)
GB = (W, LANES)
BIAS = (2, W, LANES)


def cost(count):
    return pl.CostEstimate(
        flops=count * 144 * 192 * 192 * 40, bytes_accessed=count * 144 * 192 * 6, transcendentals=0
    )


def const_specs():
    return [whole((1, D)), whole((D, 768)), whole((3 * D, D)), whole((D, D))]


def halves(rows):
    return [pltpu.VMEM((rows, 128), F32) for _ in range(6)]


def inner_specs(first):
    def cols(n):
        return pl.BlockSpec((2, 6, 24, D), lambda i: (i + first, n, 0, 0))

    four = [cols(n) for n in range(1, 5)]
    return four + four, pl.BlockSpec((2, 24, 24, D), lambda i: (i + first, 0, 0, 0))


def early_windows(x, y, weights, pair_bias, last, steps):
    ins, out = inner_specs(0)
    return pl.pallas_call(
        early_kernel,
        grid=(steps,),
        in_specs=ins
        + [whole((1, D)), whole((D, 3 * D)), whole((D, D)), whole((HEADS, W, W)), whole((1, 1))],
        out_specs=[out, whole(GW), whole(GB), whole(BIAS)] + const_specs()[1:],
        out_shape=[
            jax.ShapeDtypeStruct((x.shape[0], 24, 24, D), BF16),
            jax.ShapeDtypeStruct(GW, F32),
            jax.ShapeDtypeStruct(GB, F32),
            jax.ShapeDtypeStruct(BIAS, F32),
            jax.ShapeDtypeStruct((D, 768), BF16),
            jax.ShapeDtypeStruct((3 * D, D), BF16),
            jax.ShapeDtypeStruct((D, D), BF16),
        ],
        scratch_shapes=halves(1152),
        compiler_params=PARAMS,
        cost_estimate=cost(6 * steps),
        name="early_windows",
    )(x, x, x, x, y, y, y, y, *weights, pair_bias, last)


def late_windows(x, y, consts, bias, sums, core, inner, first):
    steps = x.shape[0] // 2 - first
    ins, out = inner_specs(first)
    return pl.pallas_call(
        late_kernel,
        grid=(steps,),
        in_specs=ins
        + const_specs()
        + [whole(BIAS), whole(GW), whole(GB), whole((1, 1)), pl.BlockSpec(memory_space=pl.ANY)],
        out_specs=[out, whole((ROWS // 2, 128)), whole((ROWS // 2, 128))],
        out_shape=[
            jax.ShapeDtypeStruct(inner.shape, BF16),
            jax.ShapeDtypeStruct((ROWS // 2, 128), BF16),
            jax.ShapeDtypeStruct((ROWS // 2, 128), F32),
        ],
        scratch_shapes=[pltpu.VMEM(GW, F32), pltpu.VMEM(GB, F32), pltpu.VMEM((ROWS, 128), F32)]
        + halves(1152),
        input_output_aliases={16: 0},
        compiler_params=PARAMS,
        cost_estimate=cost(6 * steps),
        name="late_windows",
    )(x, x, x, x, y, y, y, y, *consts, bias, *sums, core, inner)


def both(*rest):
    zeros = (0,) * len(rest)
    return pl.BlockSpec((2, 2) + rest, lambda i: (0, i) + zeros)


def one(*rest):
    zeros = (0,) * len(rest)
    return pl.BlockSpec((2,) + rest, lambda i: (i,) + zeros)


def both_corner():
    return pl.BlockSpec((2, 1, 56, 128), lambda i: (0, i, 0, 0))


def one_corner():
    return pl.BlockSpec((1, 56, 128), lambda i: (i, 0, 0))


def pack_halo(x, y):
    levels = x.shape[0]
    return pl.pallas_call(
        pack_kernel,
        grid=(levels // 2,),
        in_specs=[one(36, 24, D), one(36, 24, D)],
        out_specs=[both(216, 128), both(144, 128), both_corner()],
        out_shape=[
            jax.ShapeDtypeStruct((2, levels, 216, 128), BF16),
            jax.ShapeDtypeStruct((2, levels, 144, 128), BF16),
            jax.ShapeDtypeStruct((2, levels // 2, 56, 128), BF16),
        ],
        scratch_shapes=[pltpu.VMEM((512, 128), F32), pltpu.VMEM((512, 128), F32)],
        compiler_params=PARAMS,
        name="pack_halo",
    )(x, y)


def edge_windows(x, y, e, s, c, consts, bias, sums):
    levels = x.shape[0]
    return pl.pallas_call(
        edge_kernel,
        grid=(levels // 2,),
        in_specs=[one(36, 24, D), one(36, 24, D), both(216, 128), both(144, 128), both_corner()]
        + const_specs()
        + [whole(BIAS), whole(GW), whole(GB)],
        out_specs=[
            one(6, 24, D),
            one(24, 8, D),
            one(216, 128),
            one(144, 128),
            one_corner(),
            whole(GW),
            whole(GB),
        ],
        out_shape=[
            jax.ShapeDtypeStruct((levels, 6, 24, D), BF16),
            jax.ShapeDtypeStruct((levels, 24, 8, D), BF16),
            jax.ShapeDtypeStruct((levels, 216, 128), BF16),
            jax.ShapeDtypeStruct((levels, 144, 128), BF16),
            jax.ShapeDtypeStruct((levels // 2, 56, 128), BF16),
            jax.ShapeDtypeStruct(GW, F32),
            jax.ShapeDtypeStruct(GB, F32),
        ],
        scratch_shapes=halves(1536),
        compiler_params=PARAMS,
        cost_estimate=cost(24),
        name="edge_windows",
    )(x, y, e, s, c, *consts, bias, *sums)


def assemble_kernel(inner, oe, os_, gl, gs, gc, *rest):
    out_ref, low, high = rest[-3:]
    row = lax.broadcasted_iota(jnp.int32, (8, D), 0)
    cleft, cright = undense_corner(gc[0])
    for lv in range(2):
        base = 288 * lv
        left, right = undense(gs[lv])
        for t in range(3):
            at = pl.ds(base + 48 + t, 30, stride=8)
            low[at, :] = left[32 * t : 32 * t + 30]
            high[at, :] = right[32 * t : 32 * t + 30]
            at = pl.ds(base + t, 6, stride=8)
            rows = slice(18 * lv + 6 * t, 18 * lv + 6 * t + 6)
            low[at, :] = cleft[rows]
            high[at, :] = cright[rows]
        left, right = undense(gl[lv])
        for lon in range(36):
            if lon < 6:
                at = slice(24 * lon, 24 * lon + 24)
                rows = jnp.concatenate([left[at], right[at, :64]], axis=1)
            elif lon < 30:
                rows = inner[lv, lon - 6].astype(F32)
                tail = os_[lv, lon - 6].astype(F32)
                rows = jnp.concatenate([rows[:16], jnp.where(row >= 5, tail, rows[16:])], axis=0)
            else:
                rows = oe[lv, lon - 30].astype(F32)
            head = jnp.where(row < 3, joined(low, high, pl.ds(base + 8 * lon, 8)), rows[:8])
            out_ref[lv, lon] = jnp.concatenate([head, rows[8:]], axis=0).astype(BF16)


def assemble(first, steps, grad_x, inner, oe, os_, got_lon, got_lat, got_both):
    def at(count, *rest):
        zeros = (0,) * len(rest)
        return pl.BlockSpec((count,) + rest, lambda i: (i + first,) + zeros)

    ins = [inner, oe, os_, got_lon, got_lat, got_both]
    specs = [
        at(2, 24, 24, D),
        at(2, 6, 24, D),
        at(2, 24, 8, D),
        at(2, 216, 128),
        at(2, 144, 128),
        at(1, 56, 128),
    ]
    aliases = {}
    if grad_x is not None:
        ins.append(grad_x)
        specs.append(pl.BlockSpec(memory_space=pl.ANY))
        aliases = {6: 0}
    return pl.pallas_call(
        assemble_kernel,
        grid=(steps,),
        in_specs=specs,
        out_specs=at(2, 36, 24, D),
        out_shape=jax.ShapeDtypeStruct((inner.shape[0], 36, 24, D), BF16),
        scratch_shapes=[pltpu.VMEM((576, 128), F32), pltpu.VMEM((576, 128), F32)],
        input_output_aliases=aliases,
        compiler_params=PARAMS,
        cost_estimate=pl.CostEstimate(
            flops=0, bytes_accessed=1_500_000 * steps, transcendentals=0
        ),
        name="assemble",
    )(*ins)


def finish_kernel(
    factor, line_ref, other_ref, core, gain_ref, w_ref, gq_ref, go_ref, gb_ref, gg_ref, sum_ref
):
    line, other = line_ref[...].astype(F32), other_ref[...].astype(F32)
    first = core[...] == 0
    sum_ref[: ROWS // 2] = jnp.where(first, line, other)
    sum_ref[ROWS // 2 :] = jnp.where(first, other, line)
    both = jnp.concatenate(
        [sum_ref[D * t : D * t + D] for t in range(6)], axis=1
    )
    gq = both[:, : 3 * D] * factor
    gq_ref[...] = gq
    go_ref[...] = both[:, 3 * D :] * factor
    products = (gq * w_ref[...].astype(F32)).T
    gg_ref[...] = jnp.sum(products, axis=0, keepdims=True) / gain_ref[...]
    base = WROWS + 6 * W
    rest = sum_ref[base : base + W]
    for h in range(HEADS):
        main = sum_ref[WROWS + W * h : WROWS + W * h + W]
        turned = jnp.concatenate([main, rest[:, 16 * h : 16 * h + 16]], axis=1)
        gb_ref[h] = regroup(regroup(turned, True).T, True)


def finish(line, other, core, gain_row, qkv_weight, factor):
    return pl.pallas_call(
        lambda *refs: finish_kernel(factor, *refs),
        out_shape=[
            jax.ShapeDtypeStruct((D, 3 * D), F32),
            jax.ShapeDtypeStruct((D, D), F32),
            jax.ShapeDtypeStruct((HEADS, W, W), F32),
            jax.ShapeDtypeStruct((1, D), F32),
        ],
        scratch_shapes=[pltpu.VMEM((ROWS, 128), F32)],
        compiler_params=PARAMS,
        name="finish_sums",
    )(line, other, core, gain_row, qkv_weight)


def shift(value, axes, steps):
    sizes = [lax.axis_size(a) for a in axes]
    total = 1
    for s in sizes:
        total *= s
    pairs = []
    for source in range(total):
        rest, place = source, []
        for s in reversed(sizes):
            place.append(rest % s)
            rest //= s
        place.reverse()
        target = 0
        for p, s, d in zip(place, sizes, steps):
            target = target * s + (p + d) % s
        pairs.append((source, target))
    return lax.ppermute(value, axes if len(axes) > 1 else axes[0], pairs)


def moved(value, axis, to_of):
    count = lax.axis_size(axis)
    return lax.ppermute(value, axis, [(n, to_of(n)) for n in range(count)])


def flip(value, axis, bits):
    return moved(value, axis, lambda n: n ^ bits)


def lon_core(n):
    return n % 2


def sum_over_devices(give, mine, beside):
    y = (lax.axis_index("lon") // 2) % 4
    mine = mine + flip(give, "lon", 1).astype(F32)
    quarters = mine.reshape(4, ROWS // 8, 128)
    qlow = quarters.astype(BF16)
    total = lax.dynamic_index_in_dim(quarters, y, 0, keepdims=False)
    for step in range(1, 4):
        piece = lax.dynamic_index_in_dim(qlow, y ^ step, 0, keepdims=False)
        total = total + flip(piece, "lon", 2 * step).astype(F32)
    total, grad_x = lax.optimization_barrier((total, beside(0, None)))
    low = total.astype(BF16)
    for step in range(1, 4):
        total = total + flip(low, "lat", 2 * step).astype(F32)
    total, grad_x = lax.optimization_barrier((total, beside(1, grad_x)))
    low = total.astype(BF16)
    total = (
        total
        + flip(low, "lat", 1).astype(F32)
        + flip(low, "lon", 8).astype(F32)
        + shift_x(low).astype(F32)
    )
    low = total.astype(BF16)
    others = [low] + [flip(low, "lon", 2 * step) for step in range(1, 4)]
    stacked = jnp.stack(others)
    line = jnp.concatenate(
        [lax.dynamic_index_in_dim(stacked, y ^ n, 0, keepdims=True) for n in range(4)], axis=0
    )
    other = flip(line, "lon", 1)
    return line.reshape(ROWS // 2, 128), other.reshape(ROWS // 2, 128), grad_x


def shift_x(value):
    lat = lax.axis_size("lat")
    total = lax.axis_size("lon") * lat
    pairs = []
    for source in range(total):
        lon_at, lat_at = source // lat, source % lat
        pairs.append((source, (lon_at ^ 8) * lat + (lat_at ^ 1)))
    return lax.ppermute(value, ("lon", "lat"), pairs)


def local(tokens, cotangent, ln_gain, qkv_weight, out_weight, pair_bias):
    levels, lat_count, lon_count, _ = tokens.shape
    x = jnp.transpose(tokens, (0, 2, 1, 3))
    y = jnp.transpose(cotangent, (0, 2, 1, 3))
    e, s, c = pack_halo(x, y)
    s = shift(s, ("lat",), (-1,))
    e = shift(e, ("lon",), (-1,))
    c = shift(c, ("lon", "lat"), (-1, -1))
    gain = ln_gain.reshape(1, D)
    core = (lax.axis_index("lon") % 2).astype(jnp.int32).reshape(1, 1)
    last = (lax.axis_index("lat") == lax.axis_size("lat") - 1).astype(jnp.int32).reshape(1, 1)
    inner, gw, gb, bias, *laid = early_windows(
        x, y, (gain, qkv_weight, out_weight), pair_bias, last, EARLY
    )
    consts = [gain] + laid
    oe, os_, be, bs, bc, gw, gb = edge_windows(x, y, e, s, c, consts, bias, (gw, gb))
    got_lat = shift(bs, ("lat",), (1,))
    got_lon = shift(be, ("lon",), (1,))
    got_both = shift(bc, ("lon", "lat"), (1, 1))
    inner, give, mine = late_windows(x, y, consts, bias, (gw, gb), core, inner, EARLY)
    give, got_lat, got_lon, got_both = lax.optimization_barrier((give, got_lat, got_lon, got_both))
    half = levels // 4

    def beside(part, grad_x):
        return assemble(half * part, half, grad_x, inner, oe, os_, got_lon, got_lat, got_both)

    *sums, grad_x = sum_over_devices(give, mine, beside)
    factor = float(
        levels * lat_count * lax.axis_size("lat") * lon_count * lax.axis_size("lon")
    ) ** (-0.5)
    gq, go, gbias, gg = finish(*sums, core, gain, qkv_weight, factor)
    return (jnp.transpose(grad_x, (0, 2, 1, 3)), gq, go, gbias, gg.reshape(D))


def solution(mesh):
    placed = (P(None, "lat", "lon", None), P(None, "lat", "lon", None), P(), P(), P(), P())
    return jax.shard_map(
        local,
        mesh=mesh,
        in_specs=placed,
        out_specs=(P(None, "lat", "lon", None), P(), P(), P(), P()),
        check_vma=False,
    )
```

```python
import jax
import jax.numpy as jnp
from jax import lax
from jax.experimental import pallas as pl
from jax.experimental.pallas import tpu as pltpu
from jax.sharding import PartitionSpec as P

WIN_LEV = 2
WIN_LAT = 6
WIN_LON = 12
W = 144
HEADS = 6
HEAD = 32
D = 192
HALF_LAT = 3
HALF_LON = 6
LANES = 896
LOG2E = 1.4426950408889634
SCALE = HEAD**-0.5
F32 = jnp.float32
BF16 = jnp.bfloat16
WROWS = 6 * D
BROWS = 7 * W
ROWS = 2176

NN = (((1,), (0,)), ((), ()))
NT = (((1,), (1,)), ((), ()))
TN = (((0,), (0,)), ((), ()))


def mm(a, b, dims):
    return lax.dot_general(a, b, dims, preferred_element_type=F32)


def pair_rows(rows, c):
    part = rows[:128, 64 * c : 64 * c + 64]
    first = lax.broadcasted_iota(jnp.int32, (1, 64), 1) < HEAD
    zero = jnp.zeros_like(part)
    return jnp.concatenate([jnp.where(first, part, zero), jnp.where(first, zero, part)], axis=0)


def rest_rows(rows):
    head_of = lax.broadcasted_iota(jnp.int32, (1, D), 1) // HEAD
    rest = rows[128:]
    zero = jnp.zeros_like(rest)
    return jnp.concatenate(
        [jnp.where(head_of == h, rest, zero) for h in range(HEADS)] + [zero, zero], axis=0
    )


def fold_rest(rest):
    head_of = lax.broadcasted_iota(jnp.int32, (1, D), 1) // HEAD
    total = rest[:16]
    for h in range(1, HEADS):
        total = jnp.where(head_of == h, rest[16 * h : 16 * h + 16], total)
    return total


class Window:
    def __init__(self, fetch, put, bias_at, refs):
        self.fetch, self.put, self.bias_at, self.refs = fetch, put, bias_at, refs
        self.also_first = self.also_last = lambda: None

    def front(self):
        r = self.refs
        x, dy = self.fetch()
        mean = jnp.mean(x, axis=-1, keepdims=True)
        centred = x - mean
        self.inv_std = lax.rsqrt(jnp.mean(centred * centred, axis=-1, keepdims=True) + 1e-05)
        self.unit = centred * self.inv_std
        self.normed = (self.unit * r["gain"][...]).astype(BF16)
        self.dy = dy
        self.dyb = dy.astype(BF16)
        packed = mm(self.normed, r["wqkv"][...], NN).astype(BF16)
        self.q = packed[:, 0:192]
        self.k = packed[:, 256:448]
        self.v = packed[:, 512:704]
        self.da = mm(self.dyb, r["wout_t"][...], NN).astype(BF16)
        self.kt = self.k.T
        self.vt = self.v.T
        self.raw, self.low, self.dv, self.dk, self.at, self.dqt = {}, {}, {}, {}, {}, {}
        self.qm, self.dam = {}, {}

    def scores(self, c):
        if c < 3:
            cols = slice(64 * c, 64 * c + 64)
            self.qm[c] = pair_rows(self.q, c)
            self.dam[c] = pair_rows(self.da, c)
            k, v = self.k[:, cols], self.v[:, cols]
        else:
            self.qm[c] = rest_rows(self.q)
            self.dam[c] = rest_rows(self.da)
            k, v = self.k, self.v
        self.raw[c] = (mm(k, self.qm[c], NT), mm(v, self.dam[c], NT))

    def softmax(self, c):
        lanes = slice(256 * c, 256 * c + 256) if c < 3 else slice(768, 896)
        raw, dp = self.raw.pop(c)
        s = raw * (SCALE * LOG2E) + self.refs["bias"][self.bias_at, :, lanes]
        e = jnp.exp2(s - jnp.max(s, axis=0, keepdims=True))
        p = e * (1.0 / jnp.sum(e, axis=0, keepdims=True))
        ds = p * (dp - jnp.sum(p * dp, axis=0, keepdims=True))
        self.refs["gb"][:, lanes] += ds
        self.low[c] = (p.astype(BF16), ds.astype(BF16))

    def products(self, c):
        pb, dsb = self.low.pop(c)
        self.dv[c] = mm(pb, self.dam.pop(c), NN)
        self.dk[c] = mm(dsb, self.qm.pop(c), NN)
        if c < 3:
            self.at[c] = mm(self.vt[64 * c : 64 * c + 64], pb, NN)
            self.dqt[c] = mm(self.kt[64 * c : 64 * c + 64], dsb, NN)
        else:
            self.at[c] = fold_rest(mm(pb, self.v, TN))
            self.dqt[c] = fold_rest(mm(dsb, self.k, TN))

    def back(self):
        r = self.refs

        def queries(parts):
            main = [p for c in range(3) for p in (parts[c][:32, :128], parts[c][32:, 128:])]
            return jnp.concatenate([jnp.concatenate(main, axis=0).T, parts[3]], axis=0)

        def keys(parts):
            return jnp.concatenate([parts[c] for c in range(3)], axis=1) + parts[3]

        self.a = queries(self.at).astype(BF16)
        self.dqb = (queries(self.dqt) * SCALE).astype(BF16)
        self.dkb = (keys(self.dk) * SCALE).astype(BF16)
        self.dvb = keys(self.dv).astype(BF16)
        w = r["wqkv_t"]
        dn = mm(self.dqb, w[0:192], NN) + mm(self.dkb, w[192:384], NN) + mm(self.dvb, w[384:576], NN)
        du = dn * r["gain"][...]
        dx = self.inv_std * (
            du
            - jnp.mean(du, axis=-1, keepdims=True)
            - self.unit * jnp.mean(du * self.unit, axis=-1, keepdims=True)
        )
        self.put(self.dy + dx)

    def steps(self):
        yield lambda: (self.front(), self.also_first())
        yield lambda: self.scores(0)
        yield lambda: (self.scores(1), self.softmax(0))
        yield lambda: (self.scores(2), self.softmax(1), self.products(0))
        yield lambda: (self.scores(3), self.softmax(2), self.products(1))
        yield lambda: (self.softmax(3), self.products(2))
        yield lambda: self.products(3)
        yield lambda: (self.back(), self.also_last())


STAGGER = 2


def run_windows(windows, gw_ref):
    plans = [list(w.steps()) for w in windows]
    for tick in range(STAGGER * (len(plans) - 1) + len(plans[0])):
        for n in reversed(range(len(plans))):
            at = tick - STAGGER * n
            if 0 <= at < len(plans[n]):
                plans[n][at]()
    normed = jnp.concatenate([w.normed for w in windows], axis=0)
    for n, name in enumerate(("dqb", "dkb", "dvb")):
        gw_ref[n] += mm(normed, jnp.concatenate([getattr(w, name) for w in windows], axis=0), TN)
    gw_ref[3] += mm(
        jnp.concatenate([w.a for w in windows], axis=0),
        jnp.concatenate([w.dyb for w in windows], axis=0),
        TN,
    )


def fetch_rows(low, high, start, stride):
    lats = [pl.ds(start + n, 24, stride=stride) for n in range(WIN_LAT)]
    return jnp.concatenate(
        [
            jnp.concatenate([low[at, :] for at in lats], axis=0),
            jnp.concatenate([high[at, :] for at in lats], axis=0)[:, :64],
        ],
        axis=1,
    )


def put_rows(low, high, start, stride, value):
    right = jnp.concatenate([value[:, 128:], jnp.zeros((W, 64), F32)], axis=1)
    for n in range(WIN_LAT):
        at = pl.ds(start + n, 24, stride=stride)
        low[at, :] = value[24 * n : 24 * n + 24, :128]
        high[at, :] = right[24 * n : 24 * n + 24]


def keep(low, high, at, rows):
    wide = rows.astype(F32)
    n = rows.shape[0]
    low[at : at + n, :] = wide[:, :128]
    high[at : at + n, :64] = wide[:, 128:]


def kept(low, high, at, n):
    return jnp.concatenate([low[at : at + n, :], high[at : at + n, :64]], axis=1).astype(BF16)


def window_of(scratch, start, stride, bias_at, refs):
    x0, x1, y0, y1, o0, o1 = scratch

    def fetch():
        return fetch_rows(x0, x1, start, stride), fetch_rows(y0, y1, start, stride)

    def put(value):
        put_rows(o0, o1, start, stride, value)

    return Window(fetch, put, bias_at, refs)


def regroup(rows, back=False):
    if back:
        order = [la * 2 + lv for lv in range(2) for la in range(6)]
    else:
        order = [lv * 6 + la for la in range(6) for lv in range(2)]
    return jnp.concatenate([rows[12 * n : 12 * n + 12] for n in order], axis=0)


def lay_bias(pair_ref, last_ref, bias_ref):
    turned = [regroup(regroup(pair_ref[h]).T) * LOG2E for h in range(HEADS)]
    flat = jnp.concatenate(
        [t[:, :128] for t in turned] + [t[:, 128:] for t in turned] + [jnp.zeros((W, 32), F32)],
        axis=1,
    )
    bias_ref[0] = flat
    key_south = lax.broadcasted_iota(jnp.int32, (W, LANES), 0) >= W // 2
    lane = lax.broadcasted_iota(jnp.int32, (W, LANES), 1)
    query_south = (lane >= 768) | (lane % 128 >= W // 2)
    apart = (key_south != query_south) & (last_ref[...] > 0)
    bias_ref[1] = jnp.where(apart, F32(-1e30), flat)


def inner_steps(xs, ys, consts, bias, dx_ref, gw_ref, gb_ref, scratch):
    def place(lv, lon):
        return 24 * (24 * (lon // 12) + 12 * lv + lon % 12)

    def take(k):
        for lv in range(2):
            for lon in range(12 * k, 12 * k + 12):
                keep(scratch[0], scratch[1], place(lv, lon), xs[lon // 6][lv, lon % 6])
                keep(scratch[2], scratch[3], place(lv, lon), ys[lon // 6][lv, lon % 6])

    def give(k):
        for lv in range(2):
            for lon in range(12 * k, 12 * k + 12):
                dx_ref[lv, lon] = kept(scratch[4], scratch[5], place(lv, lon), 24)

    take(0)
    refs = dict(zip(("gain", "wqkv", "wqkv_t", "wout_t"), consts), bias=bias, gb=gb_ref)
    windows = [
        window_of(scratch, 576 * k + 3 + 6 * a, 24, 0, refs) for k in range(2) for a in range(3)
    ]
    windows[1].also_first = lambda: take(1)
    windows[2].also_last = lambda: give(0)
    run_windows(windows, gw_ref)
    give(1)


def inner_kernel(
    x0, x1, x2, x3, y0, y1, y2, y3, gain, weight, out_weight, pair, last, dx_ref, gw_ref, gb_ref, bias_ref, wqkv, wqkv_t, wout_t, *scratch
):
    @pl.when(pl.program_id(0) == 0)
    def _():
        gw_ref[...] = jnp.zeros_like(gw_ref)
        gb_ref[...] = jnp.zeros_like(gb_ref)
        lay_bias(pair, last, bias_ref)
        part = weight[...]
        gap = jnp.zeros((D, 64), BF16)
        wqkv[...] = jnp.concatenate(
            [p for n in range(3) for p in (part[:, D * n : D * n + D], gap)], axis=1
        )
        wqkv_t[...] = part.T
        wout_t[...] = out_weight[...].T

    consts = (gain, wqkv, wqkv_t, wout_t)
    inner_steps((x0, x1, x2, x3), (y0, y1, y2, y3), consts, bias_ref, dx_ref, gw_ref, gb_ref, scratch)


def write_halves(core, give_ref, mine_ref, gw_ref, gb_ref, sum_ref):
    @pl.when(pl.program_id(0) == pl.num_programs(0) - 1)
    def _():
        whole = jnp.concatenate([gw_ref[n] for n in range(4)], axis=1)
        for t in range(6):
            sum_ref[D * t : D * t + D] = whole[:, 128 * t : 128 * t + 128]
        for t in range(7):
            sum_ref[WROWS + W * t : WROWS + W * t + W] = gb_ref[:, 128 * t : 128 * t + 128]
        sum_ref[WROWS + BROWS :] = jnp.zeros((ROWS - WROWS - BROWS, 128), F32)
        first = core[...] == 0
        upper, lower = sum_ref[: ROWS // 2], sum_ref[ROWS // 2 :]
        give_ref[...] = jnp.where(first, lower, upper).astype(BF16)
        mine_ref[...] = jnp.where(first, upper, lower)


def split(rows):
    return rows[:, :128], jnp.concatenate(
        [rows[:, 128:], jnp.zeros((rows.shape[0], 64), F32)], axis=1
    )


def joined(low, high, at):
    return jnp.concatenate([low[at, :], high[at, :][:, :64]], axis=1)


def dense(left, right):
    half = left.shape[0] // 2
    return jnp.concatenate(
        [left, jnp.concatenate([right[:half], right[half:]], axis=1)], axis=0
    ).astype(BF16)


def undense(packed):
    wide = packed.astype(F32)
    rows = 2 * packed.shape[0] // 3
    tail = wide[rows:]
    high = jnp.concatenate([tail[:, :64], tail[:, 64:]], axis=0)
    return wide[:rows], jnp.concatenate([high, jnp.zeros((rows, 64), F32)], axis=1)


def dense_corner(rows):
    right = jnp.concatenate([rows[:18, 128:], rows[18:, 128:]], axis=1)
    return jnp.concatenate([rows[:, :128], right, jnp.zeros((2, 128), F32)], axis=0).astype(BF16)


def undense_corner(packed):
    wide = packed.astype(F32)
    high = jnp.concatenate([wide[36:54, :64], wide[36:54, 64:]], axis=0)
    return wide[:36], jnp.concatenate([high, jnp.zeros((36, 64), F32)], axis=1)


def pack_kernel(x, y, e_ref, s_ref, c_ref, low, high):
    pad = jnp.zeros((2, D), F32)
    for n, own in enumerate((x, y)):
        corners = []
        for lv in range(2):
            base = 288 * (2 * n + lv)
            east = jnp.concatenate([own[lv, lon].astype(F32) for lon in range(6)], axis=0)
            e_ref[n, lv] = dense(east[:, :128], east[:, 128:])
            for lon in range(36):
                rows = own[lv, lon].astype(F32)[:8]
                at = slice(base + 8 * lon, base + 8 * lon + 8)
                low[at, :] = rows[:, :128]
                high[at, :64] = rows[:, 128:]
            parts = []
            for t in range(3):
                parts += [joined(low, high, pl.ds(base + 48 + t, 30, stride=8)), pad]
                corners.append(joined(low, high, pl.ds(base + t, 6, stride=8)))
            rows = jnp.concatenate(parts, axis=0)
            s_ref[n, lv] = dense(rows[:, :128], rows[:, 128:])
        c_ref[n, 0] = dense_corner(jnp.concatenate(corners, axis=0))


def south_kernel(
    x, y, e, s, c, gain, wqkv, wqkv_t, wout_t, bias, gw_in, gb_in, os_ref, tail_ref, bs_ref, bc_ref, gw_ref, gb_ref, *scratch
):
    @pl.when(pl.program_id(0) == 0)
    def _():
        gw_ref[...] = gw_in[...]
        gb_ref[...] = gb_in[...]

    def place(lv, lon):
        return 1152 * (lv // 2) + 16 * (24 * (lon // 12) + 12 * (lv % 2) + lon % 12)

    def south(lv, t):
        return [
            pl.ds(place(lv, 12 * m) + 8 + t, 12 if m < 2 else 6, stride=16) for m in range(3)
        ]

    def corner(lv, t):
        return pl.ds(place(lv, 30) + 8 + t, 6, stride=16)

    for n, own in enumerate((x, y)):
        low, high = scratch[2 * n], scratch[2 * n + 1]
        for lv in range(4):
            if lv % 2 == 0:
                cleft, cright = undense_corner(c[n, lv // 2])
            for lon in range(30):
                keep(low, high, place(lv, lon), own[lv, 6 + lon].astype(F32)[16:])
            left, right = undense(e[n, lv])
            for lon in range(6):
                at = place(lv, 30 + lon)
                low[at : at + 8, :] = left[24 * lon + 16 : 24 * lon + 24]
                high[at : at + 8, :] = right[24 * lon + 16 : 24 * lon + 24]
            left, right = undense(s[n, lv])
            for t in range(3):
                for m, at in enumerate(south(lv, t)):
                    rows = slice(32 * t + 12 * m, 32 * t + min(12 * m + 12, 30))
                    low[at, :] = left[rows]
                    high[at, :] = right[rows]
                rows = slice(18 * (lv % 2) + 6 * t, 18 * (lv % 2) + 6 * t + 6)
                low[corner(lv, t), :] = cleft[rows]
                high[corner(lv, t), :] = cright[rows]
    refs = dict(gain=gain, wqkv=wqkv, wqkv_t=wqkv_t, wout_t=wout_t, bias=bias, gb=gb_ref)
    run_windows(
        [
            window_of(scratch, 1152 * p + 384 * k + 5, 16, 1, refs)
            for p in range(2)
            for k in range(3)
        ],
        gw_ref,
    )
    low, high = scratch[4], scratch[5]
    pad = jnp.zeros((2, D), F32)
    corners = []
    for lv in range(4):
        for lon in range(30):
            os_ref[lv, lon] = kept(low, high, place(lv, lon), 8)
        for lon in range(6):
            tail_ref[lv, lon] = kept(low, high, place(lv, 30 + lon), 8)
        parts = []
        for t in range(3):
            parts += [joined(low, high, at) for at in south(lv, t)] + [pad]
            corners.append(joined(low, high, corner(lv, t)))
        rows = jnp.concatenate(parts, axis=0)
        bs_ref[lv] = dense(rows[:, :128], rows[:, 128:])
    for p in range(2):
        bc_ref[p] = dense_corner(jnp.concatenate(corners[6 * p : 6 * p + 6], axis=0))


def east_kernel(
    x, y, e, tail, gain, wqkv, wqkv_t, wout_t, bias, gw_in, gb_in, core, oe_ref, be_ref, give_ref, mine_ref, gw_ref, gb_ref, sum_ref, *scratch
):
    @pl.when(pl.program_id(0) == 0)
    def _():
        gw_ref[...] = gw_in[...]
        gb_ref[...] = gb_in[...]

    def place(lv, lon):
        return 576 * (lv // 2) + 24 * (12 * (lv % 2) + lon)

    for n, own in enumerate((x, y)):
        low, high = scratch[2 * n], scratch[2 * n + 1]
        for lv in range(4):
            left, right = undense(e[n, lv])
            for lon in range(6):
                keep(low, high, place(lv, lon), own[lv, lon])
                at = place(lv, 6 + lon)
                low[at : at + 24, :] = left[24 * lon : 24 * lon + 24]
                high[at : at + 24, :] = right[24 * lon : 24 * lon + 24]
    refs = dict(gain=gain, wqkv=wqkv, wqkv_t=wqkv_t, wout_t=wout_t, bias=bias, gb=gb_ref)
    run_windows(
        [
            window_of(scratch, 576 * p + 3 + 6 * a, 24, 0, refs)
            for p in range(2)
            for a in range(3)
        ],
        gw_ref,
    )
    low, high = scratch[4], scratch[5]
    row = lax.broadcasted_iota(jnp.int32, (8, D), 0)
    for lv in range(4):
        east = []
        for lon in range(6):
            oe_ref[lv, lon] = kept(low, high, place(lv, lon), 24)
            at = place(lv, 6 + lon)
            last = joined(low, high, pl.ds(at + 16, 8))
            east += [
                joined(low, high, pl.ds(at, 16)),
                jnp.where(row >= 5, tail[lv, lon].astype(F32), last),
            ]
        east = jnp.concatenate(east, axis=0)
        be_ref[lv] = dense(east[:, :128], east[:, 128:])
    write_halves(core, give_ref, mine_ref, gw_ref, gb_ref, sum_ref)


def whole(shape):
    return pl.BlockSpec(shape, lambda *_: (0,) * len(shape))


PARAMS = pltpu.CompilerParams(vmem_limit_bytes=60 * 1024 * 1024)
GW = (4, D, D)
GB = (W, LANES)
BIAS = (2, W, LANES)


def cost(count):
    return pl.CostEstimate(
        flops=count * 144 * 192 * 192 * 40, bytes_accessed=count * 144 * 192 * 6, transcendentals=0
    )


def const_specs():
    return [whole((1, D)), whole((D, 768)), whole((3 * D, D)), whole((D, D))]


def halves(rows):
    return [pltpu.VMEM((rows, 128), F32) for _ in range(6)]


def inner_specs():
    def cols(n):
        return pl.BlockSpec((2, 6, 24, D), lambda i: (i, n, 0, 0))

    four = [cols(n) for n in range(1, 5)]
    return four + four, pl.BlockSpec((2, 24, 24, D), lambda i: (i, 0, 0, 0))


def inner_windows(x, y, weights, pair_bias, last):
    steps = x.shape[0] // 2
    ins, out = inner_specs()
    return pl.pallas_call(
        inner_kernel,
        grid=(steps,),
        in_specs=ins
        + [whole((1, D)), whole((D, 3 * D)), whole((D, D)), whole((HEADS, W, W)), whole((1, 1))],
        out_specs=[out, whole(GW), whole(GB), whole(BIAS)] + const_specs()[1:],
        out_shape=[
            jax.ShapeDtypeStruct((x.shape[0], 24, 24, D), BF16),
            jax.ShapeDtypeStruct(GW, F32),
            jax.ShapeDtypeStruct(GB, F32),
            jax.ShapeDtypeStruct(BIAS, F32),
            jax.ShapeDtypeStruct((D, 768), BF16),
            jax.ShapeDtypeStruct((3 * D, D), BF16),
            jax.ShapeDtypeStruct((D, D), BF16),
        ],
        scratch_shapes=halves(1152),
        compiler_params=PARAMS,
        cost_estimate=cost(6 * steps),
        name="inner_windows",
    )(x, x, x, x, y, y, y, y, *weights, pair_bias, last)


def both(*rest):
    zeros = (0,) * len(rest)
    return pl.BlockSpec((2, 2) + rest, lambda i: (0, i) + zeros)


def one(*rest):
    zeros = (0,) * len(rest)
    return pl.BlockSpec((2,) + rest, lambda i: (i,) + zeros)


def both_corner():
    return pl.BlockSpec((2, 1, 56, 128), lambda i: (0, i, 0, 0))


def one_corner():
    return pl.BlockSpec((1, 56, 128), lambda i: (i, 0, 0))


def pack_halo(x, y):
    levels = x.shape[0]
    return pl.pallas_call(
        pack_kernel,
        grid=(levels // 2,),
        in_specs=[one(36, 24, D), one(36, 24, D)],
        out_specs=[both(216, 128), both(144, 128), both_corner()],
        out_shape=[
            jax.ShapeDtypeStruct((2, levels, 216, 128), BF16),
            jax.ShapeDtypeStruct((2, levels, 144, 128), BF16),
            jax.ShapeDtypeStruct((2, levels // 2, 56, 128), BF16),
        ],
        scratch_shapes=[pltpu.VMEM((1152, 128), F32), pltpu.VMEM((1152, 128), F32)],
        compiler_params=PARAMS,
        name="pack_halo",
    )(x, y)


def four(*rest, at=0):
    zeros = (0,) * (len(rest) - 1)
    return pl.BlockSpec((4,) + rest, lambda i: (i, at) + zeros)


def both_four(count, *rest):
    return pl.BlockSpec((2, count) + rest, lambda i: (0, i, 0, 0))


def south_windows(x, y, e, s, c, consts, bias, sums):
    levels = x.shape[0]
    return pl.pallas_call(
        south_kernel,
        grid=(levels // 4,),
        in_specs=[
            four(36, 24, D),
            four(36, 24, D),
            both_four(4, 216, 128),
            both_four(4, 144, 128),
            both_four(2, 56, 128),
        ]
        + const_specs()
        + [whole(BIAS), whole(GW), whole(GB)],
        out_specs=[
            four(30, 8, D),
            four(6, 8, D),
            four(144, 128),
            pl.BlockSpec((2, 56, 128), lambda i: (i, 0, 0)),
            whole(GW),
            whole(GB),
        ],
        out_shape=[
            jax.ShapeDtypeStruct((levels, 30, 8, D), BF16),
            jax.ShapeDtypeStruct((levels, 6, 8, D), BF16),
            jax.ShapeDtypeStruct((levels, 144, 128), BF16),
            jax.ShapeDtypeStruct((levels // 2, 56, 128), BF16),
            jax.ShapeDtypeStruct(GW, F32),
            jax.ShapeDtypeStruct(GB, F32),
        ],
        scratch_shapes=halves(2304),
        compiler_params=PARAMS,
        cost_estimate=cost(12),
        name="south_windows",
    )(x, y, e, s, c, *consts, bias, *sums)


def east_windows(x, y, e, tail, consts, bias, sums, core):
    levels = x.shape[0]
    return pl.pallas_call(
        east_kernel,
        grid=(levels // 4,),
        in_specs=[
            four(6, 24, D, at=5),
            four(6, 24, D, at=5),
            both_four(4, 216, 128),
            four(6, 8, D),
        ]
        + const_specs()
        + [whole(BIAS), whole(GW), whole(GB), whole((1, 1))],
        out_specs=[
            four(6, 24, D),
            four(216, 128),
            whole((ROWS // 2, 128)),
            whole((ROWS // 2, 128)),
        ],
        out_shape=[
            jax.ShapeDtypeStruct((levels, 6, 24, D), BF16),
            jax.ShapeDtypeStruct((levels, 216, 128), BF16),
            jax.ShapeDtypeStruct((ROWS // 2, 128), BF16),
            jax.ShapeDtypeStruct((ROWS // 2, 128), F32),
        ],
        scratch_shapes=[pltpu.VMEM(GW, F32), pltpu.VMEM(GB, F32), pltpu.VMEM((ROWS, 128), F32)]
        + halves(1152),
        compiler_params=PARAMS,
        cost_estimate=cost(12),
        name="east_windows",
    )(x, y, e, tail, *consts, bias, *sums, core)


def assemble_kernel(inner, oe, os_, gl, gs, gc, *rest):
    out_ref, low, high = rest[-3:]
    row = lax.broadcasted_iota(jnp.int32, (8, D), 0)
    cleft, cright = undense_corner(gc[0])
    for lv in range(2):
        base = 288 * lv
        left, right = undense(gs[lv])
        for t in range(3):
            at = pl.ds(base + 48 + t, 30, stride=8)
            low[at, :] = left[32 * t : 32 * t + 30]
            high[at, :] = right[32 * t : 32 * t + 30]
            at = pl.ds(base + t, 6, stride=8)
            rows = slice(18 * lv + 6 * t, 18 * lv + 6 * t + 6)
            low[at, :] = cleft[rows]
            high[at, :] = cright[rows]
        left, right = undense(gl[lv])
        for lon in range(36):
            if lon < 6:
                at = slice(24 * lon, 24 * lon + 24)
                rows = jnp.concatenate([left[at], right[at, :64]], axis=1)
            else:
                rows = (inner[lv, lon - 6] if lon < 30 else oe[lv, lon - 30]).astype(F32)
                tail = os_[lv, lon - 6].astype(F32)
                rows = jnp.concatenate([rows[:16], jnp.where(row >= 5, tail, rows[16:])], axis=0)
            head = jnp.where(row < 3, joined(low, high, pl.ds(base + 8 * lon, 8)), rows[:8])
            out_ref[lv, lon] = jnp.concatenate([head, rows[8:]], axis=0).astype(BF16)


def assemble(first, steps, grad_x, inner, oe, os_, got_lon, got_lat, got_both):
    def at(count, *rest):
        zeros = (0,) * len(rest)
        return pl.BlockSpec((count,) + rest, lambda i: (i + first,) + zeros)

    ins = [inner, oe, os_, got_lon, got_lat, got_both]
    specs = [
        at(2, 24, 24, D),
        at(2, 6, 24, D),
        at(2, 30, 8, D),
        at(2, 216, 128),
        at(2, 144, 128),
        at(1, 56, 128),
    ]
    aliases = {}
    if grad_x is not None:
        ins.append(grad_x)
        specs.append(pl.BlockSpec(memory_space=pl.ANY))
        aliases = {6: 0}
    return pl.pallas_call(
        assemble_kernel,
        grid=(steps,),
        in_specs=specs,
        out_specs=at(2, 36, 24, D),
        out_shape=jax.ShapeDtypeStruct((inner.shape[0], 36, 24, D), BF16),
        scratch_shapes=[pltpu.VMEM((576, 128), F32), pltpu.VMEM((576, 128), F32)],
        input_output_aliases=aliases,
        compiler_params=PARAMS,
        cost_estimate=pl.CostEstimate(
            flops=0, bytes_accessed=1_500_000 * steps, transcendentals=0
        ),
        name="assemble",
    )(*ins)


def finish_kernel(
    factor, line_ref, other_ref, core, gain_ref, w_ref, gq_ref, go_ref, gb_ref, gg_ref, sum_ref
):
    line, other = line_ref[...].astype(F32), other_ref[...].astype(F32)
    first = core[...] == 0
    sum_ref[: ROWS // 2] = jnp.where(first, line, other)
    sum_ref[ROWS // 2 :] = jnp.where(first, other, line)
    both = jnp.concatenate(
        [sum_ref[D * t : D * t + D] for t in range(6)], axis=1
    )
    gq = both[:, : 3 * D] * factor
    gq_ref[...] = gq
    go_ref[...] = both[:, 3 * D :] * factor
    products = (gq * w_ref[...].astype(F32)).T
    gg_ref[...] = jnp.sum(products, axis=0, keepdims=True) / gain_ref[...]
    base = WROWS + 6 * W
    rest = sum_ref[base : base + W]
    for h in range(HEADS):
        main = sum_ref[WROWS + W * h : WROWS + W * h + W]
        turned = jnp.concatenate([main, rest[:, 16 * h : 16 * h + 16]], axis=1)
        gb_ref[h] = regroup(regroup(turned, True).T, True)


def finish(line, other, core, gain_row, qkv_weight, factor):
    return pl.pallas_call(
        lambda *refs: finish_kernel(factor, *refs),
        out_shape=[
            jax.ShapeDtypeStruct((D, 3 * D), F32),
            jax.ShapeDtypeStruct((D, D), F32),
            jax.ShapeDtypeStruct((HEADS, W, W), F32),
            jax.ShapeDtypeStruct((1, D), F32),
        ],
        scratch_shapes=[pltpu.VMEM((ROWS, 128), F32)],
        compiler_params=PARAMS,
        name="finish_sums",
    )(line, other, core, gain_row, qkv_weight)


def shift(value, axes, steps):
    sizes = [lax.axis_size(a) for a in axes]
    total = 1
    for s in sizes:
        total *= s
    pairs = []
    for source in range(total):
        rest, place = source, []
        for s in reversed(sizes):
            place.append(rest % s)
            rest //= s
        place.reverse()
        target = 0
        for p, s, d in zip(place, sizes, steps):
            target = target * s + (p + d) % s
        pairs.append((source, target))
    return lax.ppermute(value, axes if len(axes) > 1 else axes[0], pairs)


def moved(value, axis, to_of):
    count = lax.axis_size(axis)
    return lax.ppermute(value, axis, [(n, to_of(n)) for n in range(count)])


def flip(value, axis, bits):
    return moved(value, axis, lambda n: n ^ bits)


def lon_core(n):
    return n % 2


def sum_over_devices(give, mine, back, beside):
    y = (lax.axis_index("lon") // 2) % 4
    mine = mine + flip(give, "lon", 1).astype(F32)
    quarters = mine.reshape(4, ROWS // 8, 128)
    qlow = quarters.astype(BF16)
    total = lax.dynamic_index_in_dim(quarters, y, 0, keepdims=False)
    for step in range(1, 4):
        piece = lax.dynamic_index_in_dim(qlow, y ^ step, 0, keepdims=False)
        total = total + flip(piece, "lon", 2 * step).astype(F32)
    low = total.astype(BF16)
    for step in range(1, 4):
        total = total + flip(low, "lat", 2 * step).astype(F32)
    total, got_lon = lax.optimization_barrier((total, back[0]))
    back = (got_lon, *back[1:])
    low = total.astype(BF16)
    total = (
        total
        + flip(low, "lat", 1).astype(F32)
        + flip(low, "lon", 8).astype(F32)
        + shift_x(low).astype(F32)
    )
    total, grad_x = lax.optimization_barrier((total, beside(0, None, back)))
    low = total.astype(BF16)
    others = [low] + [flip(low, "lon", 2 * step) for step in range(1, 4)]
    stacked = jnp.stack(others)
    line = jnp.concatenate(
        [lax.dynamic_index_in_dim(stacked, y ^ n, 0, keepdims=True) for n in range(4)], axis=0
    )
    line, grad_x = lax.optimization_barrier((line, beside(1, grad_x, back)))
    other = flip(line, "lon", 1)
    return line.reshape(ROWS // 2, 128), other.reshape(ROWS // 2, 128), grad_x


def shift_x(value):
    lat = lax.axis_size("lat")
    total = lax.axis_size("lon") * lat
    pairs = []
    for source in range(total):
        lon_at, lat_at = source // lat, source % lat
        pairs.append((source, (lon_at ^ 8) * lat + (lat_at ^ 1)))
    return lax.ppermute(value, ("lon", "lat"), pairs)


def local(tokens, cotangent, ln_gain, qkv_weight, out_weight, pair_bias):
    levels, lat_count, lon_count, _ = tokens.shape
    x = jnp.transpose(tokens, (0, 2, 1, 3))
    y = jnp.transpose(cotangent, (0, 2, 1, 3))
    e, s, c = pack_halo(x, y)
    s = shift(s, ("lat",), (-1,))
    e = shift(e, ("lon",), (-1,))
    c = shift(c, ("lon", "lat"), (-1, -1))
    gain = ln_gain.reshape(1, D)
    core = (lax.axis_index("lon") % 2).astype(jnp.int32).reshape(1, 1)
    last = (lax.axis_index("lat") == lax.axis_size("lat") - 1).astype(jnp.int32).reshape(1, 1)
    inner, gw, gb, bias, *laid = inner_windows(
        x, y, (gain, qkv_weight, out_weight), pair_bias, last
    )
    consts = [gain] + laid
    os_, tail, bs, bc, gw, gb = south_windows(x, y, e, s, c, consts, bias, (gw, gb))
    got_lat = shift(bs, ("lat",), (1,))
    got_both = shift(bc, ("lon", "lat"), (1, 1))
    oe, be, give, mine = east_windows(x, y, e, tail, consts, bias, (gw, gb), core)
    got_lon = shift(be, ("lon",), (1,))
    give, got_lat, got_both = lax.optimization_barrier((give, got_lat, got_both))
    back = (got_lon, got_lat, got_both)
    half = levels // 4

    def beside(part, grad_x, got):
        return assemble(half * part, half, grad_x, inner, oe, os_, *got)

    *sums, grad_x = sum_over_devices(give, mine, back, beside)
    factor = float(
        levels * lat_count * lax.axis_size("lat") * lon_count * lax.axis_size("lon")
    ) ** (-0.5)
    gq, go, gbias, gg = finish(*sums, core, gain, qkv_weight, factor)
    return (jnp.transpose(grad_x, (0, 2, 1, 3)), gq, go, gbias, gg.reshape(D))


def solution(mesh):
    placed = (P(None, "lat", "lon", None), P(None, "lat", "lon", None), P(), P(), P(), P())
    return jax.shard_map(
        local,
        mesh=mesh,
        in_specs=placed,
        out_specs=(P(None, "lat", "lon", None), P(), P(), P(), P()),
        check_vma=False,
    )
```

```python
import jax
import jax.numpy as jnp
from jax import lax
from jax.experimental import pallas as pl
from jax.experimental.pallas import tpu as pltpu
from jax.sharding import PartitionSpec as P

WIN_LEV = 2
WIN_LAT = 6
WIN_LON = 12
W = 144
HEADS = 6
HEAD = 32
D = 192
HALF_LAT = 3
HALF_LON = 6
LANES = 896
LOG2E = 1.4426950408889634
SCALE = HEAD**-0.5
F32 = jnp.float32
BF16 = jnp.bfloat16
WROWS = 6 * D
BROWS = 7 * W
ROWS = 2176

NN = (((1,), (0,)), ((), ()))
NT = (((1,), (1,)), ((), ()))
TN = (((0,), (0,)), ((), ()))


def mm(a, b, dims):
    return lax.dot_general(a, b, dims, preferred_element_type=F32)


def pair_rows(rows, c):
    part = rows[:128, 64 * c : 64 * c + 64]
    first = lax.broadcasted_iota(jnp.int32, (1, 64), 1) < HEAD
    zero = jnp.zeros_like(part)
    return jnp.concatenate([jnp.where(first, part, zero), jnp.where(first, zero, part)], axis=0)


def rest_rows(rows):
    head_of = lax.broadcasted_iota(jnp.int32, (1, D), 1) // HEAD
    rest = rows[128:]
    zero = jnp.zeros_like(rest)
    return jnp.concatenate(
        [jnp.where(head_of == h, rest, zero) for h in range(HEADS)] + [zero, zero], axis=0
    )


def fold_rest(rest):
    head_of = lax.broadcasted_iota(jnp.int32, (1, D), 1) // HEAD
    total = rest[:16]
    for h in range(1, HEADS):
        total = jnp.where(head_of == h, rest[16 * h : 16 * h + 16], total)
    return total


class Window:
    def __init__(self, fetch, put, bias_at, refs):
        self.fetch, self.put, self.bias_at, self.refs = fetch, put, bias_at, refs
        self.also_first = self.also_last = lambda: None

    def front(self):
        r = self.refs
        x, dy = self.fetch()
        mean = jnp.mean(x, axis=-1, keepdims=True)
        centred = x - mean
        self.inv_std = lax.rsqrt(jnp.mean(centred * centred, axis=-1, keepdims=True) + 1e-05)
        self.unit = centred * self.inv_std
        self.normed = (self.unit * r["gain"][...]).astype(BF16)
        self.dy = dy
        self.dyb = dy.astype(BF16)
        packed = mm(self.normed, r["wqkv"][...], NN).astype(BF16)
        self.q = packed[:, 0:192]
        self.k = packed[:, 256:448]
        self.v = packed[:, 512:704]
        self.da = mm(self.dyb, r["wout_t"][...], NN).astype(BF16)
        self.kt = self.k.T
        self.vt = self.v.T
        self.raw, self.low, self.dv, self.dk, self.at, self.dqt = {}, {}, {}, {}, {}, {}
        self.qm, self.dam = {}, {}

    def scores(self, c):
        if c < 3:
            cols = slice(64 * c, 64 * c + 64)
            self.qm[c] = pair_rows(self.q, c)
            self.dam[c] = pair_rows(self.da, c)
            k, v = self.k[:, cols], self.v[:, cols]
        else:
            self.qm[c] = rest_rows(self.q)
            self.dam[c] = rest_rows(self.da)
            k, v = self.k, self.v
        self.raw[c] = (mm(k, self.qm[c], NT), mm(v, self.dam[c], NT))

    def softmax(self, c):
        lanes = slice(256 * c, 256 * c + 256) if c < 3 else slice(768, 896)
        raw, dp = self.raw.pop(c)
        s = raw * (SCALE * LOG2E) + self.refs["bias"][self.bias_at, :, lanes]
        e = jnp.exp2(s - jnp.max(s, axis=0, keepdims=True))
        p = e * (1.0 / jnp.sum(e, axis=0, keepdims=True))
        ds = p * (dp - jnp.sum(p * dp, axis=0, keepdims=True))
        self.refs["gb"][:, lanes] += ds
        self.low[c] = (p.astype(BF16), ds.astype(BF16))

    def products(self, c):
        pb, dsb = self.low.pop(c)
        self.dv[c] = mm(pb, self.dam.pop(c), NN)
        self.dk[c] = mm(dsb, self.qm.pop(c), NN)
        if c < 3:
            self.at[c] = mm(self.vt[64 * c : 64 * c + 64], pb, NN)
            self.dqt[c] = mm(self.kt[64 * c : 64 * c + 64], dsb, NN)
        else:
            self.at[c] = fold_rest(mm(pb, self.v, TN))
            self.dqt[c] = fold_rest(mm(dsb, self.k, TN))

    def back(self):
        r = self.refs

        def queries(parts):
            main = [p for c in range(3) for p in (parts[c][:32, :128], parts[c][32:, 128:])]
            return jnp.concatenate([jnp.concatenate(main, axis=0).T, parts[3]], axis=0)

        def keys(parts):
            return jnp.concatenate([parts[c] for c in range(3)], axis=1) + parts[3]

        self.a = queries(self.at).astype(BF16)
        self.dqb = (queries(self.dqt) * SCALE).astype(BF16)
        self.dkb = (keys(self.dk) * SCALE).astype(BF16)
        self.dvb = keys(self.dv).astype(BF16)
        w = r["wqkv_t"]
        dn = mm(self.dqb, w[0:192], NN) + mm(self.dkb, w[192:384], NN) + mm(self.dvb, w[384:576], NN)
        du = dn * r["gain"][...]
        dx = self.inv_std * (
            du
            - jnp.mean(du, axis=-1, keepdims=True)
            - self.unit * jnp.mean(du * self.unit, axis=-1, keepdims=True)
        )
        self.put(self.dy + dx)

    def steps(self):
        yield lambda: (self.front(), self.also_first())
        yield lambda: self.scores(0)
        yield lambda: (self.scores(1), self.softmax(0))
        yield lambda: (self.scores(2), self.softmax(1), self.products(0))
        yield lambda: (self.scores(3), self.softmax(2), self.products(1))
        yield lambda: (self.softmax(3), self.products(2))
        yield lambda: self.products(3)
        yield lambda: (self.back(), self.also_last())


STAGGER = 2


def run_windows(windows, gw_ref):
    plans = [list(w.steps()) for w in windows]
    for tick in range(STAGGER * (len(plans) - 1) + len(plans[0])):
        for n in reversed(range(len(plans))):
            at = tick - STAGGER * n
            if 0 <= at < len(plans[n]):
                plans[n][at]()
    normed = jnp.concatenate([w.normed for w in windows], axis=0)
    for n, name in enumerate(("dqb", "dkb", "dvb")):
        gw_ref[n] += mm(normed, jnp.concatenate([getattr(w, name) for w in windows], axis=0), TN)
    gw_ref[3] += mm(
        jnp.concatenate([w.a for w in windows], axis=0),
        jnp.concatenate([w.dyb for w in windows], axis=0),
        TN,
    )


def fetch_rows(low, high, start, stride):
    lats = [pl.ds(start + n, 24, stride=stride) for n in range(WIN_LAT)]
    return jnp.concatenate(
        [
            jnp.concatenate([low[at, :] for at in lats], axis=0),
            jnp.concatenate([high[at, :] for at in lats], axis=0)[:, :64],
        ],
        axis=1,
    )


def put_rows(low, high, start, stride, value):
    right = jnp.concatenate([value[:, 128:], jnp.zeros((W, 64), F32)], axis=1)
    for n in range(WIN_LAT):
        at = pl.ds(start + n, 24, stride=stride)
        low[at, :] = value[24 * n : 24 * n + 24, :128]
        high[at, :] = right[24 * n : 24 * n + 24]


def keep(low, high, at, rows):
    wide = rows.astype(F32)
    n = rows.shape[0]
    low[at : at + n, :] = wide[:, :128]
    high[at : at + n, :64] = wide[:, 128:]


def kept(low, high, at, n):
    return jnp.concatenate([low[at : at + n, :], high[at : at + n, :64]], axis=1).astype(BF16)


def window_of(scratch, start, stride, bias_at, refs):
    x0, x1, y0, y1, o0, o1 = scratch

    def fetch():
        return fetch_rows(x0, x1, start, stride), fetch_rows(y0, y1, start, stride)

    def put(value):
        put_rows(o0, o1, start, stride, value)

    return Window(fetch, put, bias_at, refs)


def regroup(rows, back=False):
    if back:
        order = [la * 2 + lv for lv in range(2) for la in range(6)]
    else:
        order = [lv * 6 + la for la in range(6) for lv in range(2)]
    return jnp.concatenate([rows[12 * n : 12 * n + 12] for n in order], axis=0)


def lay_bias(pair_ref, last_ref, bias_ref):
    turned = [regroup(regroup(pair_ref[h]).T) * LOG2E for h in range(HEADS)]
    flat = jnp.concatenate(
        [t[:, :128] for t in turned] + [t[:, 128:] for t in turned] + [jnp.zeros((W, 32), F32)],
        axis=1,
    )
    bias_ref[0] = flat
    key_south = lax.broadcasted_iota(jnp.int32, (W, LANES), 0) >= W // 2
    lane = lax.broadcasted_iota(jnp.int32, (W, LANES), 1)
    query_south = (lane >= 768) | (lane % 128 >= W // 2)
    apart = (key_south != query_south) & (last_ref[...] > 0)
    bias_ref[1] = jnp.where(apart, F32(-1e30), flat)


def inner_steps(xs, ys, consts, bias, dx_ref, gw_ref, gb_ref, scratch):
    def place(lv, lon):
        return 1152 * (lv // 2) + 24 * (24 * (lon // 12) + 12 * (lv % 2) + lon % 12)

    def columns(group):
        p, k = group // 2, group % 2
        return [(2 * p + lv, 12 * k + lon) for lv in range(2) for lon in range(12)]

    def take(group):
        for lv, lon in columns(group):
            keep(scratch[0], scratch[1], place(lv, lon), xs[lon // 6][lv, lon % 6])
            keep(scratch[2], scratch[3], place(lv, lon), ys[lon // 6][lv, lon % 6])

    def give(group):
        for lv, lon in columns(group):
            dx_ref[lv, lon] = kept(scratch[4], scratch[5], place(lv, lon), 24)

    refs = dict(zip(("gain", "wqkv", "wqkv_t", "wout_t"), consts), bias=bias, gb=gb_ref)
    windows = [
        window_of(scratch, 576 * group + 3 + 6 * a, 24, 0, refs)
        for group in range(4)
        for a in range(3)
    ]
    take(0)
    for group in range(3):
        windows[3 * group + 1].also_first = lambda g=group + 1: take(g)
        windows[3 * group + 2].also_last = lambda g=group: give(g)
    run_windows(windows, gw_ref)
    give(3)


def inner_kernel(
    x0, x1, x2, x3, y0, y1, y2, y3, gain, weight, out_weight, pair, last, dx_ref, gw_ref, gb_ref, bias_ref, wqkv, wqkv_t, wout_t, *scratch
):
    @pl.when(pl.program_id(0) == 0)
    def _():
        gw_ref[...] = jnp.zeros_like(gw_ref)
        gb_ref[...] = jnp.zeros_like(gb_ref)
        lay_bias(pair, last, bias_ref)
        part = weight[...]
        gap = jnp.zeros((D, 64), BF16)
        wqkv[...] = jnp.concatenate(
            [p for n in range(3) for p in (part[:, D * n : D * n + D], gap)], axis=1
        )
        wqkv_t[...] = part.T
        wout_t[...] = out_weight[...].T

    consts = (gain, wqkv, wqkv_t, wout_t)
    inner_steps((x0, x1, x2, x3), (y0, y1, y2, y3), consts, bias_ref, dx_ref, gw_ref, gb_ref, scratch)


def write_halves(core, give_ref, mine_ref, gw_ref, gb_ref, sum_ref):
    @pl.when(pl.program_id(0) == pl.num_programs(0) - 1)
    def _():
        whole = jnp.concatenate([gw_ref[n] for n in range(4)], axis=1)
        for t in range(6):
            sum_ref[D * t : D * t + D] = whole[:, 128 * t : 128 * t + 128]
        for t in range(7):
            sum_ref[WROWS + W * t : WROWS + W * t + W] = gb_ref[:, 128 * t : 128 * t + 128]
        sum_ref[WROWS + BROWS :] = jnp.zeros((ROWS - WROWS - BROWS, 128), F32)
        first = core[...] == 0
        upper, lower = sum_ref[: ROWS // 2], sum_ref[ROWS // 2 :]
        give_ref[...] = jnp.where(first, lower, upper).astype(BF16)
        mine_ref[...] = jnp.where(first, upper, lower)


def split(rows):
    return rows[:, :128], jnp.concatenate(
        [rows[:, 128:], jnp.zeros((rows.shape[0], 64), F32)], axis=1
    )


def joined(low, high, at):
    return jnp.concatenate([low[at, :], high[at, :][:, :64]], axis=1)


def dense(left, right):
    half = left.shape[0] // 2
    return jnp.concatenate(
        [left, jnp.concatenate([right[:half], right[half:]], axis=1)], axis=0
    ).astype(BF16)


def undense(packed):
    wide = packed.astype(F32)
    rows = 2 * packed.shape[0] // 3
    tail = wide[rows:]
    high = jnp.concatenate([tail[:, :64], tail[:, 64:]], axis=0)
    return wide[:rows], jnp.concatenate([high, jnp.zeros((rows, 64), F32)], axis=1)


def dense_corner(rows):
    right = jnp.concatenate([rows[:18, 128:], rows[18:, 128:]], axis=1)
    return jnp.concatenate([rows[:, :128], right, jnp.zeros((2, 128), F32)], axis=0).astype(BF16)


def undense_corner(packed):
    wide = packed.astype(F32)
    high = jnp.concatenate([wide[36:54, :64], wide[36:54, 64:]], axis=0)
    return wide[:36], jnp.concatenate([high, jnp.zeros((36, 64), F32)], axis=1)


def pack_kernel(x, y, xe, ye, e_ref, s_ref, c_ref, low, high):
    pad = jnp.zeros((2, D), F32)
    for n, (own, edge) in enumerate(((x, xe), (y, ye))):
        corners = []
        for lv in range(2):
            base = 288 * (2 * n + lv)
            east = jnp.concatenate([edge[lv, lon].astype(F32) for lon in range(6)], axis=0)
            e_ref[n, lv] = dense(east[:, :128], east[:, 128:])
            for lon in range(36):
                rows = own[lv, lon].astype(F32)[:8]
                at = slice(base + 8 * lon, base + 8 * lon + 8)
                low[at, :] = rows[:, :128]
                high[at, :64] = rows[:, 128:]
            parts = []
            for t in range(3):
                parts += [joined(low, high, pl.ds(base + 48 + t, 30, stride=8)), pad]
                corners.append(joined(low, high, pl.ds(base + t, 6, stride=8)))
            rows = jnp.concatenate(parts, axis=0)
            s_ref[n, lv] = dense(rows[:, :128], rows[:, 128:])
        c_ref[n, 0] = dense_corner(jnp.concatenate(corners, axis=0))


def south_kernel(
    x, y, e, s, c, gain, wqkv, wqkv_t, wout_t, bias, gw_in, gb_in, os_ref, tail_ref, bs_ref, bc_ref, gw_ref, gb_ref, *scratch
):
    @pl.when(pl.program_id(0) == 0)
    def _():
        gw_ref[...] = gw_in[...]
        gb_ref[...] = gb_in[...]

    def place(lv, lon):
        return 1152 * (lv // 2) + 16 * (24 * (lon // 12) + 12 * (lv % 2) + lon % 12)

    def south(lv, t):
        return [
            pl.ds(place(lv, 12 * m) + 8 + t, 12 if m < 2 else 6, stride=16) for m in range(3)
        ]

    def corner(lv, t):
        return pl.ds(place(lv, 30) + 8 + t, 6, stride=16)

    def take(p):
        for n, own in enumerate((x, y)):
            low, high = scratch[2 * n], scratch[2 * n + 1]
            for lv in (2 * p, 2 * p + 1):
                if lv % 2 == 0:
                    cleft, cright = undense_corner(c[n, lv // 2])
                for lon in range(30):
                    keep(low, high, place(lv, lon), own[lv, 6 + lon].astype(F32)[16:])
                left, right = undense(e[n, lv])
                for lon in range(6):
                    at = place(lv, 30 + lon)
                    low[at : at + 8, :] = left[24 * lon + 16 : 24 * lon + 24]
                    high[at : at + 8, :] = right[24 * lon + 16 : 24 * lon + 24]
                left, right = undense(s[n, lv])
                for t in range(3):
                    for m, at in enumerate(south(lv, t)):
                        rows = slice(32 * t + 12 * m, 32 * t + min(12 * m + 12, 30))
                        low[at, :] = left[rows]
                        high[at, :] = right[rows]
                    rows = slice(18 * (lv % 2) + 6 * t, 18 * (lv % 2) + 6 * t + 6)
                    low[corner(lv, t), :] = cleft[rows]
                    high[corner(lv, t), :] = cright[rows]

    def give(p):
        low, high = scratch[4], scratch[5]
        pad = jnp.zeros((2, D), F32)
        corners = []
        for lv in (2 * p, 2 * p + 1):
            for lon in range(30):
                os_ref[lv, lon] = kept(low, high, place(lv, lon), 8)
            for lon in range(6):
                tail_ref[lv, lon] = kept(low, high, place(lv, 30 + lon), 8)
            parts = []
            for t in range(3):
                parts += [joined(low, high, at) for at in south(lv, t)] + [pad]
                corners.append(joined(low, high, corner(lv, t)))
            rows = jnp.concatenate(parts, axis=0)
            bs_ref[lv] = dense(rows[:, :128], rows[:, 128:])
        bc_ref[p] = dense_corner(jnp.concatenate(corners, axis=0))

    take(0)
    refs = dict(gain=gain, wqkv=wqkv, wqkv_t=wqkv_t, wout_t=wout_t, bias=bias, gb=gb_ref)
    windows = [
        window_of(scratch, 1152 * p + 384 * k + 5, 16, 1, refs) for p in range(2) for k in range(3)
    ]
    windows[1].also_first = lambda: take(1)
    windows[2].also_last = lambda: give(0)
    run_windows(windows, gw_ref)
    give(1)


def east_kernel(
    x, y, e, tail, gain, wqkv, wqkv_t, wout_t, bias, gw_in, gb_in, core, oe_ref, be_ref, give_ref, mine_ref, gw_ref, gb_ref, sum_ref, *scratch
):
    @pl.when(pl.program_id(0) == 0)
    def _():
        gw_ref[...] = gw_in[...]
        gb_ref[...] = gb_in[...]

    def place(lv, lon):
        return 576 * (lv // 2) + 24 * (12 * (lv % 2) + lon)

    for n, own in enumerate((x, y)):
        low, high = scratch[2 * n], scratch[2 * n + 1]
        for lv in range(4):
            left, right = undense(e[n, lv])
            for lon in range(6):
                keep(low, high, place(lv, lon), own[lv, lon])
                at = place(lv, 6 + lon)
                low[at : at + 24, :] = left[24 * lon : 24 * lon + 24]
                high[at : at + 24, :] = right[24 * lon : 24 * lon + 24]
    refs = dict(gain=gain, wqkv=wqkv, wqkv_t=wqkv_t, wout_t=wout_t, bias=bias, gb=gb_ref)
    run_windows(
        [
            window_of(scratch, 576 * p + 3 + 6 * a, 24, 0, refs)
            for p in range(2)
            for a in range(3)
        ],
        gw_ref,
    )
    low, high = scratch[4], scratch[5]
    row = lax.broadcasted_iota(jnp.int32, (8, D), 0)
    for lv in range(4):
        east = []
        for lon in range(6):
            oe_ref[lv, lon] = kept(low, high, place(lv, lon), 24)
            at = place(lv, 6 + lon)
            last = joined(low, high, pl.ds(at + 16, 8))
            east += [
                joined(low, high, pl.ds(at, 16)),
                jnp.where(row >= 5, tail[lv, lon].astype(F32), last),
            ]
        east = jnp.concatenate(east, axis=0)
        be_ref[lv] = dense(east[:, :128], east[:, 128:])
    write_halves(core, give_ref, mine_ref, gw_ref, gb_ref, sum_ref)


def whole(shape):
    return pl.BlockSpec(shape, lambda *_: (0,) * len(shape))


PARAMS = pltpu.CompilerParams(vmem_limit_bytes=60 * 1024 * 1024)
GW = (4, D, D)
GB = (W, LANES)
BIAS = (2, W, LANES)


def cost(count):
    return pl.CostEstimate(
        flops=count * 144 * 192 * 192 * 40, bytes_accessed=count * 144 * 192 * 6, transcendentals=0
    )


def const_specs():
    return [whole((1, D)), whole((D, 768)), whole((3 * D, D)), whole((D, D))]


def halves(rows):
    return [pltpu.VMEM((rows, 128), F32) for _ in range(6)]


def inner_specs():
    def cols(n):
        return pl.BlockSpec((4, 6, 24, D), lambda i: (i, n, 0, 0))

    parts = [cols(n) for n in range(1, 5)]
    return parts + parts, pl.BlockSpec((4, 24, 24, D), lambda i: (i, 0, 0, 0))


def inner_windows(x, y, weights, pair_bias, last):
    steps = x.shape[0] // 4
    ins, out = inner_specs()
    return pl.pallas_call(
        inner_kernel,
        grid=(steps,),
        in_specs=ins
        + [whole((1, D)), whole((D, 3 * D)), whole((D, D)), whole((HEADS, W, W)), whole((1, 1))],
        out_specs=[out, whole(GW), whole(GB), whole(BIAS)] + const_specs()[1:],
        out_shape=[
            jax.ShapeDtypeStruct((x.shape[0], 24, 24, D), BF16),
            jax.ShapeDtypeStruct(GW, F32),
            jax.ShapeDtypeStruct(GB, F32),
            jax.ShapeDtypeStruct(BIAS, F32),
            jax.ShapeDtypeStruct((D, 768), BF16),
            jax.ShapeDtypeStruct((3 * D, D), BF16),
            jax.ShapeDtypeStruct((D, D), BF16),
        ],
        scratch_shapes=halves(2304),
        compiler_params=PARAMS,
        cost_estimate=cost(12 * steps),
        name="inner_windows",
    )(x, x, x, x, y, y, y, y, *weights, pair_bias, last)


def both(*rest):
    zeros = (0,) * len(rest)
    return pl.BlockSpec((2, 2) + rest, lambda i: (0, i) + zeros)


def one(*rest):
    zeros = (0,) * len(rest)
    return pl.BlockSpec((2,) + rest, lambda i: (i,) + zeros)


def both_corner():
    return pl.BlockSpec((2, 1, 56, 128), lambda i: (0, i, 0, 0))


def one_corner():
    return pl.BlockSpec((1, 56, 128), lambda i: (i, 0, 0))


def pack_halo(x, y):
    levels = x.shape[0]
    return pl.pallas_call(
        pack_kernel,
        grid=(levels // 2,),
        in_specs=[one(36, 16, D), one(36, 16, D), one(6, 24, D), one(6, 24, D)],
        out_specs=[both(216, 128), both(144, 128), both_corner()],
        out_shape=[
            jax.ShapeDtypeStruct((2, levels, 216, 128), BF16),
            jax.ShapeDtypeStruct((2, levels, 144, 128), BF16),
            jax.ShapeDtypeStruct((2, levels // 2, 56, 128), BF16),
        ],
        scratch_shapes=[pltpu.VMEM((1152, 128), F32), pltpu.VMEM((1152, 128), F32)],
        compiler_params=PARAMS,
        name="pack_halo",
    )(x, y, x, y)


def four(*rest, at=0):
    zeros = (0,) * (len(rest) - 1)
    return pl.BlockSpec((4,) + rest, lambda i: (i, at) + zeros)


def both_four(count, *rest):
    return pl.BlockSpec((2, count) + rest, lambda i: (0, i, 0, 0))


def south_windows(x, y, e, s, c, consts, bias, sums):
    levels = x.shape[0]
    return pl.pallas_call(
        south_kernel,
        grid=(levels // 4,),
        in_specs=[
            four(36, 24, D),
            four(36, 24, D),
            both_four(4, 216, 128),
            both_four(4, 144, 128),
            both_four(2, 56, 128),
        ]
        + const_specs()
        + [whole(BIAS), whole(GW), whole(GB)],
        out_specs=[
            four(30, 8, D),
            four(6, 8, D),
            four(144, 128),
            pl.BlockSpec((2, 56, 128), lambda i: (i, 0, 0)),
            whole(GW),
            whole(GB),
        ],
        out_shape=[
            jax.ShapeDtypeStruct((levels, 30, 8, D), BF16),
            jax.ShapeDtypeStruct((levels, 6, 8, D), BF16),
            jax.ShapeDtypeStruct((levels, 144, 128), BF16),
            jax.ShapeDtypeStruct((levels // 2, 56, 128), BF16),
            jax.ShapeDtypeStruct(GW, F32),
            jax.ShapeDtypeStruct(GB, F32),
        ],
        scratch_shapes=halves(2304),
        compiler_params=PARAMS,
        cost_estimate=cost(12),
        name="south_windows",
    )(x, y, e, s, c, *consts, bias, *sums)


def east_windows(x, y, e, tail, consts, bias, sums, core):
    levels = x.shape[0]
    return pl.pallas_call(
        east_kernel,
        grid=(levels // 4,),
        in_specs=[
            four(6, 24, D, at=5),
            four(6, 24, D, at=5),
            both_four(4, 216, 128),
            four(6, 8, D),
        ]
        + const_specs()
        + [whole(BIAS), whole(GW), whole(GB), whole((1, 1))],
        out_specs=[
            four(6, 24, D),
            four(216, 128),
            whole((ROWS // 2, 128)),
            whole((ROWS // 2, 128)),
        ],
        out_shape=[
            jax.ShapeDtypeStruct((levels, 6, 24, D), BF16),
            jax.ShapeDtypeStruct((levels, 216, 128), BF16),
            jax.ShapeDtypeStruct((ROWS // 2, 128), BF16),
            jax.ShapeDtypeStruct((ROWS // 2, 128), F32),
        ],
        scratch_shapes=[pltpu.VMEM(GW, F32), pltpu.VMEM(GB, F32), pltpu.VMEM((ROWS, 128), F32)]
        + halves(1152),
        compiler_params=PARAMS,
        cost_estimate=cost(12),
        name="east_windows",
    )(x, y, e, tail, *consts, bias, *sums, core)


def assemble_kernel(inner, oe, os_, gl, gs, gc, *rest):
    out_ref, low, high = rest[-3:]
    row = lax.broadcasted_iota(jnp.int32, (8, D), 0)
    cleft, cright = undense_corner(gc[0])
    for lv in range(2):
        base = 288 * lv
        left, right = undense(gs[lv])
        for t in range(3):
            at = pl.ds(base + 48 + t, 30, stride=8)
            low[at, :] = left[32 * t : 32 * t + 30]
            high[at, :] = right[32 * t : 32 * t + 30]
            at = pl.ds(base + t, 6, stride=8)
            rows = slice(18 * lv + 6 * t, 18 * lv + 6 * t + 6)
            low[at, :] = cleft[rows]
            high[at, :] = cright[rows]
        left, right = undense(gl[lv])
        for lon in range(36):
            if lon < 6:
                at = slice(24 * lon, 24 * lon + 24)
                rows = jnp.concatenate([left[at], right[at, :64]], axis=1)
            else:
                rows = (inner[lv, lon - 6] if lon < 30 else oe[lv, lon - 30]).astype(F32)
                tail = os_[lv, lon - 6].astype(F32)
                rows = jnp.concatenate([rows[:16], jnp.where(row >= 5, tail, rows[16:])], axis=0)
            head = jnp.where(row < 3, joined(low, high, pl.ds(base + 8 * lon, 8)), rows[:8])
            out_ref[lv, lon] = jnp.concatenate([head, rows[8:]], axis=0).astype(BF16)


def assemble(first, steps, grad_x, inner, oe, os_, got_lon, got_lat, got_both):
    def at(count, *rest):
        zeros = (0,) * len(rest)
        return pl.BlockSpec((count,) + rest, lambda i: (i + first,) + zeros)

    ins = [inner, oe, os_, got_lon, got_lat, got_both]
    specs = [
        at(2, 24, 24, D),
        at(2, 6, 24, D),
        at(2, 30, 8, D),
        at(2, 216, 128),
        at(2, 144, 128),
        at(1, 56, 128),
    ]
    aliases = {}
    if grad_x is not None:
        ins.append(grad_x)
        specs.append(pl.BlockSpec(memory_space=pl.ANY))
        aliases = {6: 0}
    return pl.pallas_call(
        assemble_kernel,
        grid=(steps,),
        in_specs=specs,
        out_specs=at(2, 36, 24, D),
        out_shape=jax.ShapeDtypeStruct((inner.shape[0], 36, 24, D), BF16),
        scratch_shapes=[pltpu.VMEM((576, 128), F32), pltpu.VMEM((576, 128), F32)],
        input_output_aliases=aliases,
        compiler_params=PARAMS,
        cost_estimate=pl.CostEstimate(
            flops=0, bytes_accessed=1_500_000 * steps, transcendentals=0
        ),
        name="assemble",
    )(*ins)


def finish_kernel(
    factor, line_ref, other_ref, core, gain_ref, w_ref, gq_ref, go_ref, gb_ref, gg_ref, sum_ref
):
    line, other = line_ref[...].astype(F32), other_ref[...].astype(F32)
    first = core[...] == 0
    sum_ref[: ROWS // 2] = jnp.where(first, line, other)
    sum_ref[ROWS // 2 :] = jnp.where(first, other, line)
    both = jnp.concatenate(
        [sum_ref[D * t : D * t + D] for t in range(6)], axis=1
    )
    gq = both[:, : 3 * D] * factor
    gq_ref[...] = gq
    go_ref[...] = both[:, 3 * D :] * factor
    products = (gq * w_ref[...].astype(F32)).T
    gg_ref[...] = jnp.sum(products, axis=0, keepdims=True) / gain_ref[...]
    base = WROWS + 6 * W
    rest = sum_ref[base : base + W]
    for h in range(HEADS):
        main = sum_ref[WROWS + W * h : WROWS + W * h + W]
        turned = jnp.concatenate([main, rest[:, 16 * h : 16 * h + 16]], axis=1)
        gb_ref[h] = regroup(regroup(turned, True).T, True)


def finish(line, other, core, gain_row, qkv_weight, factor):
    return pl.pallas_call(
        lambda *refs: finish_kernel(factor, *refs),
        out_shape=[
            jax.ShapeDtypeStruct((D, 3 * D), F32),
            jax.ShapeDtypeStruct((D, D), F32),
            jax.ShapeDtypeStruct((HEADS, W, W), F32),
            jax.ShapeDtypeStruct((1, D), F32),
        ],
        scratch_shapes=[pltpu.VMEM((ROWS, 128), F32)],
        compiler_params=PARAMS,
        name="finish_sums",
    )(line, other, core, gain_row, qkv_weight)


def shift(value, axes, steps):
    sizes = [lax.axis_size(a) for a in axes]
    total = 1
    for s in sizes:
        total *= s
    pairs = []
    for source in range(total):
        rest, place = source, []
        for s in reversed(sizes):
            place.append(rest % s)
            rest //= s
        place.reverse()
        target = 0
        for p, s, d in zip(place, sizes, steps):
            target = target * s + (p + d) % s
        pairs.append((source, target))
    return lax.ppermute(value, axes if len(axes) > 1 else axes[0], pairs)


def moved(value, axis, to_of):
    count = lax.axis_size(axis)
    return lax.ppermute(value, axis, [(n, to_of(n)) for n in range(count)])


def flip(value, axis, bits):
    return moved(value, axis, lambda n: n ^ bits)


def lon_core(n):
    return n % 2


def sum_over_devices(give, mine, back, beside):
    y = (lax.axis_index("lon") // 2) % 4
    mine = mine + flip(give, "lon", 1).astype(F32)
    quarters = mine.reshape(4, ROWS // 8, 128)
    qlow = quarters.astype(BF16)
    total = lax.dynamic_index_in_dim(quarters, y, 0, keepdims=False)
    for step in range(1, 4):
        piece = lax.dynamic_index_in_dim(qlow, y ^ step, 0, keepdims=False)
        total = total + flip(piece, "lon", 2 * step).astype(F32)
    low = total.astype(BF16)
    for step in range(1, 4):
        total = total + flip(low, "lat", 2 * step).astype(F32)
    total, got_lon = lax.optimization_barrier((total, back[0]))
    back = (got_lon, *back[1:])
    low = total.astype(BF16)
    total = (
        total
        + flip(low, "lat", 1).astype(F32)
        + flip(low, "lon", 8).astype(F32)
        + shift_x(low).astype(F32)
    )
    total, grad_x = lax.optimization_barrier((total, beside(0, None, back)))
    low = total.astype(BF16)
    others = [low] + [flip(low, "lon", 2 * step) for step in range(1, 4)]
    stacked = jnp.stack(others)
    line = jnp.concatenate(
        [lax.dynamic_index_in_dim(stacked, y ^ n, 0, keepdims=True) for n in range(4)], axis=0
    )
    line, grad_x = lax.optimization_barrier((line, beside(1, grad_x, back)))
    other = flip(line, "lon", 1)
    return line.reshape(ROWS // 2, 128), other.reshape(ROWS // 2, 128), grad_x


def shift_x(value):
    lat = lax.axis_size("lat")
    total = lax.axis_size("lon") * lat
    pairs = []
    for source in range(total):
        lon_at, lat_at = source // lat, source % lat
        pairs.append((source, (lon_at ^ 8) * lat + (lat_at ^ 1)))
    return lax.ppermute(value, ("lon", "lat"), pairs)


def local(tokens, cotangent, ln_gain, qkv_weight, out_weight, pair_bias):
    levels, lat_count, lon_count, _ = tokens.shape
    x = jnp.transpose(tokens, (0, 2, 1, 3))
    y = jnp.transpose(cotangent, (0, 2, 1, 3))
    e, s, c = pack_halo(x, y)
    s = shift(s, ("lat",), (-1,))
    e = shift(e, ("lon",), (-1,))
    c = shift(c, ("lon", "lat"), (-1, -1))
    gain = ln_gain.reshape(1, D)
    core = (lax.axis_index("lon") % 2).astype(jnp.int32).reshape(1, 1)
    last = (lax.axis_index("lat") == lax.axis_size("lat") - 1).astype(jnp.int32).reshape(1, 1)
    inner, gw, gb, bias, *laid = inner_windows(
        x, y, (gain, qkv_weight, out_weight), pair_bias, last
    )
    consts = [gain] + laid
    os_, tail, bs, bc, gw, gb = south_windows(x, y, e, s, c, consts, bias, (gw, gb))
    got_lat = shift(bs, ("lat",), (1,))
    got_both = shift(bc, ("lon", "lat"), (1, 1))
    oe, be, give, mine = east_windows(x, y, e, tail, consts, bias, (gw, gb), core)
    got_lon = shift(be, ("lon",), (1,))
    give, got_lat, got_both = lax.optimization_barrier((give, got_lat, got_both))
    back = (got_lon, got_lat, got_both)
    half = levels // 4

    def beside(part, grad_x, got):
        return assemble(half * part, half, grad_x, inner, oe, os_, *got)

    *sums, grad_x = sum_over_devices(give, mine, back, beside)
    factor = float(
        levels * lat_count * lax.axis_size("lat") * lon_count * lax.axis_size("lon")
    ) ** (-0.5)
    gq, go, gbias, gg = finish(*sums, core, gain, qkv_weight, factor)
    return (jnp.transpose(grad_x, (0, 2, 1, 3)), gq, go, gbias, gg.reshape(D))


def solution(mesh):
    placed = (P(None, "lat", "lon", None), P(None, "lat", "lon", None), P(), P(), P(), P())
    return jax.shard_map(
        local,
        mesh=mesh,
        in_specs=placed,
        out_specs=(P(None, "lat", "lon", None), P(), P(), P(), P()),
        check_vma=False,
    )
```
